32 devices in a mesh: wide: 8 (over z, y), narrow: 4 (over x, core).
Axes of the slice: x: 2, y: 2, z: 4, core: 2. Of those that a mesh axis runs over, the one named last changes fastest.
Arguments:
- patches: bfloat16 [8192, 1280], P('wide', 'narrow'), may hold values from -6 to 6
- norm_gain: float32 [1280], replicated, may hold values from 0.1 to 1.9
- norm_bias: float32 [1280], replicated, may hold values from -3 to 3
- w_in: bfloat16 [1280, 5120], P('wide', 'narrow'), may hold values from -0.15625 to 0.15625
- b_in: float32 [5120], P('narrow'), may hold values from -3 to 3
- w_out: bfloat16 [5120, 1280], P('narrow', 'wide'), may hold values from -0.078125 to 0.078125
- b_out: float32 [1280], P('narrow'), may hold values from -3 to 3
- w_proj: bfloat16 [4, 1280, 1280], P(None, 'narrow', 'wide'), may hold values from -0.078125 to 0.078125
- b_proj: float32 [1280], P('narrow'), may hold values from -3 to 3
- text: bfloat16 [4096, 1280], P('wide', 'narrow'), may hold values from -6 to 6
- place: int32 [2048], replicated, may hold values from -1 to 4095, as said below
Outputs:
- prompt_embeds: bfloat16 [4096, 1280], P('wide', 'narrow')
The draws below stay inside these ranges and needn't reach their ends.
Inputs may be any that keep to these rules, and one draw needn't show every extreme that they name: `place`: of the 256 entries of one wide index (entries i * 256 to (i + 1) * 256 - 1), the valid ones (>= 0) come first and -1 fills the rest; three quarters or more are valid, and all are valid for some wide index. Valid values are distinct. For one wide index, at most 64 valid entries v have the same v // 512, and every wide index reaches 64 for some value.
All inputs are finite; a program needn't handle non-finite values.
Results may differ from the reference program's by a relative error of at most 0.012.
Values may be sent and summed in bfloat16 or wider, within the bound.
No kernel may reach another device: no remote copies, remote signals or barrier semaphores. Data moves between devices by JAX's collectives and lax.ppermute only.
A program may use at most 64 MiB of HBM per device.

```python
import jax
import jax.numpy as jnp
from jax import lax

D = 1280
FF = 5120
DL = 1280
TOK_GROUP = 1024
MERGE_ROWS = 256
SEQ_GROUP = 512
BUCKET = 64
TOKENS = 8192
MERGED = 2048
SEQ_LEN = 4096
N_WIDE = 8
N_NARROW = 4


def draw_place(key, part):
    groups = MERGED // MERGE_ROWS
    slot_count = BUCKET * groups
    key_pad, key_full, key_slot, key_row, key_pos = jax.random.split(key, 5)
    padding = jax.random.randint(key_pad, (groups,), 0, MERGE_ROWS // 4 + 1)
    fullest = jax.random.randint(key_full, (), 0, groups)
    padding = jnp.where(jnp.arange(groups) == fullest, 0, padding)
    counts = MERGE_ROWS - padding

    def slot_order(subkey):
        shuffled = jax.random.permutation(subkey, slot_count)
        hottest = shuffled[0] // BUCKET
        order_rank = jnp.argsort(shuffled)
        scores = jnp.where(jnp.arange(slot_count) // BUCKET == hottest, 0, slot_count) + order_rank
        return jnp.argsort(scores)[:MERGE_ROWS]

    def row_order(subkey, row_count):
        order_rank = jnp.argsort(jax.random.permutation(subkey, MERGE_ROWS))
        positions = jnp.arange(MERGE_ROWS)
        return jnp.argsort(jnp.where(positions < row_count, order_rank, MERGE_ROWS + positions))

    def layout_order(subkey):
        return jax.random.permutation(subkey, SEQ_GROUP)
    chosen = jax.vmap(slot_order)(jax.random.split(key_slot, groups))
    row_perm = jax.vmap(row_order)(jax.random.split(key_row, groups), counts)
    slot_of_row = jnp.take_along_axis(chosen, row_perm, axis=1)
    target = slot_of_row // BUCKET
    within = slot_of_row % BUCKET
    layouts = jax.vmap(layout_order)(jax.random.split(key_pos, groups))
    source = jnp.arange(groups)[:, None]
    local_row = layouts[target, source * BUCKET + within]
    placed = target * SEQ_GROUP + local_row
    is_valid = jnp.arange(MERGE_ROWS)[None, :] < counts[:, None]
    return jnp.where(is_valid, placed, -1).reshape(-1).astype(jnp.int32)


def block_scale(key, extent, cuts, smallest, high):
    gain = 1.0
    for axis_at, shards_of in cuts:
        steps = jax.random.uniform(jax.random.fold_in(jax.random.fold_in(key, 6), axis_at), (shards_of,), jnp.float32, smallest / len(cuts), high / len(cuts))
        gain = gain * jnp.repeat(jnp.exp(steps), extent[axis_at] // shards_of).reshape((-1,) + (1,) * (len(extent) - 1 - axis_at))
    return gain


def scatter_about(rng, extent, scale, limit, cuts=(), kind=jnp.bfloat16):
    entries = jax.random.normal(rng, extent, jnp.float32) * scale
    if len(cuts) > 0:
        entries = block_scale(rng, extent, cuts, -0.22, 0.18) * entries
    return jnp.clip(entries, min=-limit, max=limit).astype(kind)


def setup_inputs(seed: int = 0) -> dict:
    seeds = jax.random.split(jax.random.key(seed), 12)
    return {
        "patches": scatter_about(seeds[0], (TOKENS, D), 1.0, 6.0, ((0, 8), (1, 4))),
        "norm_gain": jnp.clip(1.0 + 0.18 * jax.random.normal(seeds[1], (D,), jnp.float32), 0.1, 1.9),
        "norm_bias": scatter_about(seeds[2], (D,), 0.5, 3.0, (), jnp.float32),
        "w_in": scatter_about(seeds[3], (D, FF), D ** -0.5, 0.15625, ((0, 8), (1, 4))),
        "b_in": scatter_about(seeds[4], (FF,), 0.5, 3.0, ((0, 4),), jnp.float32),
        "w_out": scatter_about(seeds[5], (FF, D), FF ** -0.5, 0.078125, ((0, 4), (1, 8))),
        "b_out": scatter_about(seeds[6], (D,), 0.5, 3.0, ((0, 4),), jnp.float32),
        "w_proj": scatter_about(seeds[7], (4, D, DL), (4 * D) ** -0.5, 0.078125, ((1, 4), (2, 8))),
        "b_proj": scatter_about(seeds[8], (DL,), 0.5, 3.0, ((0, 4),), jnp.float32),
        "text": scatter_about(seeds[9], (SEQ_LEN, DL), 1.0, 6.0, ((0, 8), (1, 4))),
        "place": draw_place(jax.random.fold_in(seeds[11], 71), 0),
    }


def block_sums(left, right):
    width = left.shape[1] // N_NARROW
    total = jnp.zeros((left.shape[0], right.shape[1]), jnp.float32)
    for block in range(N_NARROW):
        term = jnp.dot(left[:, block * width:(block + 1) * width], right[block * width:(block + 1) * width], preferred_element_type=jnp.float32).astype(jnp.bfloat16)
        term = lax.optimization_barrier(term)
        total = total + term.astype(jnp.float32)
    return total

def encode_group(group_rows, norm_gain, norm_bias, w_in, b_in, w_out, b_out, w_proj, b_proj):
    values = group_rows.astype(jnp.float32)
    center = lax.optimization_barrier(jnp.mean(values, axis=-1, keepdims=True))
    spread = lax.optimization_barrier(jnp.mean(jnp.square(values - center), axis=-1, keepdims=True))
    normed = ((values - center) * lax.rsqrt(spread + 1e-06) * norm_gain + norm_bias).astype(jnp.bfloat16)
    product = jnp.dot(normed, w_in, preferred_element_type=jnp.float32) + b_in
    hidden = jax.nn.gelu(product, approximate=False).astype(jnp.bfloat16)
    mlp_out = block_sums(hidden, w_out) + b_out
    stream = (values + mlp_out).astype(jnp.bfloat16)
    window_rows = stream.shape[0] // 4
    width = D // N_NARROW
    windows = stream.reshape(window_rows, 4, N_NARROW, width).transpose(0, 2, 1, 3).reshape(window_rows, N_NARROW * 4 * width)
    proj_rows = w_proj.reshape(4, N_NARROW, width, DL).transpose(1, 0, 2, 3).reshape(N_NARROW * 4 * width, DL)
    vision = block_sums(windows, proj_rows) + b_proj
    return vision.astype(jnp.bfloat16)

def reference(patches, norm_gain, norm_bias, w_in, b_in, w_out, b_out, w_proj, b_proj, text, place):
    grouped = patches.reshape(N_WIDE, TOK_GROUP, D)

    def one_group(group_rows):
        return encode_group(group_rows, norm_gain, norm_bias, w_in, b_in, w_out, b_out, w_proj, b_proj)
    vision = lax.map(one_group, grouped).reshape(MERGED, DL)
    target = jnp.where(place >= 0, place, SEQ_LEN).astype(jnp.int32)
    return text.at[target].set(vision, mode='drop')
```

```python
import functools

import jax
import jax.numpy as jnp
from jax import lax
from jax.experimental import pallas as pl
from jax.experimental.pallas import tpu as pltpu
from jax.sharding import PartitionSpec as P

F32 = jnp.float32
BF16 = jnp.bfloat16
WINDOW = 4
ANY = pl.BlockSpec(memory_space=pl.ANY)
SMEM = pl.BlockSpec(memory_space=pltpu.SMEM)
VMEM = pl.BlockSpec(memory_space=pltpu.VMEM)


def call(kernel, operands, specs, outs, scratch=(), flops=0, moved=0, special=0, name=None):
    single = not isinstance(outs, (list, tuple))
    return pl.pallas_call(
        kernel,
        out_shape=outs,
        in_specs=specs,
        out_specs=VMEM if single else [VMEM] * len(outs),
        scratch_shapes=list(scratch),
        compiler_params=pltpu.CompilerParams(vmem_limit_bytes=48 * 1024 * 1024),
        cost_estimate=pl.CostEstimate(
            flops=flops, bytes_accessed=moved, transcendentals=special
        ),
        name=name,
    )(*operands)


def shape(*dims, dtype=BF16):
    return jax.ShapeDtypeStruct(dims, dtype)


def load_rows(offsets, sources, layout, target, sem):
    copies = []
    for i, (array_at, start, rows) in enumerate(layout):
        at = pl.multiple_of(offsets[i], 16)
        copies.append(
            pltpu.make_async_copy(
                sources[array_at].at[pl.ds(start, rows)], target.at[pl.ds(at, rows)], sem.at[i]
            )
        )
    for copy in copies:
        copy.start()
    return copies


def order_kernel(x_ref, o_ref):
    tokens = x_ref.shape[1]
    windows = tokens // WINDOW
    source = lax.broadcasted_iota(jnp.int32, (tokens, windows), 0)
    window = lax.broadcasted_iota(jnp.int32, (tokens, windows), 1)
    for p in range(WINDOW):
        pick = jnp.where(source == WINDOW * window + p, 1.0, 0.0).astype(BF16)
        o_ref[:, p * windows : (p + 1) * windows] = jnp.dot(
            x_ref[...], pick, preferred_element_type=F32
        ).astype(BF16)


def norm_kernel(layout, count, offsets, gain, bias, *refs):
    sources, o_ref, whole, sem = refs[:count], refs[count], refs[count + 1], refs[count + 2]
    for copy in load_rows(offsets, sources, layout, whole, sem):
        copy.wait()
    width, tokens = whole.shape
    step = 128
    for t in range(0, tokens, step):
        values = whole[:, t : t + step].astype(F32)
        center = jnp.sum(values, axis=0, keepdims=True) * (1.0 / width)
        values = values - center
        spread = jnp.sum(values * values, axis=0, keepdims=True) * (1.0 / width)
        values = (values * lax.rsqrt(spread + 1e-06)).T
        o_ref[t : t + step, :] = (values * gain[...] + bias[...]).astype(BF16)


def hidden_kernel(layout, count, offsets, normed, bias, *refs):
    sources, o_ref, whole, sem = refs[:count], refs[count], refs[count + 1], refs[count + 2]
    for copy in load_rows(offsets, sources, layout, whole, sem):
        copy.wait()
    step = 256
    for f in range(0, whole.shape[1], step):
        v = jnp.dot(normed[...], whole[:, f : f + step], preferred_element_type=F32)
        v = v + bias[:, f : f + step]
        o_ref[:, f : f + step] = (0.5 * v * (1.0 + lax.erf(v * (2.0**-0.5)))).astype(BF16)


def out_kernel(layout, count, offsets, hidden, *refs):
    sources, keep, give, whole, sem = refs[:count], *refs[count:]
    for copy in load_rows(offsets, sources, layout, whole, sem):
        copy.wait()
    tokens = hidden.shape[0]
    half, rows = whole.shape[0] // 2, keep.shape[1]
    step = 256
    for target, base in ((give, half), (keep, 0)):
        for t in range(0, tokens, step):
            v = lax.dot_general(
                whole[base : base + half, :],
                hidden[t : t + step, :],
                (((1,), (1,)), ((), ())),
                preferred_element_type=F32,
            ).astype(BF16)
            for j in range(2):
                target[j, :, t : t + step] = v[j * rows : (j + 1) * rows]


def proj_kernel(layout, count, offsets, merged, *refs):
    sources, keep, give, whole, sem = refs[:count], *refs[count:]
    for copy in load_rows(offsets, sources, layout, whole, sem):
        copy.wait()
    half, rows = whole.shape[0] // 2, keep.shape[1]
    for target, base in ((give, half), (keep, 0)):
        v = jnp.dot(
            whole[base : base + half, :], merged[...], preferred_element_type=F32
        ).astype(BF16)
        for j in range(2):
            target[j] = v[j * rows : (j + 1) * rows]


def stream_kernel(own, keep, near, far, bias, o_ref):
    total = keep[0].astype(F32) + near[0].astype(F32) + far[...].astype(F32)
    stream = (own[...].astype(F32) + (total + bias[...])).astype(BF16)
    rows, windows = own.shape[0], own.shape[1] // WINDOW
    for p in range(WINDOW):
        o_ref[p * rows : (p + 1) * rows, :] = stream[:, p * windows : (p + 1) * windows]


def pack_kernel(slots_of, keep, near, far, bias, o_ref):
    total = keep[0].astype(F32) + near[0].astype(F32) + far[...].astype(F32)
    vision = (total + bias[...]).astype(BF16)
    slots = o_ref.shape[0]
    windows = vision.shape[1]
    slot = lax.broadcasted_iota(jnp.int32, (slots, windows), 0)
    pick = jnp.where(slot == slots_of[...], 1.0, 0.0).astype(BF16)
    o_ref[...] = lax.dot_general(
        pick, vision, (((1,), (1,)), ((), ())), preferred_element_type=F32
    ).astype(BF16)


def place_kernel(targets, arrived, text, o_ref):
    slots, rows = arrived.shape[0], text.shape[1]
    row = lax.broadcasted_iota(jnp.int32, (slots, rows), 1)
    pick = jnp.where(row == targets[...], 1.0, 0.0)
    hit = jnp.sum(pick, axis=0, keepdims=True) > 0.5
    moved = lax.dot_general(
        arrived[...], pick.astype(BF16), (((0,), (0,)), ((), ())), preferred_element_type=F32
    ).astype(BF16)
    o_ref[...] = jnp.where(hit, moved, text[...])


def ring_order(count):
    return list(range(0, count, 2)) + list(range(count - 1, 0, -2))


class Rings:
    def __init__(self, axis, count, depth):
        self.axis, self.count, self.depth = axis, count, depth
        order = ring_order(count)
        self.right = [(order[i], order[(i + 1) % count]) for i in range(count)]
        self.left = [(b, a) for a, b in self.right]
        self.table = jnp.asarray(order, jnp.int32)
        place_of = [order.index(i) for i in range(count)]
        self.place = jnp.asarray(place_of, jnp.int32)[lax.axis_index(axis)]
        self.sent = {0: [], 1: []}

    def hop(self, block, way, tied):
        past = self.sent[way]
        if tied and len(past) >= self.depth:
            block, _ = lax.optimization_barrier((block, past[-self.depth]))
        block = lax.ppermute(block, self.axis, self.right if way == 0 else self.left)
        past.append(block)
        return block

    def gather(self, shard):
        rows = shard.shape[0] // 2
        me = lax.axis_index(self.axis)
        halves = [shard[:rows], shard[rows:]]
        pieces = [(halves[0], me, 0), (halves[1], me, 1)]
        last = self.count // 2
        held = {(way, h): halves[h] for way in (0, 1) for h in (0, 1)}
        for step in range(1, last + 1):
            for h in (0, 1):
                for way in (0, 1):
                    half = h if way == 0 else 1 - h
                    if step == last and h == 1:
                        continue
                    block = self.hop(held[way, half], way, step == 1)
                    held[way, half] = block
                    shift = -step if way == 0 else step
                    owner = self.table[(self.place + shift) % self.count]
                    pieces.append((block, owner, half))
        return pieces


def per_device(
    patches, norm_gain, norm_bias, w_in, b_in, w_out, b_out, w_proj, b_proj, text, place
):
    groups, parts = lax.axis_size("wide"), lax.axis_size("narrow")
    me, part = lax.axis_index("wide"), lax.axis_index("narrow")
    tokens, width = patches.shape[0], patches.shape[1]
    full = width * parts
    windows = tokens // WINDOW
    seq_rows = text.shape[0]
    bucket = seq_rows // groups
    slots = groups * bucket

    near_pairs = [(i, i ^ 1) for i in range(parts)]
    far_pairs = [(i, i ^ 2) for i in range(parts)]

    def near(x):
        return lax.ppermute(x, "narrow", near_pairs)

    def far(x):
        return lax.ppermute(x, "narrow", far_pairs)

    shards = [
        w_in,
        w_out.T,
        jnp.transpose(w_proj, (2, 0, 1)).reshape(w_proj.shape[2], -1),
    ]
    rows = [s.shape[0] for s in shards]
    block = full // parts
    swap = part ^ jnp.arange(parts, dtype=jnp.int32)
    place_of_block = (swap % 2) * 2 + swap // 2

    if groups <= 8 and all(r % 32 == 0 for r in rows):
        rings = Rings("wide", groups, 2)
        gathered = []
        for i, shard in enumerate(shards):
            pieces = rings.gather(shard)
            r = rows[i]
            per_block = block // r
            offsets = []
            for _, owner, half in pieces:
                if i == 0:
                    at = owner * r
                else:
                    at = place_of_block[owner // per_block] * block + (owner % per_block) * r
                offsets.append(at + half * (r // 2))
            layout = [(k, 0, r // 2) for k in range(len(pieces))]
            gathered.append((layout, [p[0] for p in pieces], jnp.stack(offsets).astype(jnp.int32)))
    else:
        gathered = []
        for i, shard in enumerate(shards):
            whole = lax.all_gather(shard, "wide", axis=0, tiled=True)
            layout = [(0, k * block, block) for k in range(parts)]
            at = jnp.arange(parts, dtype=jnp.int32) if i == 0 else place_of_block
            gathered.append((layout, [whole], (at * block).astype(jnp.int32)))

    own = call(
        order_kernel, (patches.T,), [VMEM], shape(width, tokens),
        flops=2 * width * tokens * tokens, moved=4 * width * tokens, name="order_tokens",
    )
    over_x = far(own)
    over_core = near(own)
    over_both = near(over_x)
    feature_blocks = [own, over_x, over_core, over_both]
    feature_at = (part ^ jnp.asarray([0, 2, 1, 3], jnp.int32)) * width
    layout = [(k, 0, width) for k in range(parts)]
    normed = call(
        functools.partial(norm_kernel, layout, parts),
        (feature_at.astype(jnp.int32), norm_gain[None], norm_bias[None], *feature_blocks),
        [SMEM, VMEM, VMEM] + [ANY] * parts,
        shape(tokens, full),
        scratch=[pltpu.VMEM((full, tokens), BF16), pltpu.SemaphoreType.DMA((parts,))],
        flops=10 * full * tokens, moved=4 * full * tokens, name="norm",
    )

    def weighted(kernel, which, operands, outs, flops, moved, special, name):
        layout, sources, offsets = gathered[which]
        columns = sources[0].shape[1]
        return call(
            functools.partial(kernel, layout, len(sources)),
            (offsets, *operands, *sources),
            [SMEM] + [VMEM] * len(operands) + [ANY] * len(sources),
            outs,
            scratch=[
                pltpu.VMEM((full, columns), BF16),
                pltpu.SemaphoreType.DMA((len(layout),)),
            ],
            flops=flops, moved=moved, special=special, name=name,
        )

    ff = w_in.shape[1]
    hidden = weighted(
        hidden_kernel, 0, (normed, b_in[None]), shape(tokens, ff),
        2 * tokens * full * ff, 2 * (tokens * full + full * ff + tokens * ff), tokens * ff,
        "hidden",
    )
    keep, give = weighted(
        out_kernel, 1, (hidden,),
        [shape(2, width, tokens), shape(2, width, tokens)],
        2 * tokens * full * ff, 2 * (tokens * ff + full * ff + tokens * full), 0, "mlp_out",
    )
    core_sums = near(give)
    x_give = (keep[1].astype(F32) + core_sums[1].astype(F32)).astype(BF16)
    x_sums = far(x_give)
    merged = call(
        stream_kernel, (own, keep, core_sums, x_sums, b_out[:, None]),
        [VMEM] * 5, shape(WINDOW * width, windows),
        flops=4 * width * tokens, moved=10 * width * tokens, name="stream",
    )

    place_table = place.reshape(groups, windows)
    owners = jnp.where(place_table >= 0, place_table // seq_rows, groups)
    own_owners = lax.dynamic_index_in_dim(owners, me, 0, keepdims=False)
    earlier = (jnp.arange(windows)[:, None] <= jnp.arange(windows)[None, :]).astype(BF16)
    owner_hits = own_owners[None, :] == jnp.arange(groups, dtype=jnp.int32)[:, None]
    rank_out = jnp.dot(owner_hits.astype(BF16), earlier, preferred_element_type=F32)
    rank_out = jnp.sum(jnp.where(owner_hits, rank_out, 0.0), axis=0).astype(jnp.int32) - 1
    slots_of = jnp.where(own_owners < groups, own_owners * bucket + rank_out, slots)
    arriving = owners == me
    rank_in = jnp.dot(arriving.astype(BF16), earlier, preferred_element_type=F32).astype(jnp.int32)
    match = (
        rank_in[:, None, :] == jnp.arange(1, bucket + 1, dtype=jnp.int32)[None, :, None]
    ) & arriving[:, None, :]
    local_row = (place_table % seq_rows + 1)[:, None, :]
    targets = jnp.sum(jnp.where(match, local_row, 0), axis=2) - 1
    targets = targets.reshape(slots, 1)

    keep, give = weighted(
        proj_kernel, 2, (merged,),
        [shape(2, width, windows), shape(2, width, windows)],
        2 * windows * full * WINDOW * width,
        2 * (full * WINDOW * width + windows * WINDOW * width + windows * full), 0, "proj",
    )
    core_sums = near(give)
    x_give = (keep[1].astype(F32) + core_sums[1].astype(F32)).astype(BF16)
    x_sums = far(x_give)
    buffer = call(
        pack_kernel, (slots_of[None], keep, core_sums, x_sums, b_proj[:, None]),
        [VMEM] * 5, shape(slots, width),
        flops=2 * slots * windows * width, moved=8 * width * windows + 2 * slots * width,
        name="pack",
    )
    arrived = lax.all_to_all(
        buffer.reshape(groups, bucket, width), "wide", split_axis=0, concat_axis=0, tiled=True
    )
    out = call(
        place_kernel, (targets, arrived.reshape(slots, width), text.T),
        [VMEM] * 3, shape(width, seq_rows),
        flops=2 * slots * seq_rows * width, moved=6 * width * seq_rows, name="place",
    )
    return out.T


def solution(mesh):
    placed = (
        P("wide", "narrow"),
        P(),
        P(),
        P("wide", "narrow"),
        P("narrow"),
        P("narrow", "wide"),
        P("narrow"),
        P(None, "narrow", "wide"),
        P("narrow"),
        P("wide", "narrow"),
        P(),
    )
    return jax.shard_map(
        per_device, mesh=mesh, in_specs=placed, out_specs=P("wide", "narrow"), check_vma=False
    )
```

```python
import functools

import jax
import jax.numpy as jnp
from jax import lax
from jax.experimental import pallas as pl
from jax.experimental.pallas import tpu as pltpu
from jax.sharding import PartitionSpec as P

F32 = jnp.float32
BF16 = jnp.bfloat16
WINDOW = 4
VMEM = pl.BlockSpec(memory_space=pltpu.VMEM)


def call(kernel, operands, outs, scratch=(), flops=0, moved=0, special=0, name=None):
    single = not isinstance(outs, (list, tuple))
    return pl.pallas_call(
        kernel,
        out_shape=outs,
        in_specs=[VMEM] * len(operands),
        out_specs=VMEM if single else [VMEM] * len(outs),
        scratch_shapes=list(scratch),
        compiler_params=pltpu.CompilerParams(vmem_limit_bytes=28 * 1024 * 1024),
        cost_estimate=pl.CostEstimate(
            flops=flops, bytes_accessed=moved, transcendentals=special
        ),
        name=name,
    )(*operands)


def shape(*dims, dtype=BF16):
    return jax.ShapeDtypeStruct(dims, dtype)


def after(x, *others):
    return lax.optimization_barrier((x, *others))[0]


def ring_order(count):
    return list(range(0, count, 2)) + list(range(count - 1, 0, -2))


def ring_owner(me, shift, count):
    half = me // 2
    at = jnp.where(me % 2 == 0, half, count - 1 - half) + (shift + count)
    at = at % count
    return jnp.where(at < count // 2, 2 * at, 2 * (count - 1 - at) + 1)


class Piece:
    def __init__(self, array, start, rows, shift, base, index=0):
        self.array, self.start, self.rows = array, start, rows
        self.shift, self.base, self.index = shift, base, index

    def row(self, count, shard_rows):
        if self.shift is None:
            return self.index * self.rows
        return ring_owner(lax.axis_index("wide"), self.shift, count) * shard_rows + self.base

    def block_row(self, count, shard_rows, block):
        if self.shift is None:
            of, inside = self.index, 0
        else:
            owner = ring_owner(lax.axis_index("wide"), self.shift, count)
            per_block = block // shard_rows
            of, inside = owner // per_block, (owner % per_block) * shard_rows + self.base
        mine = lax.axis_index("narrow")
        over_x = jnp.where(of // 2 == mine // 2, 0, 1)
        over_core = jnp.where(of % 2 == mine % 2, 0, 1)
        return over_x, over_core, inside


def rows_at(start, rows):
    return pl.ds(pl.multiple_of(start, 16), rows)


def order_kernel(x_ref, o_ref):
    tokens = x_ref.shape[1]
    windows = tokens // WINDOW
    source = lax.broadcasted_iota(jnp.int32, (tokens, windows), 0)
    window = lax.broadcasted_iota(jnp.int32, (tokens, windows), 1)
    for p in range(WINDOW):
        pick = jnp.where(source == WINDOW * window + p, 1.0, 0.0).astype(BF16)
        o_ref[:, p * windows : (p + 1) * windows] = jnp.dot(
            x_ref[...], pick, preferred_element_type=F32
        ).astype(BF16)


def shards_kernel(w_out, w_proj, *outs):
    rows, width = w_proj.shape[1], w_proj.shape[2]
    half = rows // (len(outs) // 2)
    flat = jnp.concatenate([w_proj[p] for p in range(WINDOW)], axis=1)
    for i in range(len(outs) // 2):
        outs[i][...] = w_out[i * half : (i + 1) * half, :]
        outs[len(outs) // 2 + i][...] = flat[i * half : (i + 1) * half, :]


def route_kernel(relative, seq_rows, bucket, place, slots_of, targets):
    groups, windows = place.shape
    me = lax.axis_index("wide")
    table = place[...]
    owner = jnp.where(table >= 0, 0, -1)
    for d in range(1, groups):
        owner = owner + jnp.where(table >= d * seq_rows, 1, 0)
    earlier = jnp.where(
        lax.broadcasted_iota(jnp.int32, (windows, windows), 0)
        <= lax.broadcasted_iota(jnp.int32, (windows, windows), 1),
        1.0,
        0.0,
    ).astype(BF16)
    here = jnp.where(owner == me, 1.0, 0.0)
    rank = jnp.dot(here.astype(BF16), earlier, preferred_element_type=F32)
    rank = jnp.where(owner == me, rank, 0.0).astype(jnp.int32)
    local = table - me * seq_rows
    slot = lax.broadcasted_iota(jnp.int32, (bucket, windows), 0) + 1
    source_at = lax.broadcasted_iota(jnp.int32, (groups, windows), 0)
    for k in range(groups):
        wanted = source_at == ((me ^ k) if relative else k)
        of_rank = jnp.sum(jnp.where(wanted, rank, 0), axis=0, keepdims=True)
        of_local = jnp.sum(jnp.where(wanted, local, 0), axis=0, keepdims=True)
        found = jnp.where(of_rank == slot, of_local + 1, 0)
        targets[k * bucket : (k + 1) * bucket, :] = jnp.sum(found, axis=1, keepdims=True) - 1
    mine = jnp.sum(jnp.where(source_at == me, owner, 0), axis=0, keepdims=True)
    hits = source_at == mine
    rank = jnp.dot(
        jnp.where(hits, 1.0, 0.0).astype(BF16), earlier, preferred_element_type=F32
    )
    rank = jnp.sum(jnp.where(hits, rank, 0.0), axis=0, keepdims=True).astype(jnp.int32)
    towards = (mine ^ me) if relative else mine
    slots_of[...] = jnp.where(mine >= 0, towards * bucket + rank - 1, groups * bucket)


def norm_kernel(first, tokens, own, over_x, over_core, over_both, gain, bias, o_ref, whole):
    parts = (own, over_x, over_core, over_both)
    rows = own.shape[0]
    mine = lax.axis_index("narrow")
    for part, flip in zip(parts, (0, 2, 1, 3)):
        at = (mine ^ flip) * rows
        whole[rows_at(at, rows), :] = part[:, first : first + tokens]
    width = whole.shape[0]
    step = 128
    for t in range(0, tokens, step):
        values = whole[:, t : t + step].astype(F32)
        center = jnp.sum(values, axis=0, keepdims=True) * (1.0 / width)
        values = values - center
        spread = jnp.sum(values * values, axis=0, keepdims=True) * (1.0 / width)
        values = (values * lax.rsqrt(spread + 1e-06)).T
        o_ref[t : t + step, :] = (values * gain[...] + bias[...]).astype(BF16)


def hidden_kernel(pieces, count, shard_rows, first, columns, bias, *refs):
    arrays = 1 + max(p.array for p in pieces)
    sources, normed, (o_ref, part) = refs[:arrays], refs[arrays:-2], refs[-2:]
    for p in pieces:
        part[rows_at(p.row(count, shard_rows), p.rows), :] = sources[p.array][
            p.start : p.start + p.rows, first : first + columns
        ]
    at = 0
    for rows in normed:
        v = jnp.dot(rows[...], part[...], preferred_element_type=F32)
        v = v + bias[:, first : first + columns]
        o_ref[at : at + rows.shape[0], :] = (
            0.5 * v * (1.0 + lax.erf(v * (2.0**-0.5)))
        ).astype(BF16)
        at += rows.shape[0]


def out_kernel(pieces, count, shard_rows, over_x, hidden_count, *refs):
    hidden, refs = refs[:hidden_count], refs[hidden_count:]
    sources, (keep, give, part) = refs[:-3], refs[-3:]
    block, tokens = keep.shape
    for p in pieces:
        x, core, inside = p.block_row(count, shard_rows, block)

        @pl.when(x == over_x)
        def _():
            part[rows_at(core * block + inside, p.rows), :] = sources[p.array][
                p.start : p.start + p.rows, :
            ]

    columns = hidden[0].shape[1]
    step = 256
    for t in range(0, tokens, step):
        total = None
        for i, h in enumerate(hidden):
            v = lax.dot_general(
                part[:, i * columns : (i + 1) * columns],
                h[t : t + step, :],
                (((1,), (1,)), ((), ())),
                preferred_element_type=F32,
            )
            total = v if total is None else total + v
        total = total.astype(BF16)
        keep[:, t : t + step] = total[:block]
        give[:, t : t + step] = total[block:]


def proj_kernel(pieces, missing, count, shard_rows, merged, *refs):
    sources, (keep, give, part) = refs[:-3], refs[-3:]
    block = keep.shape[1]
    for p in pieces:
        x, core, inside = p.block_row(count, shard_rows, block)
        at = rows_at(core * 2 * block + x * block + inside, p.rows)
        part[at, :] = sources[p.array][p.start : p.start + p.rows, :]
    if missing is not None:
        x, core, inside = missing.block_row(count, shard_rows, block)
        at = rows_at(core * 2 * block + x * block + inside, missing.rows)
        part[at, :] = jnp.zeros((missing.rows, part.shape[1]), BF16)
    for core, target in ((1, give), (0, keep)):
        v = jnp.dot(
            part[core * 2 * block : (core + 1) * 2 * block, :],
            merged[...],
            preferred_element_type=F32,
        ).astype(BF16)
        target[0] = v[:block]
        target[1] = v[block:]


def last_kernel(first, second, merged, o_ref):
    rows = first.shape[0]
    whole = jnp.concatenate([first[...], second[...]], axis=0)
    o_ref[...] = jnp.dot(whole, merged[...], preferred_element_type=F32).astype(BF16)


def stream_kernel(own, keep, near, far, bias, o_ref):
    total = keep[...].astype(F32) + near[...].astype(F32) + far[...].astype(F32)
    stream = (own[...].astype(F32) + (total + bias[...])).astype(BF16)
    rows, windows = own.shape[0], own.shape[1] // WINDOW
    for p in range(WINDOW):
        o_ref[p * rows : (p + 1) * rows, :] = stream[:, p * windows : (p + 1) * windows]


def pack_kernel(missing, count, shard_rows, extra, slots_of, keep, near, far, bias, *refs):
    late, outs, total = refs[:extra], refs[extra:-1], refs[-1]
    total[...] = keep[0].astype(F32) + near[0].astype(F32) + far[...].astype(F32)
    if extra:
        x, core, inside = missing.block_row(count, shard_rows, total.shape[0])

        @pl.when(x + core == 0)
        def _():
            at = pl.ds(pl.multiple_of(inside, 16), missing.rows)
            added = late[0][...].astype(F32)
            for r in late[1:]:
                added = added + r[...].astype(F32)
            total[at, :] = total[at, :] + added

    vision = (total[...] + bias[...]).astype(BF16)
    slots = outs[0].shape[0]
    slot = lax.broadcasted_iota(jnp.int32, (slots * len(outs), vision.shape[1]), 0)
    pick = jnp.where(slot == slots_of[...], 1.0, 0.0).astype(BF16)
    moved = lax.dot_general(
        pick, vision, (((1,), (1,)), ((), ())), preferred_element_type=F32
    ).astype(BF16)
    for k, o_ref in enumerate(outs):
        o_ref[...] = moved[k * slots : (k + 1) * slots]


def place_kernel(targets, text, *refs):
    arrived, o_ref = refs[:-1], refs[-1]
    slots, rows = arrived[0].shape[0] * len(arrived), text.shape[1]
    row = lax.broadcasted_iota(jnp.int32, (slots, rows), 1)
    pick = jnp.where(row == targets[...], 1.0, 0.0)
    hit = jnp.sum(pick, axis=0, keepdims=True) > 0.5
    whole = jnp.concatenate([r[...] for r in arrived], axis=0)
    moved = lax.dot_general(
        whole, pick.astype(BF16), (((0,), (0,)), ((), ())), preferred_element_type=F32
    ).astype(BF16)
    o_ref[...] = jnp.where(hit, moved, text[...])


def add_kernel(keep, near, o_ref):
    o_ref[...] = (keep[...].astype(F32) + near[...].astype(F32)).astype(BF16)


class Ring:
    def __init__(self, count):
        self.count = count
        order = ring_order(count)
        self.right = [(order[i], order[(i + 1) % count]) for i in range(count)]
        self.left = [(b, a) for a, b in self.right]
        self.done = []
        self.work = []

    def step(self, to_right, to_left):
        waits = list(self.work)
        if len(self.done) >= 2:
            waits += self.done[-2]
        self.work = []
        if waits:
            to_right, to_left = lax.optimization_barrier((to_right, to_left, *waits))[:2]
        pair = (
            lax.ppermute(to_right, "wide", self.right),
            lax.ppermute(to_left, "wide", self.left),
        )
        self.done.append(pair)
        return pair

    def between(self, x):
        if len(self.done) >= 3:
            return after(x, *self.done[-3])
        return x


def per_device(
    patches, norm_gain, norm_bias, w_in, b_in, w_out, b_out, w_proj, b_proj, text, place
):
    groups, parts = lax.axis_size("wide"), lax.axis_size("narrow")
    width, tokens = patches.shape[1], patches.shape[0]
    full = width * parts
    ff = w_in.shape[1]
    windows = tokens // WINDOW
    seq_rows = text.shape[0]
    bucket = seq_rows // groups
    slots = groups * bucket
    shard_rows = [w_in.shape[0], w_out.shape[1], w_proj.shape[2]]
    small = groups == 8 and all(r % 32 == 0 for r in shard_rows)

    near_pairs = [(i, i ^ 1) for i in range(parts)]
    far_pairs = [(i, i ^ 2) for i in range(parts)]

    def near(x):
        return lax.ppermute(x, "narrow", near_pairs)

    def far(x):
        return lax.ppermute(x, "narrow", far_pairs)


    def order(x):
        return call(
            order_kernel, (x,), shape(width, tokens),
            flops=2 * width * tokens * tokens, moved=4 * width * tokens, name="order_tokens",
        )

    def shards(count):
        rows = shard_rows[1] // count
        return call(
            shards_kernel, (w_out.T, jnp.transpose(w_proj, (0, 2, 1))),
            [shape(rows, full)] * (2 * count), moved=8 * shard_rows[1] * full, name="shards",
        )

    def route():
        return call(
            functools.partial(route_kernel, small, seq_rows, bucket),
            (place.reshape(groups, windows),),
            [shape(1, windows, dtype=jnp.int32), shape(slots, 1, dtype=jnp.int32)],
            flops=4 * groups * windows * windows, moved=4 * groups * windows, name="route",
        )

    def norm(blocks, first, count):
        return call(
            functools.partial(norm_kernel, first, count),
            (*blocks, norm_gain[None], norm_bias[None]), shape(count, full),
            scratch=[pltpu.VMEM((full, count), BF16)],
            flops=10 * full * count, moved=4 * full * count, name="norm",
        )

    def hidden(pieces, arrays, normed, first, columns):
        return call(
            functools.partial(hidden_kernel, pieces, groups, shard_rows[0], first, columns),
            (b_in[None], *arrays, *normed), shape(tokens, columns),
            scratch=[pltpu.VMEM((full, columns), BF16)],
            flops=2 * tokens * full * columns,
            moved=2 * (tokens * full + full * columns + tokens * columns),
            special=tokens * columns, name="hidden",
        )

    def mlp_out(pieces, arrays, hiddens, over_x):
        return call(
            functools.partial(
                out_kernel, pieces, groups, shard_rows[1], over_x, len(hiddens)
            ),
            (*hiddens, *arrays), [shape(width, tokens)] * 2,
            scratch=[pltpu.VMEM((2 * width, ff), BF16)],
            flops=4 * tokens * width * ff, moved=2 * (tokens * ff + full * ff), name="mlp_out",
        )

    def add(keep, other):
        return call(
            add_kernel, (keep, other), shape(*keep.shape), flops=keep.size,
            moved=6 * keep.size, name="add",
        )

    def stream(own, keep, core_sums, x_sums):
        return call(
            stream_kernel, (own, keep, core_sums, x_sums, b_out[:, None]),
            shape(WINDOW * width, windows),
            flops=4 * width * tokens, moved=10 * width * tokens, name="stream",
        )

    def proj(pieces, missing, arrays, merged):
        return call(
            functools.partial(proj_kernel, pieces, missing, groups, shard_rows[2]),
            (merged, *arrays), [shape(2, width, windows)] * 2,
            scratch=[pltpu.VMEM((full, WINDOW * width), BF16)],
            flops=2 * windows * full * WINDOW * width,
            moved=2 * (full * WINDOW * width + windows * (WINDOW * width + full)), name="proj",
        )

    def pack(slots_of, missing, keep, core_sums, x_sums, late, count):
        return call(
            functools.partial(pack_kernel, missing, groups, shard_rows[2], len(late)),
            (slots_of, keep, core_sums, x_sums, b_proj[:, None], *late),
            [shape(slots // count, width)] * count,
            scratch=[pltpu.VMEM((width, windows), F32)],
            flops=2 * slots * windows * width, moved=8 * width * windows + 2 * slots * width,
            name="pack",
        )

    def placed(targets, arrived):
        return call(
            place_kernel, (targets, text.T, *arrived), shape(width, seq_rows),
            flops=2 * slots * seq_rows * width, moved=6 * width * seq_rows, name="place",
        ).T


    if not small:
        shard = [w_in, *shards(1)]
        wholes = [lax.all_gather(s, "wide", axis=0, tiled=True) for s in shard]
        rows = full // parts
        pieces = [Piece(0, k * rows, rows, None, 0, k) for k in range(parts)]
        own = order(patches.T)
        over_x = far(own)
        blocks = (own, over_x, near(own), near(over_x))
        normed = norm(blocks, 0, tokens)
        act = hidden(pieces, wholes[:1], [normed], 0, ff)
        keep_x, give_x = mlp_out(pieces, wholes[1:2], [act], 1)
        keep, give = mlp_out(pieces, wholes[1:2], [act], 0)
        x_sums = far(add(keep_x, near(give_x)))
        merged = stream(own, keep, near(give), x_sums)
        slots_of, targets = route()
        keep, give = proj(pieces, None, wholes[2:], merged)
        core_sums = near(give)
        x_sums = far(add(keep[1], core_sums[1]))
        (buffer,) = pack(slots_of, None, keep, core_sums, x_sums, (), 1)
        arrived = lax.all_to_all(
            buffer.reshape(groups, bucket, width), "wide", split_axis=0, concat_axis=0, tiled=True
        )
        return placed(targets, [arrived.reshape(slots, width)])


    ring = Ring(groups)
    half_rows = shard_rows[0] // 2
    last = groups // 2

    def gather(halves, work):
        arrays = list(halves)
        pieces = [Piece(h, 0, half_rows, 0, h * half_rows) for h in (0, 1)]
        held = {(way, h): halves[h] for way in (0, 1) for h in (0, 1)}
        t = 0
        for step in range(1, last + 1):
            for first in (0, 1):
                if step == last and first == 1:
                    continue
                pair = ring.step(held[0, first], held[1, 1 - first])
                for way, h in ((0, first), (1, 1 - first)):
                    held[way, h] = pair[way]
                    shift = -step if way == 0 else step
                    pieces.append(Piece(len(arrays), 0, half_rows, shift, h * half_rows))
                    arrays.append(pair[way])
                if t in work:
                    ring.work += work[t]()
                t += 1
        return pieces, arrays

    state = {}

    def start_tokens():
        state["own"] = order(patches.T)
        state["over_x"] = far(state["own"])
        return [state["own"]]

    def start_shards():
        state["shards"] = shards(2)
        state["over_core"] = near(state["own"])
        return [state["shards"][0]]

    def start_route():
        state["slots_of"], state["targets"] = route()
        return [state["slots_of"]]

    def send_both():
        state["over_both"] = near(state["over_x"])
        return []

    def start_norm(i):
        def run():
            blocks = [state[k] for k in ("own", "over_x", "over_core", "over_both")]
            blocks[0] = ring.between(blocks[0])
            count = tokens // 2
            state["normed", i] = norm(blocks, i * count, count)
            return [state["normed", i]]
        return run

    pieces_in, arrays_in = gather(
        [w_in[:half_rows], w_in[half_rows:]],
        {0: start_tokens, 1: start_shards, 2: start_route, 4: send_both, 5: start_norm(0),
         6: start_norm(1)},
    )

    columns = 256
    hiddens = []

    def start_hidden(i):
        def run():
            normed = [state["normed", 0], state["normed", 1]]
            normed[0] = ring.between(normed[0])
            hiddens.append(hidden(pieces_in, arrays_in, normed, i * columns, columns))
            return [hiddens[-1]]
        return run

    pieces_out, arrays_out = gather(
        state["shards"][:2], {i + 1: start_hidden(i) for i in range(ff // columns)}
    )

    def start_out(over_x):
        def run():
            acts = [ring.between(hiddens[0]), *hiddens[1:]]
            keep, give = mlp_out(pieces_out, arrays_out, acts, over_x)
            state["keep", over_x] = keep
            state["core", over_x] = near(give)
            return [keep]
        return run

    def start_sums():
        state["x_give"] = add(state["keep", 1], state["core", 1])
        state["x_sums"] = far(state["x_give"])
        return [state["x_give"]]

    pieces_proj, arrays_proj = gather(
        state["shards"][2:], {1: start_out(1), 2: start_out(0), 3: start_sums}
    )

    merged = stream(state["own"], state["keep", 0], state["core", 0], state["x_sums"])
    missing = Piece(0, 0, shard_rows[2], last, 0)
    keep, give = proj(pieces_proj[:-2], missing, arrays_proj[:-2], merged)
    core_sums = near(give)
    x_sums = far(add(keep[1], core_sums[1]))

    halves = sorted(pieces_proj[-2:], key=lambda p: p.base)
    late = call(
        last_kernel, (*[arrays_proj[p.array] for p in halves], merged),
        shape(shard_rows[2], windows), flops=2 * windows * shard_rows[2] * WINDOW * width,
        moved=2 * WINDOW * width * (shard_rows[2] + windows), name="proj_last",
    )
    order_of = ring_order(groups)
    keeper = [
        order_of[(order_of.index(w) + last) % groups] * shard_rows[2] // width
        for w in range(groups)
    ]
    lates = [late]
    for flip in range(1, parts):
        pairs = [(w * parts + (keeper[w] ^ flip), w * parts + keeper[w]) for w in range(groups)]
        lates.append(lax.ppermute(late, ("wide", "narrow"), pairs))

    out_blocks = pack(state["slots_of"], missing, keep, core_sums, x_sums, lates, groups)
    arrived = [out_blocks[0]]
    for k in range(1, groups):
        arrived.append(lax.ppermute(out_blocks[k], "wide", [(w, w ^ k) for w in range(groups)]))
    return placed(state["targets"], arrived)


def solution(mesh):
    placed = (
        P("wide", "narrow"),
        P(),
        P(),
        P("wide", "narrow"),
        P("narrow"),
        P("narrow", "wide"),
        P("narrow"),
        P(None, "narrow", "wide"),
        P("narrow"),
        P("wide", "narrow"),
        P(),
    )
    return jax.shard_map(
        per_device, mesh=mesh, in_specs=placed, out_specs=P("wide", "narrow"), check_vma=False
    )
```

```python
import functools

import jax
import jax.numpy as jnp
from jax import lax
from jax.experimental import pallas as pl
from jax.experimental.pallas import tpu as pltpu
from jax.sharding import PartitionSpec as P

F32 = jnp.float32
BF16 = jnp.bfloat16
WINDOW = 4
VMEM = pl.BlockSpec(memory_space=pltpu.VMEM)


def call(kernel, operands, outs, scratch=(), name=None):
    single = not isinstance(outs, (list, tuple))
    return pl.pallas_call(
        kernel,
        out_shape=outs,
        in_specs=[VMEM] * len(operands),
        out_specs=VMEM if single else [VMEM] * len(outs),
        scratch_shapes=list(scratch),
        compiler_params=pltpu.CompilerParams(vmem_limit_bytes=28 * 1024 * 1024),
        cost_estimate=pl.CostEstimate(flops=0, bytes_accessed=0, transcendentals=0),
        name=name,
    )(*operands)


def shape(*dims, dtype=BF16):
    return jax.ShapeDtypeStruct(dims, dtype)


def after(x, *others):
    return lax.optimization_barrier((x, *others))[0]


def ring_order(count):
    return list(range(0, count, 2)) + list(range(count - 1, 0, -2))


def ring_owner(me, shift, count):
    half = me // 2
    at = jnp.where(me % 2 == 0, half, count - 1 - half) + (shift + count)
    at = at % count
    return jnp.where(at < count // 2, 2 * at, 2 * (count - 1 - at) + 1)


class Piece:
    def __init__(self, array, start, rows, shift, base, index=0):
        self.array, self.start, self.rows = array, start, rows
        self.shift, self.base, self.index = shift, base, index

    def row(self, count, shard_rows):
        if self.shift is None:
            return self.index * self.rows
        return ring_owner(lax.axis_index("wide"), self.shift, count) * shard_rows + self.base

    def block_row(self, count, shard_rows, block):
        if self.shift is None:
            of, inside = self.index, 0
        else:
            owner = ring_owner(lax.axis_index("wide"), self.shift, count)
            per_block = block // shard_rows
            of, inside = owner // per_block, (owner % per_block) * shard_rows + self.base
        mine = lax.axis_index("narrow")
        over_x = jnp.where(of // 2 == mine // 2, 0, 1)
        over_core = jnp.where(of % 2 == mine % 2, 0, 1)
        return over_x, over_core, inside


def rows_at(start, rows):
    return pl.ds(pl.multiple_of(start, 16), rows)


def order_kernel(x_ref, *outs):
    tokens = x_ref.shape[1]
    windows = tokens // WINDOW
    source = lax.broadcasted_iota(jnp.int32, (tokens, windows), 0)
    window = lax.broadcasted_iota(jnp.int32, (tokens, windows), 1)
    each = WINDOW // len(outs)
    for p in range(WINDOW):
        pick = jnp.where(source == WINDOW * window + p, 1.0, 0.0).astype(BF16)
        outs[p // each][p % each] = jnp.dot(
            x_ref[...], pick, preferred_element_type=F32
        ).astype(BF16)


def shards_kernel(w_out, w_proj, *outs):
    rows, width = w_proj.shape[1], w_proj.shape[2]
    half = rows // (len(outs) // 2)
    flat = jnp.concatenate([w_proj[p] for p in range(WINDOW)], axis=1)
    for i in range(len(outs) // 2):
        outs[i][...] = w_out[i * half : (i + 1) * half, :]
        outs[len(outs) // 2 + i][...] = flat[i * half : (i + 1) * half, :]


def route_kernel(seq_rows, bucket, place, slots_of, targets):
    groups, windows = place.shape
    me = lax.axis_index("wide")
    table = place[...]
    owner = jnp.where(table >= 0, 0, -1)
    for d in range(1, groups):
        owner = owner + jnp.where(table >= d * seq_rows, 1, 0)
    earlier = jnp.where(
        lax.broadcasted_iota(jnp.int32, (windows, windows), 0)
        <= lax.broadcasted_iota(jnp.int32, (windows, windows), 1),
        1.0,
        0.0,
    ).astype(BF16)
    here = jnp.where(owner == me, 1.0, 0.0)
    rank = jnp.dot(here.astype(BF16), earlier, preferred_element_type=F32)
    rank = jnp.where(owner == me, rank, 0.0).astype(jnp.int32)
    local = table - me * seq_rows
    slot = lax.broadcasted_iota(jnp.int32, (bucket, windows), 0) + 1
    source_at = lax.broadcasted_iota(jnp.int32, (groups, windows), 0)
    for k in range(groups):
        wanted = source_at == k
        of_rank = jnp.sum(jnp.where(wanted, rank, 0), axis=0, keepdims=True)
        of_local = jnp.sum(jnp.where(wanted, local, 0), axis=0, keepdims=True)
        found = jnp.where(of_rank == slot, of_local + 1, 0)
        targets[k * bucket : (k + 1) * bucket, :] = jnp.sum(found, axis=1, keepdims=True) - 1
    mine = jnp.sum(jnp.where(source_at == me, owner, 0), axis=0, keepdims=True)
    hits = source_at == mine
    rank = jnp.dot(
        jnp.where(hits, 1.0, 0.0).astype(BF16), earlier, preferred_element_type=F32
    )
    rank = jnp.sum(jnp.where(hits, rank, 0.0), axis=0, keepdims=True).astype(jnp.int32)
    slots_of[...] = jnp.where(mine >= 0, mine * bucket + rank - 1, groups * bucket)


def norm_kernel(own, over_x, over_core, over_both, gain, bias, o_ref, whole):
    parts = (own, over_x, over_core, over_both)
    each, rows, windows = own.shape
    tokens = each * windows
    mine = lax.axis_index("narrow")
    for part, flip in zip(parts, (0, 2, 1, 3)):
        at = (mine ^ flip) * rows
        for j in range(each):
            whole[rows_at(at, rows), j * windows : (j + 1) * windows] = part[j]
    width = whole.shape[0]
    step = 128
    for t in range(0, tokens, step):
        values = whole[:, t : t + step].astype(F32)
        center = jnp.sum(values, axis=0, keepdims=True) * (1.0 / width)
        values = values - center
        spread = jnp.sum(values * values, axis=0, keepdims=True) * (1.0 / width)
        values = (values * lax.rsqrt(spread + 1e-06)).T
        o_ref[t : t + step, :] = (values * gain[...] + bias[...]).astype(BF16)


def hidden_kernel(pieces, count, shard_rows, first, columns, bias, *refs):
    arrays = 1 + max(p.array for p in pieces)
    sources, normed, (o_ref, part) = refs[:arrays], refs[arrays:-2], refs[-2:]
    for p in pieces:
        part[rows_at(p.row(count, shard_rows), p.rows), :] = sources[p.array][
            p.start : p.start + p.rows, first : first + columns
        ]
    at = 0
    for rows in normed:
        v = jnp.dot(rows[...], part[...], preferred_element_type=F32)
        v = v + bias[:, first : first + columns]
        o_ref[at : at + rows.shape[0], :] = (
            0.5 * v * (1.0 + lax.erf(v * (2.0**-0.5)))
        ).astype(BF16)
        at += rows.shape[0]


def out_kernel(pieces, count, shard_rows, over_x, hidden_count, chunks, *refs):
    hidden, refs = refs[:hidden_count], refs[hidden_count:]
    outs, part = refs[-1 - 2 * chunks : -1], refs[-1]
    keep, give = outs[:chunks], outs[chunks:]
    sources = refs[: -1 - 2 * chunks]
    block, tokens = keep[0].shape
    for p in pieces:
        x, core, inside = p.block_row(count, shard_rows, block)

        @pl.when(x == over_x)
        def _():
            part[rows_at(core * block + inside, p.rows), :] = sources[p.array][
                p.start : p.start + p.rows, :
            ]

    columns = hidden[0].shape[1]
    step = 256
    for t in range(0, tokens * chunks, step):
        total = None
        for i, h in enumerate(hidden):
            v = lax.dot_general(
                part[:, i * columns : (i + 1) * columns],
                h[t : t + step, :],
                (((1,), (1,)), ((), ())),
                preferred_element_type=F32,
            )
            total = v if total is None else total + v
        total = total.astype(BF16)
        c, at = t // tokens, t % tokens
        keep[c][:, at : at + step] = total[:block]
        give[c][:, at : at + step] = total[block:]


def proj_kernel(pieces, missing, count, shard_rows, merged, *refs):
    sources, (keep, give, part) = refs[:-3], refs[-3:]
    block = keep.shape[1]
    for p in pieces:
        x, core, inside = p.block_row(count, shard_rows, block)
        at = rows_at(core * 2 * block + x * block + inside, p.rows)
        part[at, :] = sources[p.array][p.start : p.start + p.rows, :]
    if missing is not None:
        x, core, inside = missing.block_row(count, shard_rows, block)
        at = rows_at(core * 2 * block + x * block + inside, missing.rows)
        part[at, :] = jnp.zeros((missing.rows, part.shape[1]), BF16)
    for core, target in ((1, give), (0, keep)):
        v = jnp.dot(
            part[core * 2 * block : (core + 1) * 2 * block, :],
            merged[...],
            preferred_element_type=F32,
        ).astype(BF16)
        target[0] = v[:block]
        target[1] = v[block:]


def last_kernel(first, second, merged, o_ref):
    rows = first.shape[0]
    whole = jnp.concatenate([first[...], second[...]], axis=0)
    o_ref[...] = jnp.dot(whole, merged[...], preferred_element_type=F32).astype(BF16)


def stream_kernel(chunks, bias, *refs):
    o_ref = refs[-1]
    own, keep, near, far = (refs[i * chunks : (i + 1) * chunks] for i in range(4))
    each, rows, windows = own[0].shape
    for c in range(chunks):
        total = keep[c][...].astype(F32) + near[c][...].astype(F32) + far[c][...].astype(F32)
        total = total + bias[...]
        for j in range(each):
            v = own[c][j].astype(F32) + total[:, j * windows : (j + 1) * windows]
            p = c * each + j
            o_ref[p * rows : (p + 1) * rows, :] = v.astype(BF16)


LANES = 128


def compact(width, bucket):
    rest = width % LANES
    return rest > 0 and LANES % rest == 0 and bucket % (16 * (LANES // rest)) == 0


def pack_kernel(missing, count, shard_rows, groups, extra, slots_of, keep, near, far, bias, *refs):
    late, o_ref, total = refs[:extra], refs[-2], refs[-1]
    total[...] = keep[0].astype(F32) + near[0].astype(F32) + far[...].astype(F32)
    if extra:
        x, core, inside = missing.block_row(count, shard_rows, total.shape[0])

        @pl.when(x + core == 0)
        def _():
            at = pl.ds(pl.multiple_of(inside, 16), missing.rows)
            added = late[0][...].astype(F32)
            for r in late[1:]:
                added = added + r[...].astype(F32)
            total[at, :] = total[at, :] + added

    vision = (total[...] + bias[...]).astype(BF16)
    width = vision.shape[0]
    bucket = o_ref.shape[1] * o_ref.shape[2] // width
    slot = lax.broadcasted_iota(jnp.int32, (groups * bucket, vision.shape[1]), 0)
    pick = jnp.where(slot == slots_of[...], 1.0, 0.0).astype(BF16)
    moved = lax.dot_general(
        pick, vision, (((1,), (1,)), ((), ())), preferred_element_type=F32
    ).astype(BF16)
    for k in range(groups):
        rows = moved[k * bucket : (k + 1) * bucket]
        if o_ref.shape[2] == width:
            o_ref[k] = rows
            continue
        tiles = width // LANES
        for i in range(tiles):
            o_ref[k, i * bucket : (i + 1) * bucket, :] = rows[:, i * LANES : (i + 1) * LANES]
        rest = rows[:, tiles * LANES :]
        fold = LANES // rest.shape[1]
        piece = bucket // fold
        o_ref[k, tiles * bucket :, :] = jnp.concatenate(
            [rest[i * piece : (i + 1) * piece] for i in range(fold)], axis=1
        )


def place_kernel(targets, text, arrived, o_ref):
    width, rows = text.shape
    groups = arrived.shape[0]
    bucket = arrived.shape[1] * arrived.shape[2] // width
    slots = groups * bucket
    row = lax.broadcasted_iota(jnp.int32, (slots, rows), 1)
    pick = jnp.where(row == targets[...], 1.0, 0.0)
    hit = jnp.sum(pick, axis=0, keepdims=True) > 0.5
    pick = pick.astype(BF16)

    def moved(blocks):
        return lax.dot_general(
            blocks, pick, (((0,), (0,)), ((), ())), preferred_element_type=F32
        ).astype(BF16)

    if arrived.shape[2] == width:
        whole = jnp.concatenate([arrived[k] for k in range(groups)], axis=0)
        o_ref[...] = jnp.where(hit, moved(whole), text[...])
        return
    tiles = width // LANES
    for i in range(tiles):
        part = jnp.concatenate(
            [arrived[k, i * bucket : (i + 1) * bucket, :] for k in range(groups)], axis=0
        )
        at = slice(i * LANES, (i + 1) * LANES)
        o_ref[at, :] = jnp.where(hit, moved(part), text[at, :])
    rest = width % LANES
    parts = []
    for k in range(groups):
        folded = arrived[k, tiles * bucket :, :]
        parts += [folded[:, i * rest : (i + 1) * rest] for i in range(LANES // rest)]
    at = slice(tiles * LANES, width)
    o_ref[at, :] = jnp.where(hit, moved(jnp.concatenate(parts, axis=0)), text[at, :])


def add_kernel(keep, near, o_ref):
    o_ref[...] = (keep[...].astype(F32) + near[...].astype(F32)).astype(BF16)


class Ring:
    def __init__(self, count):
        self.count = count
        order = ring_order(count)
        self.right = [(order[i], order[(i + 1) % count]) for i in range(count)]
        self.left = [(b, a) for a, b in self.right]
        self.done = []
        self.work = []

    def step(self, to_right, to_left):
        t = len(self.done)
        waits = [x for at, x in self.work if at == t - 2]
        if t >= 2:
            to_right = after(to_right, self.done[t - 2][0], *waits)
            to_left = after(to_left, self.done[t - 2][1])
        pair = (
            lax.ppermute(to_right, "wide", self.right),
            lax.ppermute(to_left, "wide", self.left),
        )
        self.done.append(pair)
        return pair

    def now(self, x):
        if len(self.done) >= 2:
            return after(x, *self.done[-2])
        return x

    def add_work(self, x):
        self.work.append((len(self.done) - 1, x))


def per_device(
    patches, norm_gain, norm_bias, w_in, b_in, w_out, b_out, w_proj, b_proj, text, place
):
    groups, parts = lax.axis_size("wide"), lax.axis_size("narrow")
    width, tokens = patches.shape[1], patches.shape[0]
    full = width * parts
    ff = w_in.shape[1]
    windows = tokens // WINDOW
    seq_rows = text.shape[0]
    bucket = seq_rows // groups
    slots = groups * bucket
    shard_rows = [w_in.shape[0], w_out.shape[1], w_proj.shape[2]]
    small = groups == 8 and all(r % 32 == 0 for r in shard_rows)
    chunks = 2

    near_pairs = [(i, i ^ 1) for i in range(parts)]
    far_pairs = [(i, i ^ 2) for i in range(parts)]

    def near(x):
        return lax.ppermute(x, "narrow", near_pairs)

    def far(x):
        return lax.ppermute(x, "narrow", far_pairs)


    def order(x):
        return call(
            order_kernel, (x,), [shape(WINDOW // chunks, width, windows)] * chunks,
            name="order_tokens",
        )

    def shards(count):
        rows = shard_rows[1] // count
        return call(
            shards_kernel, (w_out.T, jnp.transpose(w_proj, (0, 2, 1))),
            [shape(rows, full)] * (2 * count), name="shards",
        )

    def route():
        return call(
            functools.partial(route_kernel, seq_rows, bucket), (place.reshape(groups, windows),),
            [shape(1, windows, dtype=jnp.int32), shape(slots, 1, dtype=jnp.int32)], name="route",
        )

    def norm(blocks):
        count = tokens // chunks
        return call(
            norm_kernel, (*blocks, norm_gain[None], norm_bias[None]), shape(count, full),
            scratch=[pltpu.VMEM((full, count), BF16)], name="norm",
        )

    def hidden(pieces, arrays, normed, first, columns):
        return call(
            functools.partial(hidden_kernel, pieces, groups, shard_rows[0], first, columns),
            (b_in[None], *arrays, *normed), shape(tokens, columns),
            scratch=[pltpu.VMEM((full, columns), BF16)], name="hidden",
        )

    def mlp_out(pieces, arrays, hiddens, over_x):
        outs = call(
            functools.partial(
                out_kernel, pieces, groups, shard_rows[1], over_x, len(hiddens), chunks
            ),
            (*hiddens, *arrays), [shape(width, tokens // chunks)] * (2 * chunks),
            scratch=[pltpu.VMEM((2 * width, ff), BF16)], name="mlp_out",
        )
        return outs[:chunks], outs[chunks:]

    def add(keep, other):
        return call(add_kernel, (keep, other), shape(*keep.shape), name="add")

    def stream(own, keep, core_sums, x_sums):
        return call(
            functools.partial(stream_kernel, chunks),
            (b_out[:, None], *own, *keep, *core_sums, *x_sums),
            shape(WINDOW * width, windows), name="stream",
        )

    def proj(pieces, missing, arrays, merged):
        return call(
            functools.partial(proj_kernel, pieces, missing, groups, shard_rows[2]),
            (merged, *arrays), [shape(2, width, windows)] * 2,
            scratch=[pltpu.VMEM((full, WINDOW * width), BF16)], name="proj",
        )

    def pack(slots_of, missing, keep, core_sums, x_sums, late):
        block = (bucket, width)
        if compact(width, bucket):
            block = (bucket * width // LANES, LANES)
        return call(
            functools.partial(pack_kernel, missing, groups, shard_rows[2], groups, len(late)),
            (slots_of, keep, core_sums, x_sums, b_proj[:, None], *late), shape(groups, *block),
            scratch=[pltpu.VMEM((width, windows), F32)], name="pack",
        )

    def exchange_and_place(buffer, targets):
        arrived = lax.all_to_all(buffer, "wide", split_axis=0, concat_axis=0, tiled=True)
        return call(
            place_kernel, (targets, text.T, arrived), shape(width, seq_rows), name="place"
        ).T


    if not small:
        shard = [w_in, *shards(1)]
        wholes = [lax.all_gather(s, "wide", axis=0, tiled=True) for s in shard]
        pieces = [Piece(0, k * width, width, None, 0, k) for k in range(parts)]
        own = order(patches.T)
        over_x = [far(x) for x in own]
        normed = [norm((x, y, near(x), near(y))) for x, y in zip(own, over_x)]
        act = hidden(pieces, wholes[:1], normed, 0, ff)
        keep_x, give_x = mlp_out(pieces, wholes[1:2], [act], 1)
        keep, give = mlp_out(pieces, wholes[1:2], [act], 0)
        x_sums = [far(add(k, near(g))) for k, g in zip(keep_x, give_x)]
        merged = stream(own, keep, [near(g) for g in give], x_sums)
        slots_of, targets = route()
        keep, give = proj(pieces, None, wholes[2:], merged)
        core_sums = near(give)
        x_sums = far(add(keep[1], core_sums[1]))
        return exchange_and_place(pack(slots_of, None, keep, core_sums, x_sums, ()), targets)


    ring = Ring(groups)
    half_rows = shard_rows[0] // 2
    last = groups // 2

    def gather(halves, work):
        arrays = list(halves)
        pieces = [Piece(h, 0, half_rows, 0, h * half_rows) for h in (0, 1)]
        held = {(way, h): halves[h] for way in (0, 1) for h in (0, 1)}
        t = 0
        for step in range(1, last + 1):
            for first in (0, 1):
                if step == last and first == 1:
                    continue
                pair = ring.step(held[0, first], held[1, 1 - first])
                for way, h in ((0, first), (1, 1 - first)):
                    held[way, h] = pair[way]
                    shift = -step if way == 0 else step
                    pieces.append(Piece(len(arrays), 0, half_rows, shift, h * half_rows))
                    arrays.append(pair[way])
                if t in work:
                    work[t]()
                t += 1
        return pieces, arrays

    own, over_x, over_core, over_both, normed = [], [], [], [], []
    got = {}

    def start_tokens():
        own.extend(order(patches.T))
        over_x.append(far(own[0]))
        ring.add_work(own[0])

    def start_shards():
        got["shards"] = shards(2)
        ring.add_work(got["shards"][0])
        over_core.extend(near(x) for x in own)

    def send_second():
        over_x.append(far(ring.now(own[1])))
        got["slots_of"], got["targets"] = route()

    def send_both():
        over_both.append(near(ring.now(over_x[len(over_both)])))

    def start_norm():
        i = len(normed)
        first = ring.now(own[i])
        normed.append(norm((first, over_x[i], over_core[i], over_both[i])))
        ring.add_work(normed[i])

    def both_and_norm():
        send_both()
        start_norm()

    pieces_in, arrays_in = gather(
        [w_in[:half_rows], w_in[half_rows:]],
        {0: start_tokens, 1: start_shards, 2: send_second, 4: send_both, 5: both_and_norm,
         6: start_norm},
    )

    columns = 256
    hiddens = []

    def start_hidden():
        rows = [ring.now(normed[0]), *normed[1:]]
        hiddens.append(hidden(pieces_in, arrays_in, rows, len(hiddens) * columns, columns))
        ring.add_work(hiddens[-1])

    pieces_out, arrays_out = gather(
        got["shards"][:2], {t: start_hidden for t in range(ff // columns)}
    )

    def start_out(over_x):
        acts = [ring.now(hiddens[0]), *hiddens[1:]]
        keep, give = mlp_out(pieces_out, arrays_out, acts, over_x)
        got["keep", over_x] = keep
        got["core", over_x] = [near(g) for g in give]
        ring.add_work(keep[0])

    def start_sums():
        core = [ring.now(got["core", 1][0]), *got["core", 1][1:]]
        sums = [add(k, c) for k, c in zip(got["keep", 1], core)]
        got["x_sums"] = [far(x) for x in sums]
        ring.add_work(sums[0])
        start_out(0)

    pieces_proj, arrays_proj = gather(
        got["shards"][2:], {0: lambda: start_out(1), 1: start_sums}
    )

    merged = stream(own, got["keep", 0], got["core", 0], got["x_sums"])
    missing = Piece(0, 0, shard_rows[2], last, 0)
    keep, give = proj(pieces_proj[:-2], missing, arrays_proj[:-2], merged)
    core_sums = near(give)
    x_sums = far(add(keep[1], core_sums[1]))

    halves = sorted(pieces_proj[-2:], key=lambda p: p.base)
    late = call(
        last_kernel, (*[arrays_proj[p.array] for p in halves], merged),
        shape(shard_rows[2], windows), name="proj_last",
    )
    order_of = ring_order(groups)
    keeper = [
        order_of[(order_of.index(w) + last) % groups] * shard_rows[2] // width
        for w in range(groups)
    ]
    lates = [late]
    for flip in range(1, parts):
        pairs = [(w * parts + (keeper[w] ^ flip), w * parts + keeper[w]) for w in range(groups)]
        lates.append(lax.ppermute(late, ("wide", "narrow"), pairs))

    buffer = pack(got["slots_of"], missing, keep, core_sums, x_sums, lates)
    return exchange_and_place(buffer, got["targets"])


def solution(mesh):
    placed = (
        P("wide", "narrow"),
        P(),
        P(),
        P("wide", "narrow"),
        P("narrow"),
        P("narrow", "wide"),
        P("narrow"),
        P(None, "narrow", "wide"),
        P("narrow"),
        P("wide", "narrow"),
        P(),
    )
    return jax.shard_map(
        per_device, mesh=mesh, in_specs=placed, out_specs=P("wide", "narrow"), check_vma=False
    )
```

```python
import functools

import jax
import jax.numpy as jnp
from jax import lax
from jax.experimental import pallas as pl
from jax.experimental.pallas import tpu as pltpu
from jax.sharding import PartitionSpec as P

F32 = jnp.float32
BF16 = jnp.bfloat16
WINDOW = 4
LATE = (1, 2, 3)
VMEM = pl.BlockSpec(memory_space=pltpu.VMEM)


def call(kernel, operands, outs, scratch=(), name=None):
    single = not isinstance(outs, (list, tuple))
    return pl.pallas_call(
        kernel,
        out_shape=outs,
        in_specs=[VMEM] * len(operands),
        out_specs=VMEM if single else [VMEM] * len(outs),
        scratch_shapes=list(scratch),
        compiler_params=pltpu.CompilerParams(vmem_limit_bytes=28 * 1024 * 1024),
        cost_estimate=pl.CostEstimate(flops=0, bytes_accessed=0, transcendentals=0),
        name=name,
    )(*operands)


def shape(*dims, dtype=BF16):
    return jax.ShapeDtypeStruct(dims, dtype)


def after(x, *others):
    return lax.optimization_barrier((x, *others))[0]


def ring_order(count):
    return list(range(0, count, 2)) + list(range(count - 1, 0, -2))


def ring_owner(me, shift, count):
    half = me // 2
    at = jnp.where(me % 2 == 0, half, count - 1 - half) + (shift + count)
    at = at % count
    return jnp.where(at < count // 2, 2 * at, 2 * (count - 1 - at) + 1)


class Piece:
    def __init__(self, array, start, rows, shift, base, index=0):
        self.array, self.start, self.rows = array, start, rows
        self.shift, self.base, self.index = shift, base, index

    def row(self, count, shard_rows):
        if self.shift is None:
            return self.index * self.rows
        return ring_owner(lax.axis_index("wide"), self.shift, count) * shard_rows + self.base

    def block_row(self, count, shard_rows, block):
        if self.shift is None:
            of, inside = self.index, 0
        else:
            owner = ring_owner(lax.axis_index("wide"), self.shift, count)
            per_block = block // shard_rows
            of, inside = owner // per_block, (owner % per_block) * shard_rows + self.base
        mine = lax.axis_index("narrow")
        over_x = jnp.where(of // 2 == mine // 2, 0, 1)
        over_core = jnp.where(of % 2 == mine % 2, 0, 1)
        return over_x, over_core, inside


def rows_at(start, rows):
    return pl.ds(pl.multiple_of(start, 16), rows)


def order_kernel(x_ref, *outs):
    tokens = x_ref.shape[1]
    windows = tokens // WINDOW
    source = lax.broadcasted_iota(jnp.int32, (tokens, windows), 0)
    window = lax.broadcasted_iota(jnp.int32, (tokens, windows), 1)
    each = WINDOW // len(outs)
    for p in range(WINDOW):
        pick = jnp.where(source == WINDOW * window + p, 1.0, 0.0).astype(BF16)
        outs[p // each][p % each] = jnp.dot(
            x_ref[...], pick, preferred_element_type=F32
        ).astype(BF16)


def shards_kernel(w_out, w_proj, *outs):
    rows, width = w_proj.shape[1], w_proj.shape[2]
    half = rows // (len(outs) // 2)
    flat = jnp.concatenate([w_proj[p] for p in range(WINDOW)], axis=1)
    for i in range(len(outs) // 2):
        outs[i][...] = w_out[i * half : (i + 1) * half, :]
        outs[len(outs) // 2 + i][...] = flat[i * half : (i + 1) * half, :]


def route_kernel(seq_rows, bucket, place, slots_of, targets):
    groups, windows = place.shape
    me = lax.axis_index("wide")
    table = place[...]
    owner = jnp.where(table >= 0, 0, -1)
    for d in range(1, groups):
        owner = owner + jnp.where(table >= d * seq_rows, 1, 0)
    earlier = jnp.where(
        lax.broadcasted_iota(jnp.int32, (windows, windows), 0)
        <= lax.broadcasted_iota(jnp.int32, (windows, windows), 1),
        1.0,
        0.0,
    ).astype(BF16)
    here = jnp.where(owner == me, 1.0, 0.0)
    rank = jnp.dot(here.astype(BF16), earlier, preferred_element_type=F32)
    rank = jnp.where(owner == me, rank, 0.0).astype(jnp.int32)
    local = table - me * seq_rows
    slot = lax.broadcasted_iota(jnp.int32, (bucket, windows), 0) + 1
    source_at = lax.broadcasted_iota(jnp.int32, (groups, windows), 0)
    for k in range(groups):
        wanted = source_at == k
        of_rank = jnp.sum(jnp.where(wanted, rank, 0), axis=0, keepdims=True)
        of_local = jnp.sum(jnp.where(wanted, local, 0), axis=0, keepdims=True)
        found = jnp.where(of_rank == slot, of_local + 1, 0)
        targets[k * bucket : (k + 1) * bucket, :] = jnp.sum(found, axis=1, keepdims=True) - 1
    mine = jnp.sum(jnp.where(source_at == me, owner, 0), axis=0, keepdims=True)
    hits = source_at == mine
    rank = jnp.dot(
        jnp.where(hits, 1.0, 0.0).astype(BF16), earlier, preferred_element_type=F32
    )
    rank = jnp.sum(jnp.where(hits, rank, 0.0), axis=0, keepdims=True).astype(jnp.int32)
    slots_of[...] = jnp.where(mine >= 0, mine * bucket + rank - 1, groups * bucket)


def norm_kernel(own, over_x, over_core, over_both, gain, bias, o_ref, whole):
    parts = (own, over_x, over_core, over_both)
    each, rows, windows = own.shape
    tokens = each * windows
    mine = lax.axis_index("narrow")
    for part, flip in zip(parts, (0, 2, 1, 3)):
        at = (mine ^ flip) * rows
        for j in range(each):
            whole[rows_at(at, rows), j * windows : (j + 1) * windows] = part[j]
    width = whole.shape[0]
    step = 128
    for t in range(0, tokens, step):
        values = whole[:, t : t + step].astype(F32)
        center = jnp.sum(values, axis=0, keepdims=True) * (1.0 / width)
        values = values - center
        spread = jnp.sum(values * values, axis=0, keepdims=True) * (1.0 / width)
        values = (values * lax.rsqrt(spread + 1e-06)).T
        o_ref[t : t + step, :] = (values * gain[...] + bias[...]).astype(BF16)


def hidden_kernel(pieces, count, shard_rows, first, columns, bias, *refs):
    arrays = 1 + max(p.array for p in pieces)
    sources, normed, (o_ref, part) = refs[:arrays], refs[arrays:-2], refs[-2:]
    for p in pieces:
        part[rows_at(p.row(count, shard_rows), p.rows), :] = sources[p.array][
            p.start : p.start + p.rows, first : first + columns
        ]
    at = 0
    for rows in normed:
        v = jnp.dot(rows[...], part[...], preferred_element_type=F32)
        v = v + bias[:, first : first + columns]
        o_ref[at : at + rows.shape[0], :] = (
            0.5 * v * (1.0 + lax.erf(v * (2.0**-0.5)))
        ).astype(BF16)
        at += rows.shape[0]


def out_kernel(pieces, count, shard_rows, over_x, hidden_count, chunks, *refs):
    hidden, refs = refs[:hidden_count], refs[hidden_count:]
    outs, part = refs[-1 - 2 * chunks : -1], refs[-1]
    keep, give = outs[:chunks], outs[chunks:]
    sources = refs[: -1 - 2 * chunks]
    block, tokens = keep[0].shape
    for p in pieces:
        x, core, inside = p.block_row(count, shard_rows, block)

        @pl.when(x == over_x)
        def _():
            part[rows_at(core * block + inside, p.rows), :] = sources[p.array][
                p.start : p.start + p.rows, :
            ]

    columns = hidden[0].shape[1]
    step = 256
    for t in range(0, tokens * chunks, step):
        total = None
        for i, h in enumerate(hidden):
            v = lax.dot_general(
                part[:, i * columns : (i + 1) * columns],
                h[t : t + step, :],
                (((1,), (1,)), ((), ())),
                preferred_element_type=F32,
            )
            total = v if total is None else total + v
        total = total.astype(BF16)
        c, at = t // tokens, t % tokens
        keep[c][:, at : at + step] = total[:block]
        give[c][:, at : at + step] = total[block:]


def proj_kernel(pieces, count, shard_rows, merged, *refs):
    sources, (keep, give, part) = refs[:-3], refs[-3:]
    block = keep.shape[1]
    for p in pieces:
        x, core, inside = p.block_row(count, shard_rows, block)
        at = rows_at(core * 2 * block + x * block + inside, p.rows)
        part[at, :] = sources[p.array][p.start : p.start + p.rows, :]
    for core, target in ((1, give), (0, keep)):
        v = jnp.dot(
            part[core * 2 * block : (core + 1) * 2 * block, :],
            merged[...],
            preferred_element_type=F32,
        ).astype(BF16)
        target[0] = v[:block]
        target[1] = v[block:]


def stream_kernel(chunks, bias, *refs):
    o_ref = refs[-1]
    own = refs[:chunks]
    keep, near, far = (
        refs[chunks + i * WINDOW : chunks + (i + 1) * WINDOW] for i in range(3)
    )
    each, rows, windows = own[0].shape
    for p in range(WINDOW):
        total = keep[p][...].astype(F32) + near[p][...].astype(F32) + far[p][...].astype(F32)
        v = own[p // each][p % each].astype(F32) + (total + bias[...])
        o_ref[p * rows : (p + 1) * rows, :] = v.astype(BF16)


LANES = 128


def compact(width, bucket):
    rest = width % LANES
    return rest > 0 and LANES % rest == 0 and bucket % (16 * (LANES // rest)) == 0


def pack_kernel(groups, slots_of, keep, near, far, bias, o_ref):
    total = keep[0].astype(F32) + near[0].astype(F32) + far[...].astype(F32)
    vision = (total + bias[...]).astype(BF16)
    width = vision.shape[0]
    bucket = o_ref.shape[1] * o_ref.shape[2] // width
    slot = lax.broadcasted_iota(jnp.int32, (groups * bucket, vision.shape[1]), 0)
    pick = jnp.where(slot == slots_of[...], 1.0, 0.0).astype(BF16)
    moved = lax.dot_general(
        pick, vision, (((1,), (1,)), ((), ())), preferred_element_type=F32
    ).astype(BF16)
    for k in range(groups):
        rows = moved[k * bucket : (k + 1) * bucket]
        if o_ref.shape[2] == width:
            o_ref[k] = rows
            continue
        tiles = width // LANES
        for i in range(tiles):
            o_ref[k, i * bucket : (i + 1) * bucket, :] = rows[:, i * LANES : (i + 1) * LANES]
        rest = rows[:, tiles * LANES :]
        fold = LANES // rest.shape[1]
        piece = bucket // fold
        o_ref[k, tiles * bucket :, :] = jnp.concatenate(
            [rest[i * piece : (i + 1) * piece] for i in range(fold)], axis=1
        )


def place_kernel(targets, text, arrived, o_ref):
    width, rows = text.shape
    groups = arrived.shape[0]
    bucket = arrived.shape[1] * arrived.shape[2] // width
    slots = groups * bucket
    row = lax.broadcasted_iota(jnp.int32, (slots, rows), 1)
    pick = jnp.where(row == targets[...], 1.0, 0.0)
    hit = jnp.sum(pick, axis=0, keepdims=True) > 0.5
    pick = pick.astype(BF16)

    def moved(blocks):
        return lax.dot_general(
            blocks, pick, (((0,), (0,)), ((), ())), preferred_element_type=F32
        ).astype(BF16)

    if arrived.shape[2] == width:
        whole = jnp.concatenate([arrived[k] for k in range(groups)], axis=0)
        o_ref[...] = jnp.where(hit, moved(whole), text[...])
        return
    tiles = width // LANES
    for i in range(tiles):
        part = jnp.concatenate(
            [arrived[k, i * bucket : (i + 1) * bucket, :] for k in range(groups)], axis=0
        )
        at = slice(i * LANES, (i + 1) * LANES)
        o_ref[at, :] = jnp.where(hit, moved(part), text[at, :])
    rest = width % LANES
    parts = []
    for k in range(groups):
        folded = arrived[k, tiles * bucket :, :]
        parts += [folded[:, i * rest : (i + 1) * rest] for i in range(LANES // rest)]
    at = slice(tiles * LANES, width)
    o_ref[at, :] = jnp.where(hit, moved(jnp.concatenate(parts, axis=0)), text[at, :])


def add_kernel(keep, near, o_ref):
    o_ref[...] = (keep[...].astype(F32) + near[...].astype(F32)).astype(BF16)


class Ring:
    def __init__(self, count):
        self.count = count
        order = ring_order(count)
        self.right = [(order[i], order[(i + 1) % count]) for i in range(count)]
        self.left = [(b, a) for a, b in self.right]
        self.done = []
        self.work = []

    def step(self, to_right, to_left):
        t = len(self.done)
        waits = [x for at, x in self.work if at == t - 2]
        if t >= 2:
            before = [self.done[t - 3][1]] if t >= 3 else []
            to_right = after(to_right, self.done[t - 2][0], *before, *waits)
            to_left = after(to_left, *self.done[t - 2])
        pair = (
            lax.ppermute(to_right, "wide", self.right),
            lax.ppermute(to_left, "wide", self.left),
        )
        self.done.append(pair)
        return pair

    def now(self, x):
        if len(self.done) >= 2:
            return after(x, *self.done[-2])
        return x

    def add_work(self, x):
        self.work.append((len(self.done) - 1, x))

    def add_late(self, x, steps):
        self.work.append((len(self.done) - 1 + steps, x))


def per_device(
    patches, norm_gain, norm_bias, w_in, b_in, w_out, b_out, w_proj, b_proj, text, place
):
    groups, parts = lax.axis_size("wide"), lax.axis_size("narrow")
    width, tokens = patches.shape[1], patches.shape[0]
    full = width * parts
    ff = w_in.shape[1]
    windows = tokens // WINDOW
    seq_rows = text.shape[0]
    bucket = seq_rows // groups
    slots = groups * bucket
    shard_rows = [w_in.shape[0], w_out.shape[1], w_proj.shape[2]]
    small = groups == 8 and all(r % 32 == 0 for r in shard_rows)
    chunks = 2

    near_pairs = [(i, i ^ 1) for i in range(parts)]
    far_pairs = [(i, i ^ 2) for i in range(parts)]

    def near(x):
        return lax.ppermute(x, "narrow", near_pairs)

    def far(x):
        return lax.ppermute(x, "narrow", far_pairs)


    def order(x):
        return call(
            order_kernel, (x,), [shape(WINDOW // chunks, width, windows)] * chunks,
            name="order_tokens",
        )

    def shards(count):
        rows = shard_rows[1] // count
        return call(
            shards_kernel, (w_out.T, jnp.transpose(w_proj, (0, 2, 1))),
            [shape(rows, full)] * (2 * count), name="shards",
        )

    def route():
        return call(
            functools.partial(route_kernel, seq_rows, bucket), (place.reshape(groups, windows),),
            [shape(1, windows, dtype=jnp.int32), shape(slots, 1, dtype=jnp.int32)], name="route",
        )

    def norm(blocks):
        count = tokens // chunks
        return call(
            norm_kernel, (*blocks, norm_gain[None], norm_bias[None]), shape(count, full),
            scratch=[pltpu.VMEM((full, count), BF16)], name="norm",
        )

    def hidden(pieces, arrays, normed, first, columns):
        return call(
            functools.partial(hidden_kernel, pieces, groups, shard_rows[0], first, columns),
            (b_in[None], *arrays, *normed), shape(tokens, columns),
            scratch=[pltpu.VMEM((full, columns), BF16)], name="hidden",
        )

    def mlp_out(pieces, arrays, hiddens, over_x):
        outs = call(
            functools.partial(
                out_kernel, pieces, groups, shard_rows[1], over_x, len(hiddens), WINDOW
            ),
            (*hiddens, *arrays), [shape(width, windows)] * (2 * WINDOW),
            scratch=[pltpu.VMEM((2 * width, ff), BF16)], name="mlp_out",
        )
        return outs[:WINDOW], outs[WINDOW:]

    def add(keep, other):
        return call(add_kernel, (keep, other), shape(*keep.shape), name="add")

    def stream(own, keep, core_sums, x_sums):
        return call(
            functools.partial(stream_kernel, chunks),
            (b_out[:, None], *own, *keep, *core_sums, *x_sums),
            shape(WINDOW * width, windows), name="stream",
        )

    def proj(pieces, arrays, merged):
        return call(
            functools.partial(proj_kernel, pieces, groups, shard_rows[2]),
            (merged, *arrays), [shape(2, width, windows)] * 2,
            scratch=[pltpu.VMEM((full, WINDOW * width), BF16)], name="proj",
        )

    def pack(slots_of, keep, core_sums, x_sums):
        block = (bucket, width)
        if compact(width, bucket):
            block = (bucket * width // LANES, LANES)
        return call(
            functools.partial(pack_kernel, groups),
            (slots_of, keep, core_sums, x_sums, b_proj[:, None]), shape(groups, *block),
            name="pack",
        )

    def exchange_and_place(buffer, targets):
        arrived = lax.all_to_all(buffer, "wide", split_axis=0, concat_axis=0, tiled=True)
        return call(
            place_kernel, (targets, text.T, arrived), shape(width, seq_rows), name="place"
        ).T


    if not small:
        shard = [w_in, *shards(1)]
        wholes = [lax.all_gather(s, "wide", axis=0, tiled=True) for s in shard]
        pieces = [Piece(0, k * width, width, None, 0, k) for k in range(parts)]
        own = order(patches.T)
        over_x = [far(x) for x in own]
        normed = [norm((x, y, near(x), near(y))) for x, y in zip(own, over_x)]
        act = hidden(pieces, wholes[:1], normed, 0, ff)
        keep_x, give_x = mlp_out(pieces, wholes[1:2], [act], 1)
        keep, give = mlp_out(pieces, wholes[1:2], [act], 0)
        x_sums = [far(add(k, near(g))) for k, g in zip(keep_x, give_x)]
        merged = stream(own, keep, [near(g) for g in give], x_sums)
        slots_of, targets = route()
        keep, give = proj(pieces, wholes[2:], merged)
        core_sums = near(give)
        x_sums = far(add(keep[1], core_sums[1]))
        return exchange_and_place(pack(slots_of, keep, core_sums, x_sums), targets)


    ring = Ring(groups)
    half_rows = shard_rows[0] // 2
    last = groups // 2

    def gather(halves, work):
        arrays = list(halves)
        pieces = [Piece(h, 0, half_rows, 0, h * half_rows) for h in (0, 1)]
        held = {(way, h): halves[h] for way in (0, 1) for h in (0, 1)}
        t = 0
        for step in range(1, last + 1):
            for first in (0, 1):
                if step == last and first == 1:
                    continue
                pair = ring.step(held[0, first], held[1, 1 - first])
                for way, h in ((0, first), (1, 1 - first)):
                    held[way, h] = pair[way]
                    shift = -step if way == 0 else step
                    pieces.append(Piece(len(arrays), 0, half_rows, shift, h * half_rows))
                    arrays.append(pair[way])
                if t in work:
                    work[t]()
                t += 1
        return pieces, arrays

    own, over_x, over_core, over_both, normed = [], [], [], [], []
    got = {}

    def start_tokens():
        own.extend(order(patches.T))
        over_x.append(far(own[0]))
        ring.add_work(own[0])

    def start_shards():
        got["shards"] = shards(2)
        ring.add_work(got["shards"][0])
        over_core.extend(near(x) for x in own)

    def send_second():
        over_x.append(far(ring.now(own[1])))
        got["slots_of"], got["targets"] = route()

    def send_both():
        over_both.append(near(ring.now(over_x[len(over_both)])))

    def start_norm():
        i = len(normed)
        first = ring.now(own[i])
        normed.append(norm((first, over_x[i], over_core[i], over_both[i])))
        ring.add_work(normed[i])

    def both_and_norm():
        send_both()
        start_norm()

    pieces_in, arrays_in = gather(
        [w_in[:half_rows], w_in[half_rows:]],
        {0: start_tokens, 1: start_shards, 2: send_second, 4: send_both, 5: both_and_norm,
         6: start_norm},
    )

    columns = 256
    hiddens = []

    def start_hidden():
        rows = [ring.now(normed[0]), *normed[1:]]
        hiddens.append(hidden(pieces_in, arrays_in, rows, len(hiddens) * columns, columns))
        ring.add_work(hiddens[-1])

    pieces_out, arrays_out = gather(
        got["shards"][:2], {t: start_hidden for t in range(ff // columns)}
    )

    def start_out(over_x):
        acts = [ring.now(hiddens[0]), *hiddens[1:]]
        keep, give = mlp_out(pieces_out, arrays_out, acts, over_x)
        got["keep", over_x] = keep
        got["core", over_x] = [near(g) for g in give]
        ring.add_work(keep[0])

    def start_sums():
        core = [ring.now(got["core", 1][0]), *got["core", 1][1:]]
        sums = [add(k, c) for k, c in zip(got["keep", 1], core)]
        got["x_sums"] = [far(x) for x in sums]
        for i, x in enumerate(got["x_sums"][:-1]):
            ring.add_late(x, LATE[i])
        ring.add_work(sums[0])
        start_out(0)

    pieces_proj, arrays_proj = gather(
        got["shards"][2:], {0: lambda: start_out(1), 1: start_sums}
    )

    merged = stream(own, got["keep", 0], got["core", 0], got["x_sums"])
    keep, give = proj(pieces_proj, arrays_proj, merged)
    core_sums = near(give)
    x_sums = far(add(keep[1], core_sums[1]))
    return exchange_and_place(pack(got["slots_of"], keep, core_sums, x_sums), got["targets"])


def solution(mesh):
    placed = (
        P("wide", "narrow"),
        P(),
        P(),
        P("wide", "narrow"),
        P("narrow"),
        P("narrow", "wide"),
        P("narrow"),
        P(None, "narrow", "wide"),
        P("narrow"),
        P("wide", "narrow"),
        P(),
    )
    return jax.shard_map(
        per_device, mesh=mesh, in_specs=placed, out_specs=P("wide", "narrow"), check_vma=False
    )
```

```python
import functools

import jax
import jax.numpy as jnp
from jax import lax
from jax.experimental import pallas as pl
from jax.experimental.pallas import tpu as pltpu
from jax.sharding import PartitionSpec as P

F32 = jnp.float32
BF16 = jnp.bfloat16
WINDOW = 4
LATE = (2, 3, 4)
OWN_AT = 3
VMEM = pl.BlockSpec(memory_space=pltpu.VMEM)


def call(kernel, operands, outs, scratch=(), name=None):
    single = not isinstance(outs, (list, tuple))
    return pl.pallas_call(
        kernel,
        out_shape=outs,
        in_specs=[VMEM] * len(operands),
        out_specs=VMEM if single else [VMEM] * len(outs),
        scratch_shapes=list(scratch),
        compiler_params=pltpu.CompilerParams(vmem_limit_bytes=28 * 1024 * 1024),
        cost_estimate=pl.CostEstimate(flops=0, bytes_accessed=0, transcendentals=0),
        name=name,
    )(*operands)


def shape(*dims, dtype=BF16):
    return jax.ShapeDtypeStruct(dims, dtype)


def after(x, *others):
    return lax.optimization_barrier((x, *others))[0]


def ring_order(count):
    return list(range(0, count, 2)) + list(range(count - 1, 0, -2))


def ring_owner(me, shift, count):
    half = me // 2
    at = jnp.where(me % 2 == 0, half, count - 1 - half) + (shift + count)
    at = at % count
    return jnp.where(at < count // 2, 2 * at, 2 * (count - 1 - at) + 1)


class Piece:
    def __init__(self, array, start, rows, shift, base, index=0):
        self.array, self.start, self.rows = array, start, rows
        self.shift, self.base, self.index = shift, base, index

    def row(self, count, shard_rows):
        if self.shift is None:
            return self.index * self.rows
        return ring_owner(lax.axis_index("wide"), self.shift, count) * shard_rows + self.base

    def block_row(self, count, shard_rows, block):
        if self.shift is None:
            of, inside = self.index, 0
        else:
            owner = ring_owner(lax.axis_index("wide"), self.shift, count)
            per_block = block // shard_rows
            of, inside = owner // per_block, (owner % per_block) * shard_rows + self.base
        mine = lax.axis_index("narrow")
        over_x = jnp.where(of // 2 == mine // 2, 0, 1)
        over_core = jnp.where(of % 2 == mine % 2, 0, 1)
        return over_x, over_core, inside


def rows_at(start, rows):
    return pl.ds(pl.multiple_of(start, 16), rows)


def order_kernel(x_ref, *outs):
    tokens = x_ref.shape[1]
    windows = tokens // WINDOW
    source = lax.broadcasted_iota(jnp.int32, (tokens, windows), 0)
    window = lax.broadcasted_iota(jnp.int32, (tokens, windows), 1)
    each = WINDOW // len(outs)
    for p in range(WINDOW):
        pick = jnp.where(source == WINDOW * window + p, 1.0, 0.0).astype(BF16)
        outs[p // each][p % each] = jnp.dot(
            x_ref[...], pick, preferred_element_type=F32
        ).astype(BF16)


def shards_kernel(w_out, w_proj, *outs):
    rows, width = w_proj.shape[1], w_proj.shape[2]
    half = rows // (len(outs) // 2)
    flat = jnp.concatenate([w_proj[p] for p in range(WINDOW)], axis=1)
    for i in range(len(outs) // 2):
        outs[i][...] = w_out[i * half : (i + 1) * half, :]
        outs[len(outs) // 2 + i][...] = flat[i * half : (i + 1) * half, :]


def route_kernel(seq_rows, bucket, place, slots_of, targets):
    groups, windows = place.shape
    me = lax.axis_index("wide")
    table = place[...]
    owner = jnp.where(table >= 0, 0, -1)
    for d in range(1, groups):
        owner = owner + jnp.where(table >= d * seq_rows, 1, 0)
    earlier = jnp.where(
        lax.broadcasted_iota(jnp.int32, (windows, windows), 0)
        <= lax.broadcasted_iota(jnp.int32, (windows, windows), 1),
        1.0,
        0.0,
    ).astype(BF16)
    here = jnp.where(owner == me, 1.0, 0.0)
    rank = jnp.dot(here.astype(BF16), earlier, preferred_element_type=F32)
    rank = jnp.where(owner == me, rank, 0.0).astype(jnp.int32)
    local = table - me * seq_rows
    slot = lax.broadcasted_iota(jnp.int32, (bucket, windows), 0) + 1
    source_at = lax.broadcasted_iota(jnp.int32, (groups, windows), 0)
    for k in range(groups):
        wanted = source_at == k
        of_rank = jnp.sum(jnp.where(wanted, rank, 0), axis=0, keepdims=True)
        of_local = jnp.sum(jnp.where(wanted, local, 0), axis=0, keepdims=True)
        found = jnp.where(of_rank == slot, of_local + 1, 0)
        targets[k * bucket : (k + 1) * bucket, :] = jnp.sum(found, axis=1, keepdims=True) - 1
    mine = jnp.sum(jnp.where(source_at == me, owner, 0), axis=0, keepdims=True)
    hits = source_at == mine
    rank = jnp.dot(
        jnp.where(hits, 1.0, 0.0).astype(BF16), earlier, preferred_element_type=F32
    )
    rank = jnp.sum(jnp.where(hits, rank, 0.0), axis=0, keepdims=True).astype(jnp.int32)
    slots_of[...] = jnp.where(mine >= 0, mine * bucket + rank - 1, groups * bucket)


def norm_kernel(own, over_x, over_core, over_both, gain, bias, o_ref, whole):
    parts = (own, over_x, over_core, over_both)
    each, rows, windows = own.shape
    tokens = each * windows
    mine = lax.axis_index("narrow")
    for part, flip in zip(parts, (0, 2, 1, 3)):
        at = (mine ^ flip) * rows
        for j in range(each):
            whole[rows_at(at, rows), j * windows : (j + 1) * windows] = part[j]
    width = whole.shape[0]
    step = 128
    for t in range(0, tokens, step):
        values = whole[:, t : t + step].astype(F32)
        center = jnp.sum(values, axis=0, keepdims=True) * (1.0 / width)
        values = values - center
        spread = jnp.sum(values * values, axis=0, keepdims=True) * (1.0 / width)
        values = (values * lax.rsqrt(spread + 1e-06)).T
        o_ref[t : t + step, :] = (values * gain[...] + bias[...]).astype(BF16)


def hidden_kernel(pieces, count, shard_rows, first, columns, bias, *refs):
    arrays = 1 + max(p.array for p in pieces)
    sources, normed, (o_ref, part) = refs[:arrays], refs[arrays:-2], refs[-2:]
    for p in pieces:
        part[rows_at(p.row(count, shard_rows), p.rows), :] = sources[p.array][
            p.start : p.start + p.rows, first : first + columns
        ]
    at = 0
    for rows in normed:
        v = jnp.dot(rows[...], part[...], preferred_element_type=F32)
        v = v + bias[:, first : first + columns]
        o_ref[at : at + rows.shape[0], :] = (
            0.5 * v * (1.0 + lax.erf(v * (2.0**-0.5)))
        ).astype(BF16)
        at += rows.shape[0]


def out_kernel(pieces, count, shard_rows, over_x, hidden_count, chunks, *refs):
    hidden, refs = refs[:hidden_count], refs[hidden_count:]
    outs, part = refs[-1 - 2 * chunks : -1], refs[-1]
    keep, give = outs[:chunks], outs[chunks:]
    sources = refs[: -1 - 2 * chunks]
    block, tokens = keep[0].shape
    for p in pieces:
        x, core, inside = p.block_row(count, shard_rows, block)

        @pl.when(x == over_x)
        def _():
            part[rows_at(core * block + inside, p.rows), :] = sources[p.array][
                p.start : p.start + p.rows, :
            ]

    columns = hidden[0].shape[1]
    step = 256
    for t in range(0, tokens * chunks, step):
        total = None
        for i, h in enumerate(hidden):
            v = lax.dot_general(
                part[:, i * columns : (i + 1) * columns],
                h[t : t + step, :],
                (((1,), (1,)), ((), ())),
                preferred_element_type=F32,
            )
            total = v if total is None else total + v
        total = total.astype(BF16)
        c, at = t // tokens, t % tokens
        keep[c][:, at : at + step] = total[:block]
        give[c][:, at : at + step] = total[block:]


def proj_kernel(pieces, missing, count, shard_rows, merged, *refs):
    sources, outs, part = refs[:-5], refs[-5:-1], refs[-1]
    block = outs[0].shape[0]

    def at(piece):
        x, core, inside = piece.block_row(count, shard_rows, block)
        return rows_at((core * 2 + x) * block + inside, piece.rows)

    for p in pieces:
        part[at(p), :] = sources[p.array][p.start : p.start + p.rows, :]
    if missing is not None:
        part[at(missing), :] = jnp.zeros((missing.rows, part.shape[1]), BF16)
    for half in (1, 0):
        v = jnp.dot(
            part[half * 2 * block : (half + 1) * 2 * block, :],
            merged[...],
            preferred_element_type=F32,
        ).astype(BF16)
        outs[2 * half][...] = v[:block]
        outs[2 * half + 1][...] = v[block:]


def last_kernel(first, second, merged, o_ref):
    whole = jnp.concatenate([first[...], second[...]], axis=0)
    o_ref[...] = jnp.dot(whole, merged[...], preferred_element_type=F32).astype(BF16)


def stream_kernel(chunks, bias, *refs):
    o_ref = refs[-1]
    own = refs[:chunks]
    keep, near, far = (
        refs[chunks + i * WINDOW : chunks + (i + 1) * WINDOW] for i in range(3)
    )
    each, rows, windows = own[0].shape
    for p in range(WINDOW):
        total = keep[p][...].astype(F32) + near[p][...].astype(F32) + far[p][...].astype(F32)
        v = own[p // each][p % each].astype(F32) + (total + bias[...])
        o_ref[p * rows : (p + 1) * rows, :] = v.astype(BF16)


LANES = 128


def compact(width, bucket):
    rest = width % LANES
    return rest > 0 and LANES % rest == 0 and bucket % (16 * (LANES // rest)) == 0


def pack_kernel(missing, count, shard_rows, groups, terms, slots_of, bias, *refs):
    total, o_ref = refs[-1], refs[-2]
    total[...] = refs[0][...].astype(F32)
    for r in refs[1:terms]:
        total[...] = total[...] + r[...].astype(F32)
    late = refs[terms:-2]
    if late:
        x, core, inside = missing.block_row(count, shard_rows, total.shape[0])

        @pl.when(x + core == 0)
        def _():
            at = rows_at(inside, missing.rows)
            added = late[0][...].astype(F32)
            for r in late[1:]:
                added = added + r[...].astype(F32)
            total[at, :] = total[at, :] + added

    vision = (total[...] + bias[...]).astype(BF16)
    width = vision.shape[0]
    bucket = o_ref.shape[1] * o_ref.shape[2] // width
    slot = lax.broadcasted_iota(jnp.int32, (groups * bucket, vision.shape[1]), 0)
    pick = jnp.where(slot == slots_of[...], 1.0, 0.0).astype(BF16)
    moved = lax.dot_general(
        pick, vision, (((1,), (1,)), ((), ())), preferred_element_type=F32
    ).astype(BF16)
    for k in range(groups):
        rows = moved[k * bucket : (k + 1) * bucket]
        if o_ref.shape[2] == width:
            o_ref[k] = rows
            continue
        tiles = width // LANES
        for i in range(tiles):
            o_ref[k, i * bucket : (i + 1) * bucket, :] = rows[:, i * LANES : (i + 1) * LANES]
        rest = rows[:, tiles * LANES :]
        fold = LANES // rest.shape[1]
        piece = bucket // fold
        o_ref[k, tiles * bucket :, :] = jnp.concatenate(
            [rest[i * piece : (i + 1) * piece] for i in range(fold)], axis=1
        )


def place_kernel(targets, text, arrived, o_ref):
    width, rows = text.shape
    groups = arrived.shape[0]
    bucket = arrived.shape[1] * arrived.shape[2] // width
    slots = groups * bucket
    row = lax.broadcasted_iota(jnp.int32, (slots, rows), 1)
    pick = jnp.where(row == targets[...], 1.0, 0.0)
    hit = jnp.sum(pick, axis=0, keepdims=True) > 0.5
    pick = pick.astype(BF16)

    def moved(blocks):
        return lax.dot_general(
            blocks, pick, (((0,), (0,)), ((), ())), preferred_element_type=F32
        ).astype(BF16)

    if arrived.shape[2] == width:
        whole = jnp.concatenate([arrived[k] for k in range(groups)], axis=0)
        o_ref[...] = jnp.where(hit, moved(whole), text[...])
        return
    tiles = width // LANES
    for i in range(tiles):
        part = jnp.concatenate(
            [arrived[k, i * bucket : (i + 1) * bucket, :] for k in range(groups)], axis=0
        )
        at = slice(i * LANES, (i + 1) * LANES)
        o_ref[at, :] = jnp.where(hit, moved(part), text[at, :])
    rest = width % LANES
    parts = []
    for k in range(groups):
        folded = arrived[k, tiles * bucket :, :]
        parts += [folded[:, i * rest : (i + 1) * rest] for i in range(LANES // rest)]
    at = slice(tiles * LANES, width)
    o_ref[at, :] = jnp.where(hit, moved(jnp.concatenate(parts, axis=0)), text[at, :])


def add_kernel(keep, near, o_ref):
    o_ref[...] = (keep[...].astype(F32) + near[...].astype(F32)).astype(BF16)


class Ring:
    def __init__(self, count):
        self.count = count
        order = ring_order(count)
        self.right = [(order[i], order[(i + 1) % count]) for i in range(count)]
        self.left = [(b, a) for a, b in self.right]
        self.done = []
        self.work = []

    def step(self, to_right, to_left):
        t = len(self.done)
        waits = [x for at, x in self.work if at == t - 2]
        if t >= 2:
            before = [self.done[t - 3][1]] if t >= 3 else []
            to_right = after(to_right, self.done[t - 2][0], *before, *waits)
            to_left = after(to_left, *self.done[t - 2])
        pair = (
            lax.ppermute(to_right, "wide", self.right),
            lax.ppermute(to_left, "wide", self.left),
        )
        self.done.append(pair)
        return pair

    def now(self, x):
        if len(self.done) >= 2:
            return after(x, *self.done[-2])
        return x

    def add_work(self, x):
        self.work.append((len(self.done) - 1, x))

    def add_late(self, x, steps):
        self.work.append((len(self.done) - 1 + steps, x))


def per_device(
    patches, norm_gain, norm_bias, w_in, b_in, w_out, b_out, w_proj, b_proj, text, place
):
    groups, parts = lax.axis_size("wide"), lax.axis_size("narrow")
    width, tokens = patches.shape[1], patches.shape[0]
    full = width * parts
    ff = w_in.shape[1]
    windows = tokens // WINDOW
    seq_rows = text.shape[0]
    bucket = seq_rows // groups
    slots = groups * bucket
    shard_rows = [w_in.shape[0], w_out.shape[1], w_proj.shape[2]]
    small = groups == 8 and all(r % 32 == 0 for r in shard_rows)
    chunks = 2

    near_pairs = [(i, i ^ 1) for i in range(parts)]
    far_pairs = [(i, i ^ 2) for i in range(parts)]

    def near(x):
        return lax.ppermute(x, "narrow", near_pairs)

    def far(x):
        return lax.ppermute(x, "narrow", far_pairs)

    def both(x):
        return lax.ppermute(x, "narrow", [(i, i ^ 3) for i in range(parts)])


    def order(x):
        return call(
            order_kernel, (x,), [shape(WINDOW // chunks, width, windows)] * chunks,
            name="order_tokens",
        )

    def shards(count):
        rows = shard_rows[1] // count
        return call(
            shards_kernel, (w_out.T, jnp.transpose(w_proj, (0, 2, 1))),
            [shape(rows, full)] * (2 * count), name="shards",
        )

    def route():
        return call(
            functools.partial(route_kernel, seq_rows, bucket), (place.reshape(groups, windows),),
            [shape(1, windows, dtype=jnp.int32), shape(slots, 1, dtype=jnp.int32)], name="route",
        )

    def norm(blocks):
        count = tokens // chunks
        return call(
            norm_kernel, (*blocks, norm_gain[None], norm_bias[None]), shape(count, full),
            scratch=[pltpu.VMEM((full, count), BF16)], name="norm",
        )

    def hidden(pieces, arrays, normed, first, columns):
        return call(
            functools.partial(hidden_kernel, pieces, groups, shard_rows[0], first, columns),
            (b_in[None], *arrays, *normed), shape(tokens, columns),
            scratch=[pltpu.VMEM((full, columns), BF16)], name="hidden",
        )

    def mlp_out(pieces, arrays, hiddens, over_x):
        outs = call(
            functools.partial(
                out_kernel, pieces, groups, shard_rows[1], over_x, len(hiddens), WINDOW
            ),
            (*hiddens, *arrays), [shape(width, windows)] * (2 * WINDOW),
            scratch=[pltpu.VMEM((2 * width, ff), BF16)], name="mlp_out",
        )
        return outs[:WINDOW], outs[WINDOW:]

    def add(keep, other):
        return call(add_kernel, (keep, other), shape(*keep.shape), name="add")

    def stream(own, keep, core_sums, x_sums):
        return call(
            functools.partial(stream_kernel, chunks),
            (b_out[:, None], *own, *keep, *core_sums, *x_sums),
            shape(WINDOW * width, windows), name="stream",
        )

    def proj(pieces, missing, arrays, merged):
        return call(
            functools.partial(proj_kernel, pieces, missing, groups, shard_rows[2]),
            (merged, *arrays), [shape(width, windows)] * parts,
            scratch=[pltpu.VMEM((full, WINDOW * width), BF16)], name="proj",
        )

    def pack(slots_of, missing, terms, late):
        block = (bucket, width)
        if compact(width, bucket):
            block = (bucket * width // LANES, LANES)
        return call(
            functools.partial(pack_kernel, missing, groups, shard_rows[2], groups, len(terms)),
            (slots_of, b_proj[:, None], *terms, *late), shape(groups, *block),
            scratch=[pltpu.VMEM((width, windows), F32)], name="pack",
        )

    def exchange_and_place(buffer, targets):
        arrived = lax.all_to_all(buffer, "wide", split_axis=0, concat_axis=0, tiled=True)
        return call(
            place_kernel, (targets, text.T, arrived), shape(width, seq_rows), name="place"
        ).T


    if not small:
        shard = [w_in, *shards(1)]
        wholes = [lax.all_gather(s, "wide", axis=0, tiled=True) for s in shard]
        pieces = [Piece(0, k * width, width, None, 0, k) for k in range(parts)]
        own = order(patches.T)
        over_x = [far(x) for x in own]
        normed = [norm((x, y, near(x), near(y))) for x, y in zip(own, over_x)]
        act = hidden(pieces, wholes[:1], normed, 0, ff)
        keep_x, give_x = mlp_out(pieces, wholes[1:2], [act], 1)
        keep, give = mlp_out(pieces, wholes[1:2], [act], 0)
        x_sums = [far(add(k, near(g))) for k, g in zip(keep_x, give_x)]
        merged = stream(own, keep, [near(g) for g in give], x_sums)
        slots_of, targets = route()
        mine, give_x, give_core, give_both = proj(pieces, None, wholes[2:], merged)
        terms = [mine, far(give_x), near(give_core), both(give_both)]
        return exchange_and_place(pack(slots_of, None, terms, ()), targets)


    ring = Ring(groups)
    half_rows = shard_rows[0] // 2
    last = groups // 2

    def gather(halves, work):
        arrays = list(halves)
        pieces = [Piece(h, 0, half_rows, 0, h * half_rows) for h in (0, 1)]
        held = {(way, h): halves[h] for way in (0, 1) for h in (0, 1)}
        t = 0
        for step in range(1, last + 1):
            for first in (0, 1):
                if step == last and first == 1:
                    continue
                pair = ring.step(held[0, first], held[1, 1 - first])
                for way, h in ((0, first), (1, 1 - first)):
                    held[way, h] = pair[way]
                    shift = -step if way == 0 else step
                    pieces.append(Piece(len(arrays), 0, half_rows, shift, h * half_rows))
                    arrays.append(pair[way])
                if t in work:
                    work[t]()
                t += 1
        return pieces, arrays

    own, over_x, over_core, over_both, normed = [], [], [], [], []
    got = {}

    def start_tokens():
        own.extend(order(patches.T))
        over_x.append(far(own[0]))
        ring.add_work(own[0])

    def start_shards():
        got["shards"] = shards(2)
        ring.add_work(got["shards"][0])
        over_core.extend(near(x) for x in own)

    def send_second():
        over_x.append(far(ring.now(own[1])))
        got["slots_of"], got["targets"] = route()

    def send_both():
        over_both.append(near(ring.now(over_x[len(over_both)])))

    def start_norm():
        i = len(normed)
        first = ring.now(own[i])
        normed.append(norm((first, over_x[i], over_core[i], over_both[i])))
        ring.add_work(normed[i])

    def both_and_norm():
        send_both()
        start_norm()

    pieces_in, arrays_in = gather(
        [w_in[:half_rows], w_in[half_rows:]],
        {0: start_tokens, 1: start_shards, 2: send_second, 4: send_both, 5: both_and_norm,
         6: start_norm},
    )

    columns = 256
    hiddens = []

    def start_hidden():
        rows = [ring.now(normed[0]), *normed[1:]]
        hiddens.append(hidden(pieces_in, arrays_in, rows, len(hiddens) * columns, columns))
        ring.add_work(hiddens[-1])

    pieces_out, arrays_out = gather(
        got["shards"][:2], {t: start_hidden for t in range(ff // columns)}
    )

    def start_out(over_x):
        acts = [ring.now(hiddens[0]), *hiddens[1:]]
        keep, give = mlp_out(pieces_out, arrays_out, acts, over_x)
        got["keep", over_x] = keep
        got["core", over_x] = [near(g) for g in give]
        ring.add_work(keep[0])

    def start_sums():
        core = [ring.now(got["core", 1][0]), *got["core", 1][1:]]
        sums = [add(k, c) for k, c in zip(got["keep", 1], core)]
        got["x_sums"] = [far(x) for x in sums]
        for i, x in zip(range(len(LATE)), got["x_sums"]):
            ring.add_late(x, LATE[i])
        ring.add_work(sums[0])

    pieces_proj, arrays_proj = gather(
        got["shards"][2:], {0: lambda: start_out(1), 1: start_sums, OWN_AT: lambda: start_out(0)}
    )

    merged = stream(own, got["keep", 0], got["core", 0], got["x_sums"])
    missing = Piece(0, 0, shard_rows[2], last, 0)
    mine, give_x, give_core, give_both = proj(pieces_proj[:-2], missing, arrays_proj[:-2], merged)
    terms = [mine, far(give_x), near(give_core), both(give_both)]

    halves = sorted(pieces_proj[-2:], key=lambda p: p.base)
    late = call(
        last_kernel, (*[arrays_proj[p.array] for p in halves], merged),
        shape(shard_rows[2], windows), name="proj_last",
    )
    late = add(late, near(late))
    return exchange_and_place(
        pack(got["slots_of"], missing, terms, [late, far(late)]), got["targets"]
    )


def solution(mesh):
    placed = (
        P("wide", "narrow"),
        P(),
        P(),
        P("wide", "narrow"),
        P("narrow"),
        P("narrow", "wide"),
        P("narrow"),
        P(None, "narrow", "wide"),
        P("narrow"),
        P("wide", "narrow"),
        P(),
    )
    return jax.shard_map(
        per_device, mesh=mesh, in_specs=placed, out_specs=P("wide", "narrow"), check_vma=False
    )
```

```python
import functools

import jax
import jax.numpy as jnp
from jax import lax
from jax.experimental import pallas as pl
from jax.experimental.pallas import tpu as pltpu
from jax.sharding import PartitionSpec as P

F32 = jnp.float32
BF16 = jnp.bfloat16
WINDOW = 4
NORM_AT = 5
HIDDEN_AT = 0
SUMS = 2
ADD_LATE = (1, 1)
LATE = ()
OWN_AT = 2
VMEM = pl.BlockSpec(memory_space=pltpu.VMEM)


def call(kernel, operands, outs, scratch=(), name=None):
    single = not isinstance(outs, (list, tuple))
    return pl.pallas_call(
        kernel,
        out_shape=outs,
        in_specs=[VMEM] * len(operands),
        out_specs=VMEM if single else [VMEM] * len(outs),
        scratch_shapes=list(scratch),
        compiler_params=pltpu.CompilerParams(vmem_limit_bytes=28 * 1024 * 1024),
        cost_estimate=pl.CostEstimate(flops=0, bytes_accessed=0, transcendentals=0),
        name=name,
    )(*operands)


def shape(*dims, dtype=BF16):
    return jax.ShapeDtypeStruct(dims, dtype)


def after(x, *others):
    return lax.optimization_barrier((x, *others))[0]


def ring_order(count):
    return list(range(0, count, 2)) + list(range(count - 1, 0, -2))


def ring_owner(me, shift, count):
    half = me // 2
    at = jnp.where(me % 2 == 0, half, count - 1 - half) + (shift + count)
    at = at % count
    return jnp.where(at < count // 2, 2 * at, 2 * (count - 1 - at) + 1)


class Piece:
    def __init__(self, array, start, rows, shift, base, index=0):
        self.array, self.start, self.rows = array, start, rows
        self.shift, self.base, self.index = shift, base, index

    def row(self, count, shard_rows):
        if self.shift is None:
            return self.index * self.rows
        return ring_owner(lax.axis_index("wide"), self.shift, count) * shard_rows + self.base

    def block(self, count, shard_rows, block):
        if self.shift is None:
            return self.index, 0
        owner = ring_owner(lax.axis_index("wide"), self.shift, count)
        per_block = block // shard_rows
        return owner // per_block, (owner % per_block) * shard_rows + self.base

    def block_row(self, count, shard_rows, block):
        of, inside = self.block(count, shard_rows, block)
        mine = lax.axis_index("narrow")
        over_x = jnp.where(of // 2 == mine // 2, 0, 1)
        over_core = jnp.where(of % 2 == mine % 2, 0, 1)
        return over_x, over_core, inside


def rows_at(start, rows):
    return pl.ds(pl.multiple_of(start, 16), rows)


def order_kernel(x_ref, o_ref):
    tokens = x_ref.shape[1]
    windows = tokens // WINDOW
    source = lax.broadcasted_iota(jnp.int32, (tokens, windows), 0)
    window = lax.broadcasted_iota(jnp.int32, (tokens, windows), 1)
    for p in range(WINDOW):
        pick = jnp.where(source == WINDOW * window + p, 1.0, 0.0).astype(BF16)
        o_ref[p] = jnp.dot(x_ref[...], pick, preferred_element_type=F32).astype(BF16)


def shards_kernel(w_out, w_proj, *outs):
    rows, width = w_proj.shape[1], w_proj.shape[2]
    half = rows // (len(outs) // 2)
    flat = jnp.concatenate([w_proj[p] for p in range(WINDOW)], axis=1)
    for i in range(len(outs) // 2):
        outs[i][...] = w_out[i * half : (i + 1) * half, :]
        outs[len(outs) // 2 + i][...] = flat[i * half : (i + 1) * half, :]


def route_kernel(seq_rows, bucket, place, slots_of, targets):
    groups, windows = place.shape
    me = lax.axis_index("wide")
    table = place[...]
    owner = jnp.where(table >= 0, 0, -1)
    for d in range(1, groups):
        owner = owner + jnp.where(table >= d * seq_rows, 1, 0)
    earlier = jnp.where(
        lax.broadcasted_iota(jnp.int32, (windows, windows), 0)
        <= lax.broadcasted_iota(jnp.int32, (windows, windows), 1),
        1.0,
        0.0,
    ).astype(BF16)
    here = jnp.where(owner == me, 1.0, 0.0)
    rank = jnp.dot(here.astype(BF16), earlier, preferred_element_type=F32)
    rank = jnp.where(owner == me, rank, 0.0).astype(jnp.int32)
    local = table - me * seq_rows
    slot = lax.broadcasted_iota(jnp.int32, (bucket, windows), 0) + 1
    source_at = lax.broadcasted_iota(jnp.int32, (groups, windows), 0)
    for k in range(groups):
        wanted = source_at == k
        of_rank = jnp.sum(jnp.where(wanted, rank, 0), axis=0, keepdims=True)
        of_local = jnp.sum(jnp.where(wanted, local, 0), axis=0, keepdims=True)
        found = jnp.where(of_rank == slot, of_local + 1, 0)
        targets[k * bucket : (k + 1) * bucket, :] = jnp.sum(found, axis=1, keepdims=True) - 1
    mine = jnp.sum(jnp.where(source_at == me, owner, 0), axis=0, keepdims=True)
    hits = source_at == mine
    rank = jnp.dot(
        jnp.where(hits, 1.0, 0.0).astype(BF16), earlier, preferred_element_type=F32
    )
    rank = jnp.sum(jnp.where(hits, rank, 0.0), axis=0, keepdims=True).astype(jnp.int32)
    slots_of[...] = jnp.where(mine >= 0, mine * bucket + rank - 1, groups * bucket)


def norm_kernel(first, each, blocks, gain, bias, o_ref, whole):
    rows, windows = blocks.shape[3:]
    for core in range(blocks.shape[0]):
        for x in range(blocks.shape[1]):
            at = (2 * x + core) * rows
            for j in range(each):
                whole[at : at + rows, j * windows : (j + 1) * windows] = blocks[core, x, first + j]
    width, tokens = whole.shape
    step = 128
    for t in range(0, tokens, step):
        values = whole[:, t : t + step].astype(F32)
        center = jnp.sum(values, axis=0, keepdims=True) * (1.0 / width)
        values = values - center
        spread = jnp.sum(values * values, axis=0, keepdims=True) * (1.0 / width)
        values = (values * lax.rsqrt(spread + 1e-06)).T
        o_ref[t : t + step, :] = (values * gain[...] + bias[...]).astype(BF16)


def hidden_kernel(pieces, count, shard_rows, first, columns, bias, *refs):
    arrays = 1 + max(p.array for p in pieces)
    sources, normed, (o_ref, part) = refs[:arrays], refs[arrays:-2], refs[-2:]
    for p in pieces:
        part[rows_at(p.row(count, shard_rows), p.rows), :] = sources[p.array][
            p.start : p.start + p.rows, first : first + columns
        ]
    at = 0
    for rows in normed:
        v = jnp.dot(rows[...], part[...], preferred_element_type=F32)
        v = v + bias[:, first : first + columns]
        o_ref[at : at + rows.shape[0], :] = (
            0.5 * v * (1.0 + lax.erf(v * (2.0**-0.5)))
        ).astype(BF16)
        at += rows.shape[0]


def out_kernel(pieces, count, shard_rows, over_x, hidden_count, chunks, *refs):
    hidden, refs = refs[:hidden_count], refs[hidden_count:]
    outs, part = refs[-1 - 2 * chunks : -1], refs[-1]
    keep, give = outs[:chunks], outs[chunks:]
    sources = refs[: -1 - 2 * chunks]
    block, tokens = keep[0].shape
    for p in pieces:
        x, core, inside = p.block_row(count, shard_rows, block)

        @pl.when(x == over_x)
        def _():
            part[rows_at(core * block + inside, p.rows), :] = sources[p.array][
                p.start : p.start + p.rows, :
            ]

    columns = hidden[0].shape[1]
    step = 256
    for t in range(0, tokens * chunks, step):
        total = None
        for i, h in enumerate(hidden):
            v = lax.dot_general(
                part[:, i * columns : (i + 1) * columns],
                h[t : t + step, :],
                (((1,), (1,)), ((), ())),
                preferred_element_type=F32,
            )
            total = v if total is None else total + v
        total = total.astype(BF16)
        c, at = t // tokens, t % tokens
        keep[c][:, at : at + step] = total[:block]
        give[c][:, at : at + step] = total[block:]


def proj_kernel(pieces, count, shard_rows, merged, *refs):
    sources, (keep, give, part) = refs[:-3], refs[-3:]
    block = keep.shape[1]
    for p in pieces:
        x, core, inside = p.block_row(count, shard_rows, block)
        at = rows_at(core * 2 * block + x * block + inside, p.rows)
        part[at, :] = sources[p.array][p.start : p.start + p.rows, :]
    for core, target in ((1, give), (0, keep)):
        v = jnp.dot(
            part[core * 2 * block : (core + 1) * 2 * block, :],
            merged[...],
            preferred_element_type=F32,
        ).astype(BF16)
        target[0] = v[:block]
        target[1] = v[block:]


def stream_kernel(own, bias, *refs):
    parts, o_ref = refs[:-1], refs[-1]
    count = len(parts) // 3
    rows, windows = own.shape[1:]
    each = WINDOW // count
    for p in range(WINDOW):
        at = slice(p % each * windows, (p % each + 1) * windows)
        terms = [parts[i * count + p // each][:, at].astype(F32) for i in range(3)]
        total = terms[0] + terms[1] + terms[2] + bias[...]
        o_ref[p * rows : (p + 1) * rows, :] = (own[p].astype(F32) + total).astype(BF16)


LANES = 128


def compact(width, bucket):
    rest = width % LANES
    return rest > 0 and LANES % rest == 0 and bucket % (16 * (LANES // rest)) == 0


def pack_kernel(groups, slots_of, keep, near, far, bias, o_ref):
    total = keep[0].astype(F32) + near[0].astype(F32) + far[...].astype(F32)
    vision = (total + bias[...]).astype(BF16)
    width = vision.shape[0]
    bucket = o_ref.shape[1] * o_ref.shape[2] // width
    slot = lax.broadcasted_iota(jnp.int32, (groups * bucket, vision.shape[1]), 0)
    pick = jnp.where(slot == slots_of[...], 1.0, 0.0).astype(BF16)
    moved = lax.dot_general(
        pick, vision, (((1,), (1,)), ((), ())), preferred_element_type=F32
    ).astype(BF16)
    for k in range(groups):
        rows = moved[k * bucket : (k + 1) * bucket]
        if o_ref.shape[2] == width:
            o_ref[k] = rows
            continue
        tiles = width // LANES
        for i in range(tiles):
            o_ref[k, i * bucket : (i + 1) * bucket, :] = rows[:, i * LANES : (i + 1) * LANES]
        rest = rows[:, tiles * LANES :]
        fold = LANES // rest.shape[1]
        piece = bucket // fold
        o_ref[k, tiles * bucket :, :] = jnp.concatenate(
            [rest[i * piece : (i + 1) * piece] for i in range(fold)], axis=1
        )


def place_kernel(targets, text, arrived, o_ref):
    width, rows = text.shape
    groups = arrived.shape[0]
    bucket = arrived.shape[1] * arrived.shape[2] // width
    slots = groups * bucket
    row = lax.broadcasted_iota(jnp.int32, (slots, rows), 1)
    pick = jnp.where(row == targets[...], 1.0, 0.0)
    hit = jnp.sum(pick, axis=0, keepdims=True) > 0.5
    pick = pick.astype(BF16)

    def moved(blocks):
        return lax.dot_general(
            blocks, pick, (((0,), (0,)), ((), ())), preferred_element_type=F32
        ).astype(BF16)

    if arrived.shape[2] == width:
        whole = jnp.concatenate([arrived[k] for k in range(groups)], axis=0)
        o_ref[...] = jnp.where(hit, moved(whole), text[...])
        return
    tiles = width // LANES
    for i in range(tiles):
        part = jnp.concatenate(
            [arrived[k, i * bucket : (i + 1) * bucket, :] for k in range(groups)], axis=0
        )
        at = slice(i * LANES, (i + 1) * LANES)
        o_ref[at, :] = jnp.where(hit, moved(part), text[at, :])
    rest = width % LANES
    parts = []
    for k in range(groups):
        folded = arrived[k, tiles * bucket :, :]
        parts += [folded[:, i * rest : (i + 1) * rest] for i in range(LANES // rest)]
    at = slice(tiles * LANES, width)
    o_ref[at, :] = jnp.where(hit, moved(jnp.concatenate(parts, axis=0)), text[at, :])


def add_kernel(keep, near, o_ref):
    o_ref[...] = (keep[...].astype(F32) + near[...].astype(F32)).astype(BF16)


class Ring:
    def __init__(self, count):
        self.count = count
        order = ring_order(count)
        self.right = [(order[i], order[(i + 1) % count]) for i in range(count)]
        self.left = [(b, a) for a, b in self.right]
        self.done = []
        self.work = []

    def step(self, to_right, to_left):
        t = len(self.done)
        waits = [x for at, x in self.work if at == t - 2]
        if t >= 2:
            before = [self.done[t - 3][1]] if t >= 3 else []
            to_right = after(to_right, self.done[t - 2][0], *before, *waits)
            to_left = after(to_left, *self.done[t - 2])
        pair = (
            lax.ppermute(to_right, "wide", self.right),
            lax.ppermute(to_left, "wide", self.left),
        )
        self.done.append(pair)
        return pair

    def now(self, x):
        if len(self.done) >= 2:
            return after(x, *self.done[-2])
        return x

    def add_work(self, x):
        self.work.append((len(self.done) - 1, x))

    def add_late(self, x, steps):
        self.work.append((len(self.done) - 1 + steps, x))


def per_device(
    patches, norm_gain, norm_bias, w_in, b_in, w_out, b_out, w_proj, b_proj, text, place
):
    groups, parts = lax.axis_size("wide"), lax.axis_size("narrow")
    width, tokens = patches.shape[1], patches.shape[0]
    full = width * parts
    ff = w_in.shape[1]
    windows = tokens // WINDOW
    seq_rows = text.shape[0]
    bucket = seq_rows // groups
    slots = groups * bucket
    shard_rows = [w_in.shape[0], w_out.shape[1], w_proj.shape[2]]
    small = groups == 8 and all(r % 32 == 0 for r in shard_rows)
    halves = 2
    x_groups = [[i, i + 2] for i in range(parts // 2)]
    core_groups = [[i, i + 1] for i in range(0, parts, 2)]

    near_pairs = [(i, i ^ 1) for i in range(parts)]
    far_pairs = [(i, i ^ 2) for i in range(parts)]

    def near(x):
        return lax.ppermute(x, "narrow", near_pairs)

    def far(x):
        return lax.ppermute(x, "narrow", far_pairs)


    def order(x):
        return call(
            order_kernel, (x,), shape(WINDOW, width, windows), name="order_tokens",
        )

    def shards(count):
        rows = shard_rows[1] // count
        return call(
            shards_kernel, (w_out.T, jnp.transpose(w_proj, (0, 2, 1))),
            [shape(rows, full)] * (2 * count), name="shards",
        )

    def route():
        return call(
            functools.partial(route_kernel, seq_rows, bucket), (place.reshape(groups, windows),),
            [shape(1, windows, dtype=jnp.int32), shape(slots, 1, dtype=jnp.int32)], name="route",
        )

    def gather(x):
        x = lax.all_gather(x, "narrow", axis_index_groups=x_groups)
        return lax.all_gather(x, "narrow", axis_index_groups=core_groups)

    def norm(blocks, half):
        each = WINDOW // halves
        count = each * windows
        return call(
            functools.partial(norm_kernel, half * each, each),
            (blocks, norm_gain[None], norm_bias[None]), shape(count, full),
            scratch=[pltpu.VMEM((full, count), BF16)], name="norm",
        )

    def hidden(pieces, arrays, normed, first, columns):
        return call(
            functools.partial(hidden_kernel, pieces, groups, shard_rows[0], first, columns),
            (b_in[None], *arrays, *normed), shape(tokens, columns),
            scratch=[pltpu.VMEM((full, columns), BF16)], name="hidden",
        )

    def mlp_out(pieces, arrays, hiddens, over_x):
        outs = call(
            functools.partial(
                out_kernel, pieces, groups, shard_rows[1], over_x, len(hiddens), SUMS
            ),
            (*hiddens, *arrays), [shape(width, tokens // SUMS)] * (2 * SUMS),
            scratch=[pltpu.VMEM((2 * width, ff), BF16)], name="mlp_out",
        )
        return outs[:SUMS], outs[SUMS:]

    def add(keep, other):
        return call(add_kernel, (keep, other), shape(*keep.shape), name="add")

    def stream(own, sums):
        return call(
            stream_kernel, (own, b_out[:, None], *sums), shape(WINDOW * width, windows),
            name="stream",
        )

    def proj(pieces, arrays, merged):
        return call(
            functools.partial(proj_kernel, pieces, groups, shard_rows[2]),
            (merged, *arrays), [shape(2, width, windows)] * 2,
            scratch=[pltpu.VMEM((full, WINDOW * width), BF16)], name="proj",
        )

    def pack(slots_of, keep, core_sums, x_sums):
        block = (bucket, width)
        if compact(width, bucket):
            block = (bucket * width // LANES, LANES)
        return call(
            functools.partial(pack_kernel, groups),
            (slots_of, keep, core_sums, x_sums, b_proj[:, None]), shape(groups, *block),
            name="pack",
        )

    def exchange_and_place(buffer, targets):
        arrived = lax.all_to_all(buffer, "wide", split_axis=0, concat_axis=0, tiled=True)
        return call(
            place_kernel, (targets, text.T, arrived), shape(width, seq_rows), name="place"
        ).T


    if not small:
        shard = [w_in, *shards(1)]
        wholes = [lax.all_gather(s, "wide", axis=0, tiled=True) for s in shard]
        pieces = [Piece(0, k * width, width, None, 0, k) for k in range(parts)]
        own = order(patches.T)
        blocks = gather(own)
        normed = [norm(blocks, i) for i in range(halves)]
        act = hidden(pieces, wholes[:1], normed, 0, ff)
        keep_x, give_x = mlp_out(pieces, wholes[1:2], [act], 1)
        keep, give = mlp_out(pieces, wholes[1:2], [act], 0)
        x_sums = [far(add(k, near(g))) for k, g in zip(keep_x, give_x)]
        merged = stream(own, [*keep, *[near(g) for g in give], *x_sums])
        slots_of, targets = route()
        keep, give = proj(pieces, wholes[2:], merged)
        core_sums = near(give)
        x_sums = far(add(keep[1], core_sums[1]))
        return exchange_and_place(pack(slots_of, keep, core_sums, x_sums), targets)


    ring = Ring(groups)
    half_rows = shard_rows[0] // 2
    last = groups // 2

    def hops(halves, work):
        arrays = list(halves)
        pieces = [Piece(h, 0, half_rows, 0, h * half_rows) for h in (0, 1)]
        held = {(way, h): halves[h] for way in (0, 1) for h in (0, 1)}
        t = 0
        for step in range(1, last + 1):
            for first in (0, 1):
                if step == last and first == 1:
                    continue
                pair = ring.step(held[0, first], held[1, 1 - first])
                for way, h in ((0, first), (1, 1 - first)):
                    held[way, h] = pair[way]
                    shift = -step if way == 0 else step
                    pieces.append(Piece(len(arrays), 0, half_rows, shift, h * half_rows))
                    arrays.append(pair[way])
                if t in work:
                    work[t]()
                t += 1
        return pieces, arrays

    got, normed = {}, []

    def start_tokens():
        got["own"] = order(patches.T)
        got["blocks"] = gather(got["own"])
        ring.add_work(got["own"])

    def start_shards():
        got["shards"] = shards(2)
        ring.add_work(got["shards"][0])

    def start_route():
        got["slots_of"], got["targets"] = route()

    def start_norm():
        normed.append(norm(ring.now(got["blocks"]), len(normed)))
        ring.add_work(normed[-1])

    pieces_in, arrays_in = hops(
        [w_in[:half_rows], w_in[half_rows:]],
        {0: start_tokens, 1: start_shards, 2: start_route, NORM_AT: start_norm,
         NORM_AT + 1: start_norm},
    )

    columns = 256
    hiddens = []

    def start_hidden():
        rows = [ring.now(normed[0]), *normed[1:]]
        hiddens.append(hidden(pieces_in, arrays_in, rows, len(hiddens) * columns, columns))
        ring.add_work(hiddens[-1])

    pieces_out, arrays_out = hops(
        got["shards"][:2], {t + HIDDEN_AT: start_hidden for t in range(ff // columns)}
    )

    def start_out(over_x):
        acts = [ring.now(hiddens[0]), *hiddens[1:]]
        keep, give = mlp_out(pieces_out, arrays_out, acts, over_x)
        got["keep", over_x] = keep
        got["core", over_x] = [near(g) for g in give]
        ring.add_work(keep[0])

    def start_sums():
        sums = [add(k, c) for k, c in zip(got["keep", 1], got["core", 1])]
        got["x_sums"] = [far(x) for x in sums]
        for steps, x in zip(ADD_LATE, sums):
            ring.add_late(x, steps)
        for steps, x in zip(LATE, got["x_sums"]):
            ring.add_late(x, steps)

    def start_first():
        start_out(1)
        start_sums()

    pieces_proj, arrays_proj = hops(
        got["shards"][2:], {0: start_first, OWN_AT: lambda: start_out(0)}
    )

    merged = stream(
        got["own"], [*got["keep", 0], *got["core", 0], *got["x_sums"]]
    )
    keep, give = proj(pieces_proj, arrays_proj, merged)
    core_sums = near(give)
    x_sums = far(add(keep[1], core_sums[1]))
    return exchange_and_place(pack(got["slots_of"], keep, core_sums, x_sums), got["targets"])


def solution(mesh):
    placed = (
        P("wide", "narrow"),
        P(),
        P(),
        P("wide", "narrow"),
        P("narrow"),
        P("narrow", "wide"),
        P("narrow"),
        P(None, "narrow", "wide"),
        P("narrow"),
        P("wide", "narrow"),
        P(),
    )
    return jax.shard_map(
        per_device, mesh=mesh, in_specs=placed, out_specs=P("wide", "narrow"), check_vma=False
    )
```

```python
import functools

import jax
import jax.numpy as jnp
from jax import lax
from jax.experimental import pallas as pl
from jax.experimental.pallas import tpu as pltpu
from jax.sharding import PartitionSpec as P

F32 = jnp.float32
BF16 = jnp.bfloat16
WINDOW = 4
NORM_AT = 0
HIDDEN_AT = 2
SUMS = 2
ADD_LATE = ()
LATE = ()
OWN_AT = 2
VMEM = pl.BlockSpec(memory_space=pltpu.VMEM)


def call(kernel, operands, outs, scratch=(), name=None):
    single = not isinstance(outs, (list, tuple))
    return pl.pallas_call(
        kernel,
        out_shape=outs,
        in_specs=[VMEM] * len(operands),
        out_specs=VMEM if single else [VMEM] * len(outs),
        scratch_shapes=list(scratch),
        compiler_params=pltpu.CompilerParams(vmem_limit_bytes=28 * 1024 * 1024),
        cost_estimate=pl.CostEstimate(flops=0, bytes_accessed=0, transcendentals=0),
        name=name,
    )(*operands)


def shape(*dims, dtype=BF16):
    return jax.ShapeDtypeStruct(dims, dtype)


def after(x, *others):
    return lax.optimization_barrier((x, *others))[0]


def ring_order(count):
    return list(range(0, count, 2)) + list(range(count - 1, 0, -2))


def ring_owner(me, shift, count):
    half = me // 2
    at = jnp.where(me % 2 == 0, half, count - 1 - half) + (shift + count)
    at = at % count
    return jnp.where(at < count // 2, 2 * at, 2 * (count - 1 - at) + 1)


class Piece:
    def __init__(self, array, start, rows, shift, base, index=0):
        self.array, self.start, self.rows = array, start, rows
        self.shift, self.base, self.index = shift, base, index

    def row(self, count, shard_rows):
        if self.shift is None:
            return self.index * self.rows
        return ring_owner(lax.axis_index("wide"), self.shift, count) * shard_rows + self.base

    def block(self, count, shard_rows, block):
        if self.shift is None:
            return self.index, 0
        owner = ring_owner(lax.axis_index("wide"), self.shift, count)
        per_block = block // shard_rows
        return owner // per_block, (owner % per_block) * shard_rows + self.base

    def block_row(self, count, shard_rows, block):
        of, inside = self.block(count, shard_rows, block)
        mine = lax.axis_index("narrow")
        over_x = jnp.where(of // 2 == mine // 2, 0, 1)
        over_core = jnp.where(of % 2 == mine % 2, 0, 1)
        return over_x, over_core, inside


def rows_at(start, rows):
    return pl.ds(pl.multiple_of(start, 16), rows)


def order_kernel(x_ref, o_ref):
    tokens = x_ref.shape[1]
    windows = tokens // WINDOW
    source = lax.broadcasted_iota(jnp.int32, (tokens, windows), 0)
    window = lax.broadcasted_iota(jnp.int32, (tokens, windows), 1)
    for p in range(WINDOW):
        pick = jnp.where(source == WINDOW * window + p, 1.0, 0.0).astype(BF16)
        o_ref[p] = jnp.dot(x_ref[...], pick, preferred_element_type=F32).astype(BF16)


def shards_kernel(w_out, w_proj, *outs):
    rows, width = w_proj.shape[1], w_proj.shape[2]
    half = rows // (len(outs) // 2)
    flat = jnp.concatenate([w_proj[p] for p in range(WINDOW)], axis=1)
    for i in range(len(outs) // 2):
        outs[i][...] = w_out[i * half : (i + 1) * half, :]
        outs[len(outs) // 2 + i][...] = flat[i * half : (i + 1) * half, :]


def route_kernel(seq_rows, bucket, place, slots_of, targets):
    groups, windows = place.shape
    me = lax.axis_index("wide")
    table = place[...]
    owner = jnp.where(table >= 0, 0, -1)
    for d in range(1, groups):
        owner = owner + jnp.where(table >= d * seq_rows, 1, 0)
    earlier = jnp.where(
        lax.broadcasted_iota(jnp.int32, (windows, windows), 0)
        <= lax.broadcasted_iota(jnp.int32, (windows, windows), 1),
        1.0,
        0.0,
    ).astype(BF16)
    here = jnp.where(owner == me, 1.0, 0.0)
    rank = jnp.dot(here.astype(BF16), earlier, preferred_element_type=F32)
    rank = jnp.where(owner == me, rank, 0.0).astype(jnp.int32)
    local = table - me * seq_rows
    slot = lax.broadcasted_iota(jnp.int32, (bucket, windows), 0) + 1
    source_at = lax.broadcasted_iota(jnp.int32, (groups, windows), 0)
    for k in range(groups):
        wanted = source_at == k
        of_rank = jnp.sum(jnp.where(wanted, rank, 0), axis=0, keepdims=True)
        of_local = jnp.sum(jnp.where(wanted, local, 0), axis=0, keepdims=True)
        found = jnp.where(of_rank == slot, of_local + 1, 0)
        targets[k * bucket : (k + 1) * bucket, :] = jnp.sum(found, axis=1, keepdims=True) - 1
    mine = jnp.sum(jnp.where(source_at == me, owner, 0), axis=0, keepdims=True)
    hits = source_at == mine
    rank = jnp.dot(
        jnp.where(hits, 1.0, 0.0).astype(BF16), earlier, preferred_element_type=F32
    )
    rank = jnp.sum(jnp.where(hits, rank, 0.0), axis=0, keepdims=True).astype(jnp.int32)
    slots_of[...] = jnp.where(mine >= 0, mine * bucket + rank - 1, groups * bucket)


def norm_kernel(first, each, blocks, gain, bias, o_ref, whole):
    rows, windows = blocks.shape[2:]
    for k in range(blocks.shape[0]):
        for j in range(each):
            whole[k * rows : (k + 1) * rows, j * windows : (j + 1) * windows] = blocks[k, first + j]
    width, tokens = whole.shape
    step = 128
    for t in range(0, tokens, step):
        values = whole[:, t : t + step].astype(F32)
        center = jnp.sum(values, axis=0, keepdims=True) * (1.0 / width)
        values = values - center
        spread = jnp.sum(values * values, axis=0, keepdims=True) * (1.0 / width)
        values = (values * lax.rsqrt(spread + 1e-06)).T
        o_ref[t : t + step, :] = (values * gain[...] + bias[...]).astype(BF16)


def hidden_kernel(pieces, count, shard_rows, first, columns, bias, *refs):
    arrays = 1 + max(p.array for p in pieces)
    sources, normed, (o_ref, part) = refs[:arrays], refs[arrays:-2], refs[-2:]
    for p in pieces:
        part[rows_at(p.row(count, shard_rows), p.rows), :] = sources[p.array][
            p.start : p.start + p.rows, first : first + columns
        ]
    at = 0
    for rows in normed:
        v = jnp.dot(rows[...], part[...], preferred_element_type=F32)
        v = v + bias[:, first : first + columns]
        o_ref[at : at + rows.shape[0], :] = (
            0.5 * v * (1.0 + lax.erf(v * (2.0**-0.5)))
        ).astype(BF16)
        at += rows.shape[0]


def out_kernel(pieces, count, shard_rows, over_x, hidden_count, chunks, *refs):
    hidden, refs = refs[:hidden_count], refs[hidden_count:]
    outs, part = refs[-1 - 2 * chunks : -1], refs[-1]
    keep, give = outs[:chunks], outs[chunks:]
    sources = refs[: -1 - 2 * chunks]
    block, tokens = keep[0].shape
    for p in pieces:
        x, core, inside = p.block_row(count, shard_rows, block)

        @pl.when(x == over_x)
        def _():
            part[rows_at(core * block + inside, p.rows), :] = sources[p.array][
                p.start : p.start + p.rows, :
            ]

    columns = hidden[0].shape[1]
    step = 256
    for t in range(0, tokens * chunks, step):
        total = None
        for i, h in enumerate(hidden):
            v = lax.dot_general(
                part[:, i * columns : (i + 1) * columns],
                h[t : t + step, :],
                (((1,), (1,)), ((), ())),
                preferred_element_type=F32,
            )
            total = v if total is None else total + v
        total = total.astype(BF16)
        c, at = t // tokens, t % tokens
        keep[c][:, at : at + step] = total[:block]
        give[c][:, at : at + step] = total[block:]


def proj_kernel(pieces, count, shard_rows, merged, *refs):
    sources, (keep, give, part) = refs[:-3], refs[-3:]
    block = keep.shape[1]
    for p in pieces:
        x, core, inside = p.block_row(count, shard_rows, block)
        at = rows_at(core * 2 * block + x * block + inside, p.rows)
        part[at, :] = sources[p.array][p.start : p.start + p.rows, :]
    for core, target in ((1, give), (0, keep)):
        v = jnp.dot(
            part[core * 2 * block : (core + 1) * 2 * block, :],
            merged[...],
            preferred_element_type=F32,
        ).astype(BF16)
        target[0] = v[:block]
        target[1] = v[block:]


def stream_kernel(own, bias, *refs):
    parts, o_ref = refs[:-1], refs[-1]
    count = len(parts) // 3
    rows, windows = own.shape[1:]
    each = WINDOW // count
    for p in range(WINDOW):
        at = slice(p % each * windows, (p % each + 1) * windows)
        terms = [parts[i * count + p // each][:, at].astype(F32) for i in range(3)]
        total = terms[0] + terms[1] + terms[2] + bias[...]
        o_ref[p * rows : (p + 1) * rows, :] = (own[p].astype(F32) + total).astype(BF16)


LANES = 128


def compact(width, bucket):
    rest = width % LANES
    return rest > 0 and LANES % rest == 0 and bucket % (16 * (LANES // rest)) == 0


def pack_kernel(groups, slots_of, keep, near, far, bias, o_ref):
    total = keep[0].astype(F32) + near[0].astype(F32) + far[...].astype(F32)
    vision = (total + bias[...]).astype(BF16)
    width = vision.shape[0]
    bucket = o_ref.shape[1] * o_ref.shape[2] // width
    slot = lax.broadcasted_iota(jnp.int32, (groups * bucket, vision.shape[1]), 0)
    pick = jnp.where(slot == slots_of[...], 1.0, 0.0).astype(BF16)
    moved = lax.dot_general(
        pick, vision, (((1,), (1,)), ((), ())), preferred_element_type=F32
    ).astype(BF16)
    for k in range(groups):
        rows = moved[k * bucket : (k + 1) * bucket]
        if o_ref.shape[2] == width:
            o_ref[k] = rows
            continue
        tiles = width // LANES
        for i in range(tiles):
            o_ref[k, i * bucket : (i + 1) * bucket, :] = rows[:, i * LANES : (i + 1) * LANES]
        rest = rows[:, tiles * LANES :]
        fold = LANES // rest.shape[1]
        piece = bucket // fold
        o_ref[k, tiles * bucket :, :] = jnp.concatenate(
            [rest[i * piece : (i + 1) * piece] for i in range(fold)], axis=1
        )


def place_kernel(targets, text, arrived, o_ref):
    width, rows = text.shape
    groups = arrived.shape[0]
    bucket = arrived.shape[1] * arrived.shape[2] // width
    slots = groups * bucket
    row = lax.broadcasted_iota(jnp.int32, (slots, rows), 1)
    pick = jnp.where(row == targets[...], 1.0, 0.0)
    hit = jnp.sum(pick, axis=0, keepdims=True) > 0.5
    pick = pick.astype(BF16)

    def moved(blocks):
        return lax.dot_general(
            blocks, pick, (((0,), (0,)), ((), ())), preferred_element_type=F32
        ).astype(BF16)

    if arrived.shape[2] == width:
        whole = jnp.concatenate([arrived[k] for k in range(groups)], axis=0)
        o_ref[...] = jnp.where(hit, moved(whole), text[...])
        return
    tiles = width // LANES
    for i in range(tiles):
        part = jnp.concatenate(
            [arrived[k, i * bucket : (i + 1) * bucket, :] for k in range(groups)], axis=0
        )
        at = slice(i * LANES, (i + 1) * LANES)
        o_ref[at, :] = jnp.where(hit, moved(part), text[at, :])
    rest = width % LANES
    parts = []
    for k in range(groups):
        folded = arrived[k, tiles * bucket :, :]
        parts += [folded[:, i * rest : (i + 1) * rest] for i in range(LANES // rest)]
    at = slice(tiles * LANES, width)
    o_ref[at, :] = jnp.where(hit, moved(jnp.concatenate(parts, axis=0)), text[at, :])


def add_kernel(keep, near, o_ref):
    o_ref[...] = (keep[...].astype(F32) + near[...].astype(F32)).astype(BF16)


class Ring:
    def __init__(self, count):
        self.count = count
        order = ring_order(count)
        self.right = [(order[i], order[(i + 1) % count]) for i in range(count)]
        self.left = [(b, a) for a, b in self.right]
        self.done = []
        self.work = []

    def step(self, to_right, to_left):
        t = len(self.done)
        waits = [x for at, x in self.work if at == t - 2]
        if t >= 2:
            before = [self.done[t - 3][1]] if t >= 3 else []
            to_right = after(to_right, self.done[t - 2][0], *before, *waits)
            to_left = after(to_left, *self.done[t - 2])
        pair = (
            lax.ppermute(to_right, "wide", self.right),
            lax.ppermute(to_left, "wide", self.left),
        )
        self.done.append(pair)
        return pair

    def now(self, x):
        if len(self.done) >= 2:
            return after(x, *self.done[-2])
        return x

    def add_work(self, x):
        self.work.append((len(self.done) - 1, x))

    def add_late(self, x, steps):
        self.work.append((len(self.done) - 1 + steps, x))


def per_device(
    patches, norm_gain, norm_bias, w_in, b_in, w_out, b_out, w_proj, b_proj, text, place
):
    groups, parts = lax.axis_size("wide"), lax.axis_size("narrow")
    width, tokens = patches.shape[1], patches.shape[0]
    full = width * parts
    ff = w_in.shape[1]
    windows = tokens // WINDOW
    seq_rows = text.shape[0]
    bucket = seq_rows // groups
    slots = groups * bucket
    shard_rows = [w_in.shape[0], w_out.shape[1], w_proj.shape[2]]
    small = groups == 8 and all(r % 32 == 0 for r in shard_rows)
    halves = 2

    near_pairs = [(i, i ^ 1) for i in range(parts)]
    far_pairs = [(i, i ^ 2) for i in range(parts)]

    def near(x):
        return lax.ppermute(x, "narrow", near_pairs)

    def far(x):
        return lax.ppermute(x, "narrow", far_pairs)


    def order(x):
        return call(
            order_kernel, (x,), shape(WINDOW, width, windows), name="order_tokens",
        )

    def shards(count):
        rows = shard_rows[1] // count
        return call(
            shards_kernel, (w_out.T, jnp.transpose(w_proj, (0, 2, 1))),
            [shape(rows, full)] * (2 * count), name="shards",
        )

    def route():
        return call(
            functools.partial(route_kernel, seq_rows, bucket), (place.reshape(groups, windows),),
            [shape(1, windows, dtype=jnp.int32), shape(slots, 1, dtype=jnp.int32)], name="route",
        )

    def norm(blocks, half):
        each = WINDOW // halves
        count = each * windows
        return call(
            functools.partial(norm_kernel, half * each, each),
            (blocks, norm_gain[None], norm_bias[None]), shape(count, full),
            scratch=[pltpu.VMEM((full, count), BF16)], name="norm",
        )

    def hidden(pieces, arrays, normed, first, columns):
        return call(
            functools.partial(hidden_kernel, pieces, groups, shard_rows[0], first, columns),
            (b_in[None], *arrays, *normed), shape(tokens, columns),
            scratch=[pltpu.VMEM((full, columns), BF16)], name="hidden",
        )

    def mlp_out(pieces, arrays, hiddens, over_x):
        outs = call(
            functools.partial(
                out_kernel, pieces, groups, shard_rows[1], over_x, len(hiddens), SUMS
            ),
            (*hiddens, *arrays), [shape(width, tokens // SUMS)] * (2 * SUMS),
            scratch=[pltpu.VMEM((2 * width, ff), BF16)], name="mlp_out",
        )
        return outs[:SUMS], outs[SUMS:]

    def add(keep, other):
        return call(add_kernel, (keep, other), shape(*keep.shape), name="add")

    def stream(own, sums):
        return call(
            stream_kernel, (own, b_out[:, None], *sums), shape(WINDOW * width, windows),
            name="stream",
        )

    def proj(pieces, arrays, merged):
        return call(
            functools.partial(proj_kernel, pieces, groups, shard_rows[2]),
            (merged, *arrays), [shape(2, width, windows)] * 2,
            scratch=[pltpu.VMEM((full, WINDOW * width), BF16)], name="proj",
        )

    def pack(slots_of, keep, core_sums, x_sums):
        block = (bucket, width)
        if compact(width, bucket):
            block = (bucket * width // LANES, LANES)
        return call(
            functools.partial(pack_kernel, groups),
            (slots_of, keep, core_sums, x_sums, b_proj[:, None]), shape(groups, *block),
            name="pack",
        )

    def exchange_and_place(buffer, targets):
        arrived = lax.all_to_all(buffer, "wide", split_axis=0, concat_axis=0, tiled=True)
        return call(
            place_kernel, (targets, text.T, arrived), shape(width, seq_rows), name="place"
        ).T


    if not small:
        shard = [w_in, *shards(1)]
        wholes = [lax.all_gather(s, "wide", axis=0, tiled=True) for s in shard]
        pieces = [Piece(0, k * width, width, None, 0, k) for k in range(parts)]
        own = order(patches.T)
        blocks = lax.all_gather(own, "narrow")
        normed = [norm(blocks, i) for i in range(halves)]
        act = hidden(pieces, wholes[:1], normed, 0, ff)
        keep_x, give_x = mlp_out(pieces, wholes[1:2], [act], 1)
        keep, give = mlp_out(pieces, wholes[1:2], [act], 0)
        x_sums = [far(add(k, near(g))) for k, g in zip(keep_x, give_x)]
        merged = stream(own, [*keep, *[near(g) for g in give], *x_sums])
        slots_of, targets = route()
        keep, give = proj(pieces, wholes[2:], merged)
        core_sums = near(give)
        x_sums = far(add(keep[1], core_sums[1]))
        return exchange_and_place(pack(slots_of, keep, core_sums, x_sums), targets)


    ring = Ring(groups)
    half_rows = shard_rows[0] // 2
    last = groups // 2

    def hops(halves, work):
        arrays = list(halves)
        pieces = [Piece(h, 0, half_rows, 0, h * half_rows) for h in (0, 1)]
        held = {(way, h): halves[h] for way in (0, 1) for h in (0, 1)}
        t = 0
        for step in range(1, last + 1):
            for first in (0, 1):
                if step == last and first == 1:
                    continue
                pair = ring.step(held[0, first], held[1, 1 - first])
                for way, h in ((0, first), (1, 1 - first)):
                    held[way, h] = pair[way]
                    shift = -step if way == 0 else step
                    pieces.append(Piece(len(arrays), 0, half_rows, shift, h * half_rows))
                    arrays.append(pair[way])
                if t in work:
                    work[t]()
                t += 1
        return pieces, arrays

    got, normed = {}, []

    def start_tokens():
        got["own"] = order(patches.T)
        got["blocks"] = lax.all_gather(got["own"], "narrow")
        ring.add_work(got["own"])

    def start_shards():
        got["shards"] = shards(2)
        ring.add_work(got["shards"][0])

    def start_route():
        got["slots_of"], got["targets"] = route()

    def start_norm():
        normed.append(norm(ring.now(got["blocks"]), len(normed)))
        ring.add_work(normed[-1])

    pieces_in, arrays_in = hops(
        [w_in[:half_rows], w_in[half_rows:]],
        {0: start_tokens, 1: start_shards, 2: start_route},
    )

    hiddens = []
    second = {NORM_AT: start_norm, NORM_AT + 1: start_norm}

    def start_hidden():
        rows = [ring.now(normed[0]), *normed[1:]]
        hiddens.append(hidden(pieces_in, arrays_in, rows, len(hiddens) * columns, columns))
        ring.add_work(hiddens[-1])

    columns = 256
    for t in range(ff // columns):
        second[HIDDEN_AT + t] = start_hidden
    pieces_out, arrays_out = hops(got["shards"][:2], second)

    def start_out(over_x):
        acts = [ring.now(hiddens[0]), *hiddens[1:]]
        if over_x == 0:
            acts[0] = after(acts[0], *got["sums"])
        keep, give = mlp_out(pieces_out, arrays_out, acts, over_x)
        got["keep", over_x] = keep
        got["core", over_x] = [near(g) for g in give]
        ring.add_work(keep[0])

    def start_sums():
        sums = [add(k, c) for k, c in zip(got["keep", 1], got["core", 1])]
        got["x_sums"] = [far(x) for x in sums]
        got["sums"] = sums
        for steps, x in zip(ADD_LATE, sums):
            ring.add_late(x, steps)
        for steps, x in zip(LATE, got["x_sums"]):
            ring.add_late(x, steps)

    def start_first():
        start_out(1)
        start_sums()

    pieces_proj, arrays_proj = hops(
        got["shards"][2:], {0: start_first, OWN_AT: lambda: start_out(0)}
    )

    merged = stream(
        got["own"], [*got["keep", 0], *got["core", 0], *got["x_sums"]]
    )
    keep, give = proj(pieces_proj, arrays_proj, merged)
    core_sums = near(give)
    x_sums = far(add(keep[1], core_sums[1]))
    return exchange_and_place(pack(got["slots_of"], keep, core_sums, x_sums), got["targets"])


def solution(mesh):
    placed = (
        P("wide", "narrow"),
        P(),
        P(),
        P("wide", "narrow"),
        P("narrow"),
        P("narrow", "wide"),
        P("narrow"),
        P(None, "narrow", "wide"),
        P("narrow"),
        P("wide", "narrow"),
        P(),
    )
    return jax.shard_map(
        per_device, mesh=mesh, in_specs=placed, out_specs=P("wide", "narrow"), check_vma=False
    )
```

```python
import functools

import jax
import jax.numpy as jnp
from jax import lax
from jax.experimental import pallas as pl
from jax.experimental.pallas import tpu as pltpu
from jax.sharding import PartitionSpec as P

F32 = jnp.float32
BF16 = jnp.bfloat16
WINDOW = 4
NORM_AT = 0
HIDDEN_AT = 2
SUMS = 2
ADD_LATE = ()
LATE = ()
OWN_AT = 2
VMEM = pl.BlockSpec(memory_space=pltpu.VMEM)


def call(kernel, operands, outs, scratch=(), name=None):
    single = not isinstance(outs, (list, tuple))
    return pl.pallas_call(
        kernel,
        out_shape=outs,
        in_specs=[VMEM] * len(operands),
        out_specs=VMEM if single else [VMEM] * len(outs),
        scratch_shapes=list(scratch),
        compiler_params=pltpu.CompilerParams(vmem_limit_bytes=28 * 1024 * 1024),
        cost_estimate=pl.CostEstimate(flops=0, bytes_accessed=0, transcendentals=0),
        name=name,
    )(*operands)


def shape(*dims, dtype=BF16):
    return jax.ShapeDtypeStruct(dims, dtype)


def after(x, *others):
    return lax.optimization_barrier((x, *others))[0]


def ring_order(count):
    return list(range(0, count, 2)) + list(range(count - 1, 0, -2))


def ring_owner(me, shift, count):
    half = me // 2
    at = jnp.where(me % 2 == 0, half, count - 1 - half) + (shift + count)
    at = at % count
    return jnp.where(at < count // 2, 2 * at, 2 * (count - 1 - at) + 1)


class Piece:
    def __init__(self, array, start, rows, shift, base, index=0):
        self.array, self.start, self.rows = array, start, rows
        self.shift, self.base, self.index = shift, base, index

    def row(self, count, shard_rows):
        if self.shift is None:
            return self.index * self.rows
        return ring_owner(lax.axis_index("wide"), self.shift, count) * shard_rows + self.base

    def block(self, count, shard_rows, block):
        if self.shift is None:
            return self.index, 0
        owner = ring_owner(lax.axis_index("wide"), self.shift, count)
        per_block = block // shard_rows
        return owner // per_block, (owner % per_block) * shard_rows + self.base

    def block_row(self, count, shard_rows, block):
        of, inside = self.block(count, shard_rows, block)
        mine = lax.axis_index("narrow")
        over_x = jnp.where(of // 2 == mine // 2, 0, 1)
        over_core = jnp.where(of % 2 == mine % 2, 0, 1)
        return over_x, over_core, inside


def rows_at(start, rows):
    return pl.ds(pl.multiple_of(start, 16), rows)


def order_kernel(x_ref, *outs):
    tokens = x_ref.shape[1]
    windows = tokens // WINDOW
    source = lax.broadcasted_iota(jnp.int32, (tokens, windows), 0)
    window = lax.broadcasted_iota(jnp.int32, (tokens, windows), 1)
    each = WINDOW // len(outs)
    for p in range(WINDOW):
        pick = jnp.where(source == WINDOW * window + p, 1.0, 0.0).astype(BF16)
        outs[p // each][p % each] = jnp.dot(
            x_ref[...], pick, preferred_element_type=F32
        ).astype(BF16)


def shards_kernel(w_out, w_proj, *outs):
    rows, width = w_proj.shape[1], w_proj.shape[2]
    half = rows // (len(outs) // 2)
    flat = jnp.concatenate([w_proj[p] for p in range(WINDOW)], axis=1)
    for i in range(len(outs) // 2):
        outs[i][...] = w_out[i * half : (i + 1) * half, :]
        outs[len(outs) // 2 + i][...] = flat[i * half : (i + 1) * half, :]


def route_kernel(seq_rows, bucket, place, slots_of, targets):
    groups, windows = place.shape
    me = lax.axis_index("wide")
    table = place[...]
    owner = jnp.where(table >= 0, 0, -1)
    for d in range(1, groups):
        owner = owner + jnp.where(table >= d * seq_rows, 1, 0)
    earlier = jnp.where(
        lax.broadcasted_iota(jnp.int32, (windows, windows), 0)
        <= lax.broadcasted_iota(jnp.int32, (windows, windows), 1),
        1.0,
        0.0,
    ).astype(BF16)
    here = jnp.where(owner == me, 1.0, 0.0)
    rank = jnp.dot(here.astype(BF16), earlier, preferred_element_type=F32)
    rank = jnp.where(owner == me, rank, 0.0).astype(jnp.int32)
    local = table - me * seq_rows
    slot = lax.broadcasted_iota(jnp.int32, (bucket, windows), 0) + 1
    source_at = lax.broadcasted_iota(jnp.int32, (groups, windows), 0)
    for k in range(groups):
        wanted = source_at == k
        of_rank = jnp.sum(jnp.where(wanted, rank, 0), axis=0, keepdims=True)
        of_local = jnp.sum(jnp.where(wanted, local, 0), axis=0, keepdims=True)
        found = jnp.where(of_rank == slot, of_local + 1, 0)
        targets[k * bucket : (k + 1) * bucket, :] = jnp.sum(found, axis=1, keepdims=True) - 1
    mine = jnp.sum(jnp.where(source_at == me, owner, 0), axis=0, keepdims=True)
    hits = source_at == mine
    rank = jnp.dot(
        jnp.where(hits, 1.0, 0.0).astype(BF16), earlier, preferred_element_type=F32
    )
    rank = jnp.sum(jnp.where(hits, rank, 0.0), axis=0, keepdims=True).astype(jnp.int32)
    slots_of[...] = jnp.where(mine >= 0, mine * bucket + rank - 1, groups * bucket)


def norm_kernel(own, over_x, over_core, over_both, gain, bias, o_ref, whole):
    each, rows, windows = own.shape
    mine = lax.axis_index("narrow")
    for part, flip in zip((own, over_x, over_core, over_both), (0, 2, 1, 3)):
        at = rows_at((mine ^ flip) * rows, rows)
        for j in range(each):
            whole[at, j * windows : (j + 1) * windows] = part[j]
    width, tokens = whole.shape
    step = 128
    for t in range(0, tokens, step):
        values = whole[:, t : t + step].astype(F32)
        center = jnp.sum(values, axis=0, keepdims=True) * (1.0 / width)
        values = values - center
        spread = jnp.sum(values * values, axis=0, keepdims=True) * (1.0 / width)
        values = (values * lax.rsqrt(spread + 1e-06)).T
        o_ref[t : t + step, :] = (values * gain[...] + bias[...]).astype(BF16)


def hidden_kernel(pieces, count, shard_rows, first, columns, bias, *refs):
    arrays = 1 + max(p.array for p in pieces)
    sources, normed, (o_ref, part) = refs[:arrays], refs[arrays:-2], refs[-2:]
    for p in pieces:
        part[rows_at(p.row(count, shard_rows), p.rows), :] = sources[p.array][
            p.start : p.start + p.rows, first : first + columns
        ]
    at = 0
    for rows in normed:
        v = jnp.dot(rows[...], part[...], preferred_element_type=F32)
        v = v + bias[:, first : first + columns]
        o_ref[at : at + rows.shape[0], :] = (
            0.5 * v * (1.0 + lax.erf(v * (2.0**-0.5)))
        ).astype(BF16)
        at += rows.shape[0]


def out_kernel(pieces, count, shard_rows, over_x, hidden_count, chunks, *refs):
    hidden, refs = refs[:hidden_count], refs[hidden_count:]
    outs, part = refs[-1 - 2 * chunks : -1], refs[-1]
    keep, give = outs[:chunks], outs[chunks:]
    sources = refs[: -1 - 2 * chunks]
    block, tokens = keep[0].shape
    for p in pieces:
        x, core, inside = p.block_row(count, shard_rows, block)

        @pl.when(x == over_x)
        def _():
            part[rows_at(core * block + inside, p.rows), :] = sources[p.array][
                p.start : p.start + p.rows, :
            ]

    columns = hidden[0].shape[1]
    step = 256
    for t in range(0, tokens * chunks, step):
        total = None
        for i, h in enumerate(hidden):
            v = lax.dot_general(
                part[:, i * columns : (i + 1) * columns],
                h[t : t + step, :],
                (((1,), (1,)), ((), ())),
                preferred_element_type=F32,
            )
            total = v if total is None else total + v
        total = total.astype(BF16)
        c, at = t // tokens, t % tokens
        keep[c][:, at : at + step] = total[:block]
        give[c][:, at : at + step] = total[block:]


def proj_kernel(pieces, count, shard_rows, merged, *refs):
    sources, (keep, give, part) = refs[:-3], refs[-3:]
    block = keep.shape[1]
    for p in pieces:
        x, core, inside = p.block_row(count, shard_rows, block)
        at = rows_at(core * 2 * block + x * block + inside, p.rows)
        part[at, :] = sources[p.array][p.start : p.start + p.rows, :]
    for core, target in ((1, give), (0, keep)):
        v = jnp.dot(
            part[core * 2 * block : (core + 1) * 2 * block, :],
            merged[...],
            preferred_element_type=F32,
        ).astype(BF16)
        target[0] = v[:block]
        target[1] = v[block:]


def stream_kernel(own_count, bias, *refs):
    own, parts, o_ref = refs[:own_count], refs[own_count:-1], refs[-1]
    count = len(parts) // 3
    rows, windows = own[0].shape[1:]
    each, own_each = WINDOW // count, WINDOW // own_count
    for p in range(WINDOW):
        at = slice(p % each * windows, (p % each + 1) * windows)
        terms = [parts[i * count + p // each][:, at].astype(F32) for i in range(3)]
        total = terms[0] + terms[1] + terms[2] + bias[...]
        v = own[p // own_each][p % own_each].astype(F32) + total
        o_ref[p * rows : (p + 1) * rows, :] = v.astype(BF16)


LANES = 128


def compact(width, bucket):
    rest = width % LANES
    return rest > 0 and LANES % rest == 0 and bucket % (16 * (LANES // rest)) == 0


def pack_kernel(groups, slots_of, keep, near, far, bias, o_ref):
    total = keep[0].astype(F32) + near[0].astype(F32) + far[...].astype(F32)
    vision = (total + bias[...]).astype(BF16)
    width = vision.shape[0]
    bucket = o_ref.shape[1] * o_ref.shape[2] // width
    slot = lax.broadcasted_iota(jnp.int32, (groups * bucket, vision.shape[1]), 0)
    pick = jnp.where(slot == slots_of[...], 1.0, 0.0).astype(BF16)
    moved = lax.dot_general(
        pick, vision, (((1,), (1,)), ((), ())), preferred_element_type=F32
    ).astype(BF16)
    for k in range(groups):
        rows = moved[k * bucket : (k + 1) * bucket]
        if o_ref.shape[2] == width:
            o_ref[k] = rows
            continue
        tiles = width // LANES
        for i in range(tiles):
            o_ref[k, i * bucket : (i + 1) * bucket, :] = rows[:, i * LANES : (i + 1) * LANES]
        rest = rows[:, tiles * LANES :]
        fold = LANES // rest.shape[1]
        piece = bucket // fold
        o_ref[k, tiles * bucket :, :] = jnp.concatenate(
            [rest[i * piece : (i + 1) * piece] for i in range(fold)], axis=1
        )


def place_kernel(targets, text, arrived, o_ref):
    width, rows = text.shape
    groups = arrived.shape[0]
    bucket = arrived.shape[1] * arrived.shape[2] // width
    slots = groups * bucket
    row = lax.broadcasted_iota(jnp.int32, (slots, rows), 1)
    pick = jnp.where(row == targets[...], 1.0, 0.0)
    hit = jnp.sum(pick, axis=0, keepdims=True) > 0.5
    pick = pick.astype(BF16)

    def moved(blocks):
        return lax.dot_general(
            blocks, pick, (((0,), (0,)), ((), ())), preferred_element_type=F32
        ).astype(BF16)

    if arrived.shape[2] == width:
        whole = jnp.concatenate([arrived[k] for k in range(groups)], axis=0)
        o_ref[...] = jnp.where(hit, moved(whole), text[...])
        return
    tiles = width // LANES
    for i in range(tiles):
        part = jnp.concatenate(
            [arrived[k, i * bucket : (i + 1) * bucket, :] for k in range(groups)], axis=0
        )
        at = slice(i * LANES, (i + 1) * LANES)
        o_ref[at, :] = jnp.where(hit, moved(part), text[at, :])
    rest = width % LANES
    parts = []
    for k in range(groups):
        folded = arrived[k, tiles * bucket :, :]
        parts += [folded[:, i * rest : (i + 1) * rest] for i in range(LANES // rest)]
    at = slice(tiles * LANES, width)
    o_ref[at, :] = jnp.where(hit, moved(jnp.concatenate(parts, axis=0)), text[at, :])


def add_kernel(keep, near, o_ref):
    o_ref[...] = (keep[...].astype(F32) + near[...].astype(F32)).astype(BF16)


class Ring:
    def __init__(self, count):
        self.count = count
        order = ring_order(count)
        self.right = [(order[i], order[(i + 1) % count]) for i in range(count)]
        self.left = [(b, a) for a, b in self.right]
        self.done = []
        self.work = []

    def step(self, to_right, to_left):
        t = len(self.done)
        waits = [x for at, x in self.work if at == t - 2]
        if t >= 2:
            before = [self.done[t - 3][1]] if t >= 3 else []
            to_right = after(to_right, self.done[t - 2][0], *before, *waits)
            to_left = after(to_left, *self.done[t - 2])
        pair = (
            lax.ppermute(to_right, "wide", self.right),
            lax.ppermute(to_left, "wide", self.left),
        )
        self.done.append(pair)
        return pair

    def now(self, x):
        if len(self.done) >= 2:
            return after(x, *self.done[-2])
        return x

    def add_work(self, x):
        self.work.append((len(self.done) - 1, x))

    def add_late(self, x, steps):
        self.work.append((len(self.done) - 1 + steps, x))


def per_device(
    patches, norm_gain, norm_bias, w_in, b_in, w_out, b_out, w_proj, b_proj, text, place
):
    groups, parts = lax.axis_size("wide"), lax.axis_size("narrow")
    width, tokens = patches.shape[1], patches.shape[0]
    full = width * parts
    ff = w_in.shape[1]
    windows = tokens // WINDOW
    seq_rows = text.shape[0]
    bucket = seq_rows // groups
    slots = groups * bucket
    shard_rows = [w_in.shape[0], w_out.shape[1], w_proj.shape[2]]
    small = groups == 8 and all(r % 32 == 0 for r in shard_rows)
    halves = 2

    near_pairs = [(i, i ^ 1) for i in range(parts)]
    far_pairs = [(i, i ^ 2) for i in range(parts)]

    def near(x):
        return lax.ppermute(x, "narrow", near_pairs)

    def far(x):
        return lax.ppermute(x, "narrow", far_pairs)


    def order(x):
        return call(
            order_kernel, (x,), [shape(WINDOW // halves, width, windows)] * halves,
            name="order_tokens",
        )

    def shards(count):
        rows = shard_rows[1] // count
        return call(
            shards_kernel, (w_out.T, jnp.transpose(w_proj, (0, 2, 1))),
            [shape(rows, full)] * (2 * count), name="shards",
        )

    def route():
        return call(
            functools.partial(route_kernel, seq_rows, bucket), (place.reshape(groups, windows),),
            [shape(1, windows, dtype=jnp.int32), shape(slots, 1, dtype=jnp.int32)], name="route",
        )

    def norm(*blocks):
        count = tokens // halves
        return call(
            norm_kernel, (*blocks, norm_gain[None], norm_bias[None]), shape(count, full),
            scratch=[pltpu.VMEM((full, count), BF16)], name="norm",
        )

    def hidden(pieces, arrays, normed, first, columns):
        return call(
            functools.partial(hidden_kernel, pieces, groups, shard_rows[0], first, columns),
            (b_in[None], *arrays, *normed), shape(tokens, columns),
            scratch=[pltpu.VMEM((full, columns), BF16)], name="hidden",
        )

    def mlp_out(pieces, arrays, hiddens, over_x):
        outs = call(
            functools.partial(
                out_kernel, pieces, groups, shard_rows[1], over_x, len(hiddens), SUMS
            ),
            (*hiddens, *arrays), [shape(width, tokens // SUMS)] * (2 * SUMS),
            scratch=[pltpu.VMEM((2 * width, ff), BF16)], name="mlp_out",
        )
        return outs[:SUMS], outs[SUMS:]

    def add(keep, other):
        return call(add_kernel, (keep, other), shape(*keep.shape), name="add")

    def stream(own, sums):
        return call(
            functools.partial(stream_kernel, halves), (b_out[:, None], *own, *sums), shape(WINDOW * width, windows),
            name="stream",
        )

    def proj(pieces, arrays, merged):
        return call(
            functools.partial(proj_kernel, pieces, groups, shard_rows[2]),
            (merged, *arrays), [shape(2, width, windows)] * 2,
            scratch=[pltpu.VMEM((full, WINDOW * width), BF16)], name="proj",
        )

    def pack(slots_of, keep, core_sums, x_sums):
        block = (bucket, width)
        if compact(width, bucket):
            block = (bucket * width // LANES, LANES)
        return call(
            functools.partial(pack_kernel, groups),
            (slots_of, keep, core_sums, x_sums, b_proj[:, None]), shape(groups, *block),
            name="pack",
        )

    def exchange_and_place(buffer, targets):
        arrived = lax.all_to_all(buffer, "wide", split_axis=0, concat_axis=0, tiled=True)
        return call(
            place_kernel, (targets, text.T, arrived), shape(width, seq_rows), name="place"
        ).T


    if not small:
        shard = [w_in, *shards(1)]
        wholes = [lax.all_gather(s, "wide", axis=0, tiled=True) for s in shard]
        pieces = [Piece(0, k * width, width, None, 0, k) for k in range(parts)]
        own = order(patches.T)
        over_x = [far(x) for x in own]
        normed = [norm(x, y, near(x), near(y)) for x, y in zip(own, over_x)]
        act = hidden(pieces, wholes[:1], normed, 0, ff)
        keep_x, give_x = mlp_out(pieces, wholes[1:2], [act], 1)
        keep, give = mlp_out(pieces, wholes[1:2], [act], 0)
        x_sums = [far(add(k, near(g))) for k, g in zip(keep_x, give_x)]
        merged = stream(own, [*keep, *[near(g) for g in give], *x_sums])
        slots_of, targets = route()
        keep, give = proj(pieces, wholes[2:], merged)
        core_sums = near(give)
        x_sums = far(add(keep[1], core_sums[1]))
        return exchange_and_place(pack(slots_of, keep, core_sums, x_sums), targets)


    ring = Ring(groups)
    half_rows = shard_rows[0] // 2
    last = groups // 2

    def hops(halves, work):
        arrays = list(halves)
        pieces = [Piece(h, 0, half_rows, 0, h * half_rows) for h in (0, 1)]
        held = {(way, h): halves[h] for way in (0, 1) for h in (0, 1)}
        t = 0
        for step in range(1, last + 1):
            for first in (0, 1):
                if step == last and first == 1:
                    continue
                pair = ring.step(held[0, first], held[1, 1 - first])
                for way, h in ((0, first), (1, 1 - first)):
                    held[way, h] = pair[way]
                    shift = -step if way == 0 else step
                    pieces.append(Piece(len(arrays), 0, half_rows, shift, h * half_rows))
                    arrays.append(pair[way])
                if t in work:
                    work[t]()
                t += 1
        return pieces, arrays

    got, normed = {}, []

    over_x, over_core, over_both = [], [], []

    def start_tokens():
        got["own"] = order(patches.T)
        over_x.append(far(got["own"][0]))
        ring.add_work(got["own"][0])

    def start_shards():
        got["shards"] = shards(2)
        ring.add_work(got["shards"][0])

    def send_second():
        over_x.append(far(ring.now(got["own"][1])))
        got["slots_of"], got["targets"] = route()

    def send_core():
        over_core.append(near(ring.now(got["own"][len(over_core)])))

    def send_both():
        over_both.append(near(ring.now(over_x[len(over_both)])))

    def start_norm():
        i = len(normed)
        normed.append(
            norm(ring.now(got["own"][i]), over_x[i], over_core[i], over_both[i])
        )
        ring.add_work(normed[-1])

    pieces_in, arrays_in = hops(
        [w_in[:half_rows], w_in[half_rows:]],
        {0: start_tokens, 1: start_shards, 2: send_second, 3: send_core, 4: send_both,
         5: send_core, 6: send_both},
    )

    hiddens = []
    second = {NORM_AT: start_norm, NORM_AT + 1: start_norm}

    def start_hidden():
        rows = [ring.now(normed[0]), *normed[1:]]
        hiddens.append(hidden(pieces_in, arrays_in, rows, len(hiddens) * columns, columns))
        ring.add_work(hiddens[-1])

    columns = 256
    for t in range(ff // columns):
        second[HIDDEN_AT + t] = start_hidden
    pieces_out, arrays_out = hops(got["shards"][:2], second)

    def start_out(over_x):
        acts = [ring.now(hiddens[0]), *hiddens[1:]]
        if over_x == 0:
            acts[0] = after(acts[0], *got["sums"])
        keep, give = mlp_out(pieces_out, arrays_out, acts, over_x)
        got["keep", over_x] = keep
        got["core", over_x] = [near(g) for g in give]
        ring.add_work(keep[0])

    def start_sums():
        sums = [add(k, c) for k, c in zip(got["keep", 1], got["core", 1])]
        got["x_sums"] = [far(x) for x in sums]
        got["sums"] = sums
        for steps, x in zip(ADD_LATE, sums):
            ring.add_late(x, steps)
        for steps, x in zip(LATE, got["x_sums"]):
            ring.add_late(x, steps)

    def start_first():
        start_out(1)
        start_sums()

    pieces_proj, arrays_proj = hops(
        got["shards"][2:], {0: start_first, OWN_AT: lambda: start_out(0)}
    )

    merged = stream(
        got["own"], [*got["keep", 0], *got["core", 0], *got["x_sums"]]
    )
    keep, give = proj(pieces_proj, arrays_proj, merged)
    core_sums = near(give)
    x_sums = far(add(keep[1], core_sums[1]))
    return exchange_and_place(pack(got["slots_of"], keep, core_sums, x_sums), got["targets"])


def solution(mesh):
    placed = (
        P("wide", "narrow"),
        P(),
        P(),
        P("wide", "narrow"),
        P("narrow"),
        P("narrow", "wide"),
        P("narrow"),
        P(None, "narrow", "wide"),
        P("narrow"),
        P("wide", "narrow"),
        P(),
    )
    return jax.shard_map(
        per_device, mesh=mesh, in_specs=placed, out_specs=P("wide", "narrow"), check_vma=False
    )
```

```python
import functools

import jax
import jax.numpy as jnp
from jax import lax
from jax.experimental import pallas as pl
from jax.experimental.pallas import tpu as pltpu
from jax.sharding import PartitionSpec as P

F32 = jnp.float32
BF16 = jnp.bfloat16
WINDOW = 4
LATE = (1, 2, 2)
HIDDEN_AT = (7, 7, 8, 8, 8)
OUT_AT = 1
SUMS_AT = 2
VMEM = pl.BlockSpec(memory_space=pltpu.VMEM)


def call(kernel, operands, outs, scratch=(), name=None):
    single = not isinstance(outs, (list, tuple))
    return pl.pallas_call(
        kernel,
        out_shape=outs,
        in_specs=[VMEM] * len(operands),
        out_specs=VMEM if single else [VMEM] * len(outs),
        scratch_shapes=list(scratch),
        compiler_params=pltpu.CompilerParams(vmem_limit_bytes=28 * 1024 * 1024),
        cost_estimate=pl.CostEstimate(flops=0, bytes_accessed=0, transcendentals=0),
        name=name,
    )(*operands)


def shape(*dims, dtype=BF16):
    return jax.ShapeDtypeStruct(dims, dtype)


def after(x, *others):
    return lax.optimization_barrier((x, *others))[0]


def ring_order(count):
    return list(range(0, count, 2)) + list(range(count - 1, 0, -2))


def ring_owner(me, shift, count):
    half = me // 2
    at = jnp.where(me % 2 == 0, half, count - 1 - half) + (shift + count)
    at = at % count
    return jnp.where(at < count // 2, 2 * at, 2 * (count - 1 - at) + 1)


class Piece:
    def __init__(self, array, start, rows, shift, base, index=0):
        self.array, self.start, self.rows = array, start, rows
        self.shift, self.base, self.index = shift, base, index

    def row(self, count, shard_rows):
        if self.shift is None:
            return self.index * self.rows
        return ring_owner(lax.axis_index("wide"), self.shift, count) * shard_rows + self.base

    def block_row(self, count, shard_rows, block):
        if self.shift is None:
            of, inside = self.index, 0
        else:
            owner = ring_owner(lax.axis_index("wide"), self.shift, count)
            per_block = block // shard_rows
            of, inside = owner // per_block, (owner % per_block) * shard_rows + self.base
        mine = lax.axis_index("narrow")
        over_x = jnp.where(of // 2 == mine // 2, 0, 1)
        over_core = jnp.where(of % 2 == mine % 2, 0, 1)
        return over_x, over_core, inside


def rows_at(start, rows):
    return pl.ds(pl.multiple_of(start, 16), rows)


def order_kernel(x_ref, *outs):
    tokens = x_ref.shape[1]
    windows = tokens // WINDOW
    source = lax.broadcasted_iota(jnp.int32, (tokens, windows), 0)
    window = lax.broadcasted_iota(jnp.int32, (tokens, windows), 1)
    each = WINDOW // len(outs)
    for p in range(WINDOW):
        pick = jnp.where(source == WINDOW * window + p, 1.0, 0.0).astype(BF16)
        outs[p // each][p % each] = jnp.dot(
            x_ref[...], pick, preferred_element_type=F32
        ).astype(BF16)


def shards_kernel(w_proj, *outs):
    half = w_proj.shape[1] // len(outs)
    flat = jnp.concatenate([w_proj[p] for p in range(WINDOW)], axis=1)
    for i, o_ref in enumerate(outs):
        o_ref[...] = flat[i * half : (i + 1) * half, :]


def route_kernel(seq_rows, bucket, place, slots_of, targets):
    groups, windows = place.shape
    me = lax.axis_index("wide")
    table = place[...]
    owner = jnp.where(table >= 0, 0, -1)
    for d in range(1, groups):
        owner = owner + jnp.where(table >= d * seq_rows, 1, 0)
    earlier = jnp.where(
        lax.broadcasted_iota(jnp.int32, (windows, windows), 0)
        <= lax.broadcasted_iota(jnp.int32, (windows, windows), 1),
        1.0,
        0.0,
    ).astype(BF16)
    here = jnp.where(owner == me, 1.0, 0.0)
    rank = jnp.dot(here.astype(BF16), earlier, preferred_element_type=F32)
    rank = jnp.where(owner == me, rank, 0.0).astype(jnp.int32)
    local = table - me * seq_rows
    slot = lax.broadcasted_iota(jnp.int32, (bucket, windows), 0) + 1
    source_at = lax.broadcasted_iota(jnp.int32, (groups, windows), 0)
    for k in range(groups):
        wanted = source_at == k
        of_rank = jnp.sum(jnp.where(wanted, rank, 0), axis=0, keepdims=True)
        of_local = jnp.sum(jnp.where(wanted, local, 0), axis=0, keepdims=True)
        found = jnp.where(of_rank == slot, of_local + 1, 0)
        targets[k * bucket : (k + 1) * bucket, :] = jnp.sum(found, axis=1, keepdims=True) - 1
    mine = jnp.sum(jnp.where(source_at == me, owner, 0), axis=0, keepdims=True)
    hits = source_at == mine
    rank = jnp.dot(
        jnp.where(hits, 1.0, 0.0).astype(BF16), earlier, preferred_element_type=F32
    )
    rank = jnp.sum(jnp.where(hits, rank, 0.0), axis=0, keepdims=True).astype(jnp.int32)
    slots_of[...] = jnp.where(mine >= 0, mine * bucket + rank - 1, groups * bucket)


def norm_kernel(own, over_x, over_core, over_both, gain, bias, o_ref, whole):
    parts = (own, over_x, over_core, over_both)
    each, rows, windows = own.shape
    tokens = each * windows
    mine = lax.axis_index("narrow")
    for part, flip in zip(parts, (0, 2, 1, 3)):
        at = (mine ^ flip) * rows
        for j in range(each):
            whole[rows_at(at, rows), j * windows : (j + 1) * windows] = part[j]
    width = whole.shape[0]
    step = 128
    for t in range(0, tokens, step):
        values = whole[:, t : t + step].astype(F32)
        center = jnp.sum(values, axis=0, keepdims=True) * (1.0 / width)
        values = values - center
        spread = jnp.sum(values * values, axis=0, keepdims=True) * (1.0 / width)
        values = (values * lax.rsqrt(spread + 1e-06)).T
        o_ref[t : t + step, :] = (values * gain[...] + bias[...]).astype(BF16)


def hidden_kernel(pieces, count, shard_rows, first, columns, bias, *refs):
    arrays = 1 + max(p.array for p in pieces)
    sources, normed, (o_ref, part) = refs[:arrays], refs[arrays:-2], refs[-2:]
    for p in pieces:
        part[rows_at(p.row(count, shard_rows), p.rows), :] = sources[p.array][
            p.start : p.start + p.rows, first : first + columns
        ]
    at = 0
    for rows in normed:
        v = jnp.dot(rows[...], part[...], preferred_element_type=F32)
        v = v + bias[:, first : first + columns]
        o_ref[at : at + rows.shape[0], :] = (
            0.5 * v * (1.0 + lax.erf(v * (2.0**-0.5)))
        ).astype(BF16)
        at += rows.shape[0]


def out_kernel(pieces, count, shard_rows, over_x, hidden_count, chunks, *refs):
    hidden, refs = refs[:hidden_count], refs[hidden_count:]
    outs, part = refs[-1 - 2 * chunks : -1], refs[-1]
    keep, give = outs[:chunks], outs[chunks:]
    sources = refs[: -1 - 2 * chunks]
    block, tokens = keep[0].shape
    for p in pieces:
        x, core, inside = p.block_row(count, shard_rows, block)

        @pl.when(x == over_x)
        def _():
            part[rows_at(core * block + inside, p.rows), :] = sources[p.array][
                p.start : p.start + p.rows, :
            ]

    columns = hidden[0].shape[1]
    step = 256
    for t in range(0, tokens * chunks, step):
        total = None
        for i, h in enumerate(hidden):
            v = lax.dot_general(
                part[:, i * columns : (i + 1) * columns],
                h[t : t + step, :],
                (((1,), (1,)), ((), ())),
                preferred_element_type=F32,
            )
            total = v if total is None else total + v
        total = total.astype(BF16)
        c, at = t // tokens, t % tokens
        keep[c][:, at : at + step] = total[:block]
        give[c][:, at : at + step] = total[block:]


def proj_kernel(pieces, count, shard_rows, merged, *refs):
    sources, (keep, give, part) = refs[:-3], refs[-3:]
    block = keep.shape[1]
    for p in pieces:
        x, core, inside = p.block_row(count, shard_rows, block)
        at = rows_at(core * 2 * block + x * block + inside, p.rows)
        part[at, :] = sources[p.array][p.start : p.start + p.rows, :]
    for core, target in ((1, give), (0, keep)):
        v = jnp.dot(
            part[core * 2 * block : (core + 1) * 2 * block, :],
            merged[...],
            preferred_element_type=F32,
        ).astype(BF16)
        target[0] = v[:block]
        target[1] = v[block:]


def stream_kernel(chunks, bias, *refs):
    o_ref = refs[-1]
    own = refs[:chunks]
    keep, near, far = (
        refs[chunks + i * WINDOW : chunks + (i + 1) * WINDOW] for i in range(3)
    )
    each, rows, windows = own[0].shape
    for p in range(WINDOW):
        total = keep[p][...].astype(F32) + near[p][...].astype(F32) + far[p][...].astype(F32)
        v = own[p // each][p % each].astype(F32) + (total + bias[...])
        o_ref[p * rows : (p + 1) * rows, :] = v.astype(BF16)


LANES = 128


def compact(width, bucket):
    rest = width % LANES
    return rest > 0 and LANES % rest == 0 and bucket % (16 * (LANES // rest)) == 0


def pack_kernel(groups, slots_of, keep, near, far, bias, o_ref):
    total = keep[0].astype(F32) + near[0].astype(F32) + far[...].astype(F32)
    vision = (total + bias[...]).astype(BF16)
    width = vision.shape[0]
    bucket = o_ref.shape[1] * o_ref.shape[2] // width
    slot = lax.broadcasted_iota(jnp.int32, (groups * bucket, vision.shape[1]), 0)
    pick = jnp.where(slot == slots_of[...], 1.0, 0.0).astype(BF16)
    moved = lax.dot_general(
        pick, vision, (((1,), (1,)), ((), ())), preferred_element_type=F32
    ).astype(BF16)
    for k in range(groups):
        rows = moved[k * bucket : (k + 1) * bucket]
        if o_ref.shape[2] == width:
            o_ref[k] = rows
            continue
        tiles = width // LANES
        for i in range(tiles):
            o_ref[k, i * bucket : (i + 1) * bucket, :] = rows[:, i * LANES : (i + 1) * LANES]
        rest = rows[:, tiles * LANES :]
        fold = LANES // rest.shape[1]
        piece = bucket // fold
        o_ref[k, tiles * bucket :, :] = jnp.concatenate(
            [rest[i * piece : (i + 1) * piece] for i in range(fold)], axis=1
        )


def place_kernel(targets, text, arrived, o_ref):
    width, rows = text.shape
    groups = arrived.shape[0]
    bucket = arrived.shape[1] * arrived.shape[2] // width
    slots = groups * bucket
    row = lax.broadcasted_iota(jnp.int32, (slots, rows), 1)
    pick = jnp.where(row == targets[...], 1.0, 0.0)
    hit = jnp.sum(pick, axis=0, keepdims=True) > 0.5
    pick = pick.astype(BF16)

    def moved(blocks):
        return lax.dot_general(
            blocks, pick, (((0,), (0,)), ((), ())), preferred_element_type=F32
        ).astype(BF16)

    if arrived.shape[2] == width:
        whole = jnp.concatenate([arrived[k] for k in range(groups)], axis=0)
        o_ref[...] = jnp.where(hit, moved(whole), text[...])
        return
    tiles = width // LANES
    for i in range(tiles):
        part = jnp.concatenate(
            [arrived[k, i * bucket : (i + 1) * bucket, :] for k in range(groups)], axis=0
        )
        at = slice(i * LANES, (i + 1) * LANES)
        o_ref[at, :] = jnp.where(hit, moved(part), text[at, :])
    rest = width % LANES
    parts = []
    for k in range(groups):
        folded = arrived[k, tiles * bucket :, :]
        parts += [folded[:, i * rest : (i + 1) * rest] for i in range(LANES // rest)]
    at = slice(tiles * LANES, width)
    o_ref[at, :] = jnp.where(hit, moved(jnp.concatenate(parts, axis=0)), text[at, :])


def add_kernel(keep, near, o_ref):
    o_ref[...] = (keep[...].astype(F32) + near[...].astype(F32)).astype(BF16)


class Ring:
    def __init__(self, count):
        self.count = count
        order = ring_order(count)
        self.right = [(order[i], order[(i + 1) % count]) for i in range(count)]
        self.left = [(b, a) for a, b in self.right]
        self.done = []
        self.work = []

    def step(self, to_right, to_left):
        t = len(self.done)
        waits = [x for at, x in self.work if at == t - 2]
        if t >= 2:
            before = [self.done[t - 3][1]] if t >= 3 else []
            to_right = after(to_right, self.done[t - 2][0], *before, *waits)
            to_left = after(to_left, *self.done[t - 2])
        pair = (
            lax.ppermute(to_right, "wide", self.right),
            lax.ppermute(to_left, "wide", self.left),
        )
        self.done.append(pair)
        return pair

    def now(self, x):
        if len(self.done) >= 2:
            return after(x, *self.done[-2])
        return x

    def add_work(self, x):
        self.work.append((len(self.done) - 1, x))

    def add_late(self, x, steps):
        self.work.append((len(self.done) - 1 + steps, x))


def per_device(
    patches, norm_gain, norm_bias, w_in, b_in, w_out, b_out, w_proj, b_proj, text, place
):
    groups, parts = lax.axis_size("wide"), lax.axis_size("narrow")
    width, tokens = patches.shape[1], patches.shape[0]
    full = width * parts
    ff = w_in.shape[1]
    windows = tokens // WINDOW
    seq_rows = text.shape[0]
    bucket = seq_rows // groups
    slots = groups * bucket
    shard_rows = [w_in.shape[0], w_out.shape[1], w_proj.shape[2]]
    small = groups == 8 and all(r % 32 == 0 for r in shard_rows)
    chunks = 2

    near_pairs = [(i, i ^ 1) for i in range(parts)]
    far_pairs = [(i, i ^ 2) for i in range(parts)]

    def near(x):
        return lax.ppermute(x, "narrow", near_pairs)

    def far(x):
        return lax.ppermute(x, "narrow", far_pairs)


    def order(x):
        return call(
            order_kernel, (x,), [shape(WINDOW // chunks, width, windows)] * chunks,
            name="order_tokens",
        )

    def shards(count):
        rows = shard_rows[2] // count
        return call(
            shards_kernel, (jnp.transpose(w_proj, (0, 2, 1)),),
            [shape(rows, WINDOW * width)] * count, name="shards",
        )

    def route():
        return call(
            functools.partial(route_kernel, seq_rows, bucket), (place.reshape(groups, windows),),
            [shape(1, windows, dtype=jnp.int32), shape(slots, 1, dtype=jnp.int32)], name="route",
        )

    def norm(blocks):
        count = tokens // chunks
        return call(
            norm_kernel, (*blocks, norm_gain[None], norm_bias[None]), shape(count, full),
            scratch=[pltpu.VMEM((full, count), BF16)], name="norm",
        )

    def hidden(pieces, arrays, normed, first, columns):
        return call(
            functools.partial(hidden_kernel, pieces, groups, shard_rows[0], first, columns),
            (b_in[None], *arrays, *normed), shape(tokens, columns),
            scratch=[pltpu.VMEM((full, columns), BF16)], name="hidden",
        )

    def mlp_out(pieces, arrays, hiddens, over_x):
        outs = call(
            functools.partial(
                out_kernel, pieces, groups, shard_rows[1], over_x, len(hiddens), WINDOW
            ),
            (*hiddens, *arrays), [shape(width, windows)] * (2 * WINDOW),
            scratch=[pltpu.VMEM((2 * width, ff), BF16)], name="mlp_out",
        )
        return outs[:WINDOW], outs[WINDOW:]

    def add(keep, other):
        return call(add_kernel, (keep, other), shape(*keep.shape), name="add")

    def stream(own, keep, core_sums, x_sums):
        return call(
            functools.partial(stream_kernel, chunks),
            (b_out[:, None], *own, *keep, *core_sums, *x_sums),
            shape(WINDOW * width, windows), name="stream",
        )

    def proj(pieces, arrays, merged):
        return call(
            functools.partial(proj_kernel, pieces, groups, shard_rows[2]),
            (merged, *arrays), [shape(2, width, windows)] * 2,
            scratch=[pltpu.VMEM((full, WINDOW * width), BF16)], name="proj",
        )

    def pack(slots_of, keep, core_sums, x_sums):
        block = (bucket, width)
        if compact(width, bucket):
            block = (bucket * width // LANES, LANES)
        return call(
            functools.partial(pack_kernel, groups),
            (slots_of, keep, core_sums, x_sums, b_proj[:, None]), shape(groups, *block),
            name="pack",
        )

    def exchange_and_place(buffer, targets):
        arrived = lax.all_to_all(buffer, "wide", split_axis=0, concat_axis=0, tiled=True)
        return call(
            place_kernel, (targets, text.T, arrived), shape(width, seq_rows), name="place"
        ).T


    if not small:
        shard = [w_in, w_out.T, *shards(1)]
        wholes = [lax.all_gather(s, "wide", axis=0, tiled=True) for s in shard]
        pieces = [Piece(0, k * width, width, None, 0, k) for k in range(parts)]
        own = order(patches.T)
        over_x = [far(x) for x in own]
        normed = [norm((x, y, near(x), near(y))) for x, y in zip(own, over_x)]
        act = hidden(pieces, wholes[:1], normed, 0, ff)
        keep_x, give_x = mlp_out(pieces, wholes[1:2], [act], 1)
        keep, give = mlp_out(pieces, wholes[1:2], [act], 0)
        x_sums = [far(add(k, near(g))) for k, g in zip(keep_x, give_x)]
        merged = stream(own, keep, [near(g) for g in give], x_sums)
        slots_of, targets = route()
        keep, give = proj(pieces, wholes[2:], merged)
        core_sums = near(give)
        x_sums = far(add(keep[1], core_sums[1]))
        return exchange_and_place(pack(slots_of, keep, core_sums, x_sums), targets)


    ring = Ring(groups)
    half_rows = shard_rows[0] // 2
    last = groups // 2

    def gather(halves, work):
        arrays = list(halves)
        pieces = [Piece(h, 0, half_rows, 0, h * half_rows) for h in (0, 1)]
        held = {(way, h): halves[h] for way in (0, 1) for h in (0, 1)}
        t = 0
        for step in range(1, last + 1):
            for first in (0, 1):
                if step == last and first == 1:
                    continue
                pair = ring.step(held[0, first], held[1, 1 - first])
                for way, h in ((0, first), (1, 1 - first)):
                    held[way, h] = pair[way]
                    shift = -step if way == 0 else step
                    pieces.append(Piece(len(arrays), 0, half_rows, shift, h * half_rows))
                    arrays.append(pair[way])
                if t in work:
                    work[t]()
                t += 1
        return pieces, arrays

    def hops_of_two(shards, work):
        arrays = [[x] for x in shards]
        pieces = [[Piece(0, 0, 2 * half_rows, 0, 0)] for _ in shards]
        held = {(way, k): x for way in (0, 1) for k, x in enumerate(shards)}
        t = 0
        for step in range(1, last + 1):
            for k in range(len(shards)):
                sent = [held[0, k], held[1, k]]
                rows, bases = 2 * half_rows, (0, 0)
                if step == last:
                    sent = [sent[0][:half_rows], sent[1][half_rows:]]
                    rows, bases = half_rows, (0, half_rows)
                pair = ring.step(*sent)
                for way in (0, 1):
                    held[way, k] = pair[way]
                    shift = -step if way == 0 else step
                    pieces[k].append(Piece(len(arrays[k]), 0, rows, shift, bases[way]))
                    arrays[k].append(pair[way])
                if t in work:
                    for run in work[t]:
                        run(pieces, arrays)
                t += 1
        return pieces, arrays

    own, over_x, over_core, over_both, normed = [], [], [], [], []
    got = {}

    def start_tokens():
        own.extend(order(patches.T))
        over_x.append(far(own[0]))
        ring.add_work(own[0])

    def start_shards():
        got["shards"] = shards(2)
        ring.add_work(got["shards"][0])
        over_core.extend(near(x) for x in own)

    def send_second():
        over_x.append(far(ring.now(own[1])))
        got["slots_of"], got["targets"] = route()

    def send_both():
        over_both.append(near(ring.now(over_x[len(over_both)])))

    def start_norm():
        i = len(normed)
        first = ring.now(own[i])
        normed.append(norm((first, over_x[i], over_core[i], over_both[i])))
        ring.add_work(normed[i])

    def both_and_norm():
        send_both()
        start_norm()

    columns = 256
    hiddens = []

    def start_hidden():
        rows = [ring.now(normed[0]), *normed[1:]]
        hiddens.append(hidden(pieces_in, arrays_in, rows, len(hiddens) * columns, columns))
        ring.add_work(hiddens[-1])

    early = {0: start_tokens, 1: send_second, 2: start_shards, 3: send_both, 4: both_and_norm,
             5: start_norm}
    work = {t: [lambda p, a, run=run: run()] for t, run in early.items()}
    first_of_last = 2 * last

    def hidden_in_pair(pieces, arrays):
        rows = [ring.now(normed[0]), *normed[1:]]
        hiddens.append(hidden(pieces[0], arrays[0], rows, len(hiddens) * columns, columns))
        ring.add_work(hiddens[-1])

    for t in HIDDEN_AT:
        if t < first_of_last:
            work.setdefault(t, []).append(hidden_in_pair)
    (pieces_in, pieces_out), (arrays_in, arrays_out) = hops_of_two([w_in, w_out.T], work)

    def start_out(over_x):
        acts = [ring.now(hiddens[0]), *hiddens[1:]]
        keep, give = mlp_out(pieces_out, arrays_out, acts, over_x)
        got["keep", over_x] = keep
        got["core", over_x] = [near(g) for g in give]
        ring.add_work(keep[0])

    def start_sums():
        core = [ring.now(got["core", 1][0]), *got["core", 1][1:]]
        sums = [add(k, c) for k, c in zip(got["keep", 1], core)]
        got["x_sums"] = [far(x) for x in sums]
        for i, x in enumerate(got["x_sums"][:-1]):
            ring.add_late(x, LATE[i])
        ring.add_work(sums[0])
        start_out(0)

    plan = {}
    for t in HIDDEN_AT:
        if t >= first_of_last:
            plan.setdefault(t - first_of_last, []).append(start_hidden)
    plan.setdefault(OUT_AT, []).append(lambda: start_out(1))
    plan.setdefault(SUMS_AT, []).append(start_sums)

    def run_all(steps):
        def run():
            for step in steps:
                step()
        return run

    pieces_proj, arrays_proj = gather(
        got["shards"], {t: run_all(steps) for t, steps in plan.items()}
    )

    merged = stream(own, got["keep", 0], got["core", 0], got["x_sums"])
    keep, give = proj(pieces_proj, arrays_proj, merged)
    core_sums = near(give)
    x_sums = far(add(keep[1], core_sums[1]))
    return exchange_and_place(pack(got["slots_of"], keep, core_sums, x_sums), got["targets"])


def solution(mesh):
    placed = (
        P("wide", "narrow"),
        P(),
        P(),
        P("wide", "narrow"),
        P("narrow"),
        P("narrow", "wide"),
        P("narrow"),
        P(None, "narrow", "wide"),
        P("narrow"),
        P("wide", "narrow"),
        P(),
    )
    return jax.shard_map(
        per_device, mesh=mesh, in_specs=placed, out_specs=P("wide", "narrow"), check_vma=False
    )
```

```python
import functools

import jax
import jax.numpy as jnp
from jax import lax
from jax.experimental import pallas as pl
from jax.experimental.pallas import tpu as pltpu
from jax.sharding import PartitionSpec as P

F32 = jnp.float32
BF16 = jnp.bfloat16
WINDOW = 4
LATE = (1, 2, 3)
HIDDEN_AT = (7, 7, 8, 8, 8)
OUT_AT = 1
OWN_PARTS = 1
SUMS_AT = 2
VMEM = pl.BlockSpec(memory_space=pltpu.VMEM)


def call(kernel, operands, outs, scratch=(), name=None):
    single = not isinstance(outs, (list, tuple))
    return pl.pallas_call(
        kernel,
        out_shape=outs,
        in_specs=[VMEM] * len(operands),
        out_specs=VMEM if single else [VMEM] * len(outs),
        scratch_shapes=list(scratch),
        compiler_params=pltpu.CompilerParams(vmem_limit_bytes=28 * 1024 * 1024),
        cost_estimate=pl.CostEstimate(flops=0, bytes_accessed=0, transcendentals=0),
        name=name,
    )(*operands)


def shape(*dims, dtype=BF16):
    return jax.ShapeDtypeStruct(dims, dtype)


def after(x, *others):
    return lax.optimization_barrier((x, *others))[0]


def ring_order(count):
    return list(range(0, count, 2)) + list(range(count - 1, 0, -2))


def ring_owner(me, shift, count):
    half = me // 2
    at = jnp.where(me % 2 == 0, half, count - 1 - half) + (shift + count)
    at = at % count
    return jnp.where(at < count // 2, 2 * at, 2 * (count - 1 - at) + 1)


class Piece:
    def __init__(self, array, start, rows, shift, base, index=0):
        self.array, self.start, self.rows = array, start, rows
        self.shift, self.base, self.index = shift, base, index

    def row(self, count, shard_rows):
        if self.shift is None:
            return self.index * self.rows
        return ring_owner(lax.axis_index("wide"), self.shift, count) * shard_rows + self.base

    def block_row(self, count, shard_rows, block):
        if self.shift is None:
            of, inside = self.index, 0
        else:
            owner = ring_owner(lax.axis_index("wide"), self.shift, count)
            per_block = block // shard_rows
            of, inside = owner // per_block, (owner % per_block) * shard_rows + self.base
        mine = lax.axis_index("narrow")
        over_x = jnp.where(of // 2 == mine // 2, 0, 1)
        over_core = jnp.where(of % 2 == mine % 2, 0, 1)
        return over_x, over_core, inside


def rows_at(start, rows):
    return pl.ds(pl.multiple_of(start, 16), rows)


def order_kernel(x_ref, *outs):
    tokens = x_ref.shape[1]
    windows = tokens // WINDOW
    source = lax.broadcasted_iota(jnp.int32, (tokens, windows), 0)
    window = lax.broadcasted_iota(jnp.int32, (tokens, windows), 1)
    each = WINDOW // len(outs)
    for p in range(WINDOW):
        pick = jnp.where(source == WINDOW * window + p, 1.0, 0.0).astype(BF16)
        outs[p // each][p % each] = jnp.dot(
            x_ref[...], pick, preferred_element_type=F32
        ).astype(BF16)


def shards_kernel(w_proj, *outs):
    half = w_proj.shape[1] // len(outs)
    flat = jnp.concatenate([w_proj[p] for p in range(WINDOW)], axis=1)
    for i, o_ref in enumerate(outs):
        o_ref[...] = flat[i * half : (i + 1) * half, :]


def route_kernel(seq_rows, bucket, place, slots_of, targets):
    groups, windows = place.shape
    me = lax.axis_index("wide")
    table = place[...]
    owner = jnp.where(table >= 0, 0, -1)
    for d in range(1, groups):
        owner = owner + jnp.where(table >= d * seq_rows, 1, 0)
    earlier = jnp.where(
        lax.broadcasted_iota(jnp.int32, (windows, windows), 0)
        <= lax.broadcasted_iota(jnp.int32, (windows, windows), 1),
        1.0,
        0.0,
    ).astype(BF16)
    here = jnp.where(owner == me, 1.0, 0.0)
    rank = jnp.dot(here.astype(BF16), earlier, preferred_element_type=F32)
    rank = jnp.where(owner == me, rank, 0.0).astype(jnp.int32)
    local = table - me * seq_rows
    slot = lax.broadcasted_iota(jnp.int32, (bucket, windows), 0) + 1
    source_at = lax.broadcasted_iota(jnp.int32, (groups, windows), 0)
    for k in range(groups):
        wanted = source_at == k
        of_rank = jnp.sum(jnp.where(wanted, rank, 0), axis=0, keepdims=True)
        of_local = jnp.sum(jnp.where(wanted, local, 0), axis=0, keepdims=True)
        found = jnp.where(of_rank == slot, of_local + 1, 0)
        targets[k * bucket : (k + 1) * bucket, :] = jnp.sum(found, axis=1, keepdims=True) - 1
    mine = jnp.sum(jnp.where(source_at == me, owner, 0), axis=0, keepdims=True)
    hits = source_at == mine
    rank = jnp.dot(
        jnp.where(hits, 1.0, 0.0).astype(BF16), earlier, preferred_element_type=F32
    )
    rank = jnp.sum(jnp.where(hits, rank, 0.0), axis=0, keepdims=True).astype(jnp.int32)
    slots_of[...] = jnp.where(mine >= 0, mine * bucket + rank - 1, groups * bucket)


def norm_kernel(own, over_x, over_core, over_both, gain, bias, o_ref, whole):
    parts = (own, over_x, over_core, over_both)
    each, rows, windows = own.shape
    tokens = each * windows
    mine = lax.axis_index("narrow")
    for part, flip in zip(parts, (0, 2, 1, 3)):
        at = (mine ^ flip) * rows
        for j in range(each):
            whole[rows_at(at, rows), j * windows : (j + 1) * windows] = part[j]
    width = whole.shape[0]
    step = 128
    for t in range(0, tokens, step):
        values = whole[:, t : t + step].astype(F32)
        center = jnp.sum(values, axis=0, keepdims=True) * (1.0 / width)
        values = values - center
        spread = jnp.sum(values * values, axis=0, keepdims=True) * (1.0 / width)
        values = (values * lax.rsqrt(spread + 1e-06)).T
        o_ref[t : t + step, :] = (values * gain[...] + bias[...]).astype(BF16)


def hidden_kernel(pieces, count, shard_rows, first, columns, bias, *refs):
    arrays = 1 + max(p.array for p in pieces)
    sources, normed, (o_ref, part) = refs[:arrays], refs[arrays:-2], refs[-2:]
    for p in pieces:
        part[rows_at(p.row(count, shard_rows), p.rows), :] = sources[p.array][
            p.start : p.start + p.rows, first : first + columns
        ]
    at = 0
    for rows in normed:
        v = jnp.dot(rows[...], part[...], preferred_element_type=F32)
        v = v + bias[:, first : first + columns]
        o_ref[at : at + rows.shape[0], :] = (
            0.5 * v * (1.0 + lax.erf(v * (2.0**-0.5)))
        ).astype(BF16)
        at += rows.shape[0]


def out_kernel(pieces, count, shard_rows, over_x, hidden_count, chunks, *refs):
    hidden, refs = refs[:hidden_count], refs[hidden_count:]
    outs, part = refs[-1 - 2 * chunks : -1], refs[-1]
    keep, give = outs[:chunks], outs[chunks:]
    sources = refs[: -1 - 2 * chunks]
    block, tokens = keep[0].shape
    for p in pieces:
        x, core, inside = p.block_row(count, shard_rows, block)

        @pl.when(x == over_x)
        def _():
            part[rows_at(core * block + inside, p.rows), :] = sources[p.array][
                p.start : p.start + p.rows, :
            ]

    columns = hidden[0].shape[1]
    step = 256
    for t in range(0, tokens * chunks, step):
        total = None
        for i, h in enumerate(hidden):
            v = lax.dot_general(
                part[:, i * columns : (i + 1) * columns],
                h[t : t + step, :],
                (((1,), (1,)), ((), ())),
                preferred_element_type=F32,
            )
            total = v if total is None else total + v
        total = total.astype(BF16)
        c, at = t // tokens, t % tokens
        keep[c][:, at : at + step] = total[:block]
        give[c][:, at : at + step] = total[block:]


def proj_kernel(pieces, count, shard_rows, merged, *refs):
    sources, (keep, give, part) = refs[:-3], refs[-3:]
    block = keep.shape[1]
    for p in pieces:
        x, core, inside = p.block_row(count, shard_rows, block)
        at = rows_at(core * 2 * block + x * block + inside, p.rows)
        part[at, :] = sources[p.array][p.start : p.start + p.rows, :]
    for core, target in ((1, give), (0, keep)):
        v = jnp.dot(
            part[core * 2 * block : (core + 1) * 2 * block, :],
            merged[...],
            preferred_element_type=F32,
        ).astype(BF16)
        target[0] = v[:block]
        target[1] = v[block:]


def stream_kernel(chunks, bias, *refs):
    o_ref = refs[-1]
    own, refs = refs[:chunks], refs[chunks:-1]
    keep, near, far = refs[:OWN_PARTS], refs[OWN_PARTS : 2 * OWN_PARTS], refs[2 * OWN_PARTS :]
    of_own = WINDOW // OWN_PARTS
    each, rows, windows = own[0].shape
    for p in range(WINDOW):
        at = slice(p % of_own * windows, (p % of_own + 1) * windows)
        total = keep[p // of_own][:, at].astype(F32) + near[p // of_own][:, at].astype(F32)
        total = total + far[p][...].astype(F32)
        v = own[p // each][p % each].astype(F32) + (total + bias[...])
        o_ref[p * rows : (p + 1) * rows, :] = v.astype(BF16)


LANES = 128


def compact(width, bucket):
    rest = width % LANES
    return rest > 0 and LANES % rest == 0 and bucket % (16 * (LANES // rest)) == 0


def pack_kernel(groups, slots_of, keep, near, far, bias, o_ref):
    total = keep[0].astype(F32) + near[0].astype(F32) + far[...].astype(F32)
    vision = (total + bias[...]).astype(BF16)
    width = vision.shape[0]
    bucket = o_ref.shape[1] * o_ref.shape[2] // width
    slot = lax.broadcasted_iota(jnp.int32, (groups * bucket, vision.shape[1]), 0)
    pick = jnp.where(slot == slots_of[...], 1.0, 0.0).astype(BF16)
    moved = lax.dot_general(
        pick, vision, (((1,), (1,)), ((), ())), preferred_element_type=F32
    ).astype(BF16)
    for k in range(groups):
        rows = moved[k * bucket : (k + 1) * bucket]
        if o_ref.shape[2] == width:
            o_ref[k] = rows
            continue
        tiles = width // LANES
        for i in range(tiles):
            o_ref[k, i * bucket : (i + 1) * bucket, :] = rows[:, i * LANES : (i + 1) * LANES]
        rest = rows[:, tiles * LANES :]
        fold = LANES // rest.shape[1]
        piece = bucket // fold
        o_ref[k, tiles * bucket :, :] = jnp.concatenate(
            [rest[i * piece : (i + 1) * piece] for i in range(fold)], axis=1
        )


def place_kernel(targets, text, arrived, o_ref):
    width, rows = text.shape
    groups = arrived.shape[0]
    bucket = arrived.shape[1] * arrived.shape[2] // width
    slots = groups * bucket
    row = lax.broadcasted_iota(jnp.int32, (slots, rows), 1)
    pick = jnp.where(row == targets[...], 1.0, 0.0)
    hit = jnp.sum(pick, axis=0, keepdims=True) > 0.5
    pick = pick.astype(BF16)

    def moved(blocks):
        return lax.dot_general(
            blocks, pick, (((0,), (0,)), ((), ())), preferred_element_type=F32
        ).astype(BF16)

    if arrived.shape[2] == width:
        whole = jnp.concatenate([arrived[k] for k in range(groups)], axis=0)
        o_ref[...] = jnp.where(hit, moved(whole), text[...])
        return
    tiles = width // LANES
    for i in range(tiles):
        part = jnp.concatenate(
            [arrived[k, i * bucket : (i + 1) * bucket, :] for k in range(groups)], axis=0
        )
        at = slice(i * LANES, (i + 1) * LANES)
        o_ref[at, :] = jnp.where(hit, moved(part), text[at, :])
    rest = width % LANES
    parts = []
    for k in range(groups):
        folded = arrived[k, tiles * bucket :, :]
        parts += [folded[:, i * rest : (i + 1) * rest] for i in range(LANES // rest)]
    at = slice(tiles * LANES, width)
    o_ref[at, :] = jnp.where(hit, moved(jnp.concatenate(parts, axis=0)), text[at, :])


def add_kernel(keep, near, o_ref):
    o_ref[...] = (keep[...].astype(F32) + near[...].astype(F32)).astype(BF16)


class Ring:
    def __init__(self, count):
        self.count = count
        order = ring_order(count)
        self.right = [(order[i], order[(i + 1) % count]) for i in range(count)]
        self.left = [(b, a) for a, b in self.right]
        self.done = []
        self.work = []

    def step(self, to_right, to_left):
        t = len(self.done)
        waits = [x for at, x in self.work if at == t - 2]
        if t >= 2:
            before = [self.done[t - 3][1]] if t >= 3 else []
            to_right = after(to_right, self.done[t - 2][0], *before, *waits)
            to_left = after(to_left, *self.done[t - 2])
        pair = (
            lax.ppermute(to_right, "wide", self.right),
            lax.ppermute(to_left, "wide", self.left),
        )
        self.done.append(pair)
        return pair

    def now(self, x):
        if len(self.done) >= 2:
            return after(x, *self.done[-2])
        return x

    def add_work(self, x):
        self.work.append((len(self.done) - 1, x))

    def add_late(self, x, steps):
        self.work.append((len(self.done) - 1 + steps, x))


def per_device(
    patches, norm_gain, norm_bias, w_in, b_in, w_out, b_out, w_proj, b_proj, text, place
):
    groups, parts = lax.axis_size("wide"), lax.axis_size("narrow")
    width, tokens = patches.shape[1], patches.shape[0]
    full = width * parts
    ff = w_in.shape[1]
    windows = tokens // WINDOW
    seq_rows = text.shape[0]
    bucket = seq_rows // groups
    slots = groups * bucket
    shard_rows = [w_in.shape[0], w_out.shape[1], w_proj.shape[2]]
    small = groups == 8 and all(r % 32 == 0 for r in shard_rows)
    chunks = 2

    near_pairs = [(i, i ^ 1) for i in range(parts)]
    far_pairs = [(i, i ^ 2) for i in range(parts)]

    def near(x):
        return lax.ppermute(x, "narrow", near_pairs)

    def far(x):
        return lax.ppermute(x, "narrow", far_pairs)


    def order(x):
        return call(
            order_kernel, (x,), [shape(WINDOW // chunks, width, windows)] * chunks,
            name="order_tokens",
        )

    def shards(count):
        rows = shard_rows[2] // count
        return call(
            shards_kernel, (jnp.transpose(w_proj, (0, 2, 1)),),
            [shape(rows, WINDOW * width)] * count, name="shards",
        )

    def route():
        return call(
            functools.partial(route_kernel, seq_rows, bucket), (place.reshape(groups, windows),),
            [shape(1, windows, dtype=jnp.int32), shape(slots, 1, dtype=jnp.int32)], name="route",
        )

    def norm(blocks):
        count = tokens // chunks
        return call(
            norm_kernel, (*blocks, norm_gain[None], norm_bias[None]), shape(count, full),
            scratch=[pltpu.VMEM((full, count), BF16)], name="norm",
        )

    def hidden(pieces, arrays, normed, first, columns):
        return call(
            functools.partial(hidden_kernel, pieces, groups, shard_rows[0], first, columns),
            (b_in[None], *arrays, *normed), shape(tokens, columns),
            scratch=[pltpu.VMEM((full, columns), BF16)], name="hidden",
        )

    def mlp_out(pieces, arrays, hiddens, over_x):
        count = WINDOW if over_x else OWN_PARTS
        outs = call(
            functools.partial(
                out_kernel, pieces, groups, shard_rows[1], over_x, len(hiddens), count
            ),
            (*hiddens, *arrays), [shape(width, tokens // count)] * (2 * count),
            scratch=[pltpu.VMEM((2 * width, ff), BF16)], name="mlp_out",
        )
        return outs[:count], outs[count:]

    def add(keep, other):
        return call(add_kernel, (keep, other), shape(*keep.shape), name="add")

    def stream(own, keep, core_sums, x_sums):
        return call(
            functools.partial(stream_kernel, chunks),
            (b_out[:, None], *own, *keep, *core_sums, *x_sums),
            shape(WINDOW * width, windows), name="stream",
        )

    def proj(pieces, arrays, merged):
        return call(
            functools.partial(proj_kernel, pieces, groups, shard_rows[2]),
            (merged, *arrays), [shape(2, width, windows)] * 2,
            scratch=[pltpu.VMEM((full, WINDOW * width), BF16)], name="proj",
        )

    def pack(slots_of, keep, core_sums, x_sums):
        block = (bucket, width)
        if compact(width, bucket):
            block = (bucket * width // LANES, LANES)
        return call(
            functools.partial(pack_kernel, groups),
            (slots_of, keep, core_sums, x_sums, b_proj[:, None]), shape(groups, *block),
            name="pack",
        )

    def exchange_and_place(buffer, targets):
        arrived = lax.all_to_all(buffer, "wide", split_axis=0, concat_axis=0, tiled=True)
        return call(
            place_kernel, (targets, text.T, arrived), shape(width, seq_rows), name="place"
        ).T


    if not small:
        shard = [w_in, w_out.T, *shards(1)]
        wholes = [lax.all_gather(s, "wide", axis=0, tiled=True) for s in shard]
        pieces = [Piece(0, k * width, width, None, 0, k) for k in range(parts)]
        own = order(patches.T)
        over_x = [far(x) for x in own]
        normed = [norm((x, y, near(x), near(y))) for x, y in zip(own, over_x)]
        act = hidden(pieces, wholes[:1], normed, 0, ff)
        keep_x, give_x = mlp_out(pieces, wholes[1:2], [act], 1)
        keep, give = mlp_out(pieces, wholes[1:2], [act], 0)
        x_sums = [far(add(k, near(g))) for k, g in zip(keep_x, give_x)]
        merged = stream(own, keep, [near(g) for g in give], x_sums)
        slots_of, targets = route()
        keep, give = proj(pieces, wholes[2:], merged)
        core_sums = near(give)
        x_sums = far(add(keep[1], core_sums[1]))
        return exchange_and_place(pack(slots_of, keep, core_sums, x_sums), targets)


    ring = Ring(groups)
    half_rows = shard_rows[0] // 2
    last = groups // 2

    def gather(halves, work):
        arrays = list(halves)
        pieces = [Piece(h, 0, half_rows, 0, h * half_rows) for h in (0, 1)]
        held = {(way, h): halves[h] for way in (0, 1) for h in (0, 1)}
        t = 0
        for step in range(1, last + 1):
            for first in (0, 1):
                if step == last and first == 1:
                    continue
                pair = ring.step(held[0, first], held[1, 1 - first])
                for way, h in ((0, first), (1, 1 - first)):
                    held[way, h] = pair[way]
                    shift = -step if way == 0 else step
                    pieces.append(Piece(len(arrays), 0, half_rows, shift, h * half_rows))
                    arrays.append(pair[way])
                if t in work:
                    work[t]()
                t += 1
        return pieces, arrays

    def hops_of_two(shards, work):
        arrays = [[x] for x in shards]
        pieces = [[Piece(0, 0, 2 * half_rows, 0, 0)] for _ in shards]
        held = {(way, k): x for way in (0, 1) for k, x in enumerate(shards)}
        t = 0
        for step in range(1, last + 1):
            for k in range(len(shards)):
                sent = [held[0, k], held[1, k]]
                rows, bases = 2 * half_rows, (0, 0)
                if step == last:
                    sent = [sent[0][:half_rows], sent[1][half_rows:]]
                    rows, bases = half_rows, (0, half_rows)
                pair = ring.step(*sent)
                for way in (0, 1):
                    held[way, k] = pair[way]
                    shift = -step if way == 0 else step
                    pieces[k].append(Piece(len(arrays[k]), 0, rows, shift, bases[way]))
                    arrays[k].append(pair[way])
                if t in work:
                    for run in work[t]:
                        run(pieces, arrays)
                t += 1
        return pieces, arrays

    own, over_x, over_core, over_both, normed = [], [], [], [], []
    got = {}

    def start_tokens():
        own.extend(order(patches.T))
        over_x.append(far(own[0]))
        ring.add_work(own[0])

    def start_shards():
        got["shards"] = shards(2)
        ring.add_work(got["shards"][0])
        over_core.extend(near(x) for x in own)

    def send_second():
        over_x.append(far(ring.now(own[1])))
        got["slots_of"], got["targets"] = route()

    def send_both():
        over_both.append(near(ring.now(over_x[len(over_both)])))

    def start_norm():
        i = len(normed)
        first = ring.now(own[i])
        normed.append(norm((first, over_x[i], over_core[i], over_both[i])))
        ring.add_work(normed[i])

    def both_and_norm():
        send_both()
        start_norm()

    columns = 256
    hiddens = []

    def start_hidden():
        rows = [ring.now(normed[0]), *normed[1:]]
        hiddens.append(hidden(pieces_in, arrays_in, rows, len(hiddens) * columns, columns))
        ring.add_work(hiddens[-1])

    early = {0: start_tokens, 1: send_second, 2: start_shards, 3: send_both, 4: both_and_norm,
             5: start_norm}
    work = {t: [lambda p, a, run=run: run()] for t, run in early.items()}
    first_of_last = 2 * last

    def hidden_in_pair(pieces, arrays):
        rows = [ring.now(normed[0]), *normed[1:]]
        hiddens.append(hidden(pieces[0], arrays[0], rows, len(hiddens) * columns, columns))
        ring.add_work(hiddens[-1])

    for t in HIDDEN_AT:
        if t < first_of_last:
            work.setdefault(t, []).append(hidden_in_pair)
    (pieces_in, pieces_out), (arrays_in, arrays_out) = hops_of_two([w_in, w_out.T], work)

    def start_out(over_x):
        acts = [ring.now(hiddens[0]), *hiddens[1:]]
        keep, give = mlp_out(pieces_out, arrays_out, acts, over_x)
        got["keep", over_x] = keep
        got["core", over_x] = [near(g) for g in give]
        ring.add_work(keep[0])

    def start_sums():
        core = [ring.now(got["core", 1][0]), *got["core", 1][1:]]
        sums = [add(k, c) for k, c in zip(got["keep", 1], core)]
        got["x_sums"] = [far(x) for x in sums]
        for steps, x in zip(LATE, got["x_sums"]):
            ring.add_late(x, steps)
        ring.add_work(sums[0])
        start_out(0)

    plan = {}
    for t in HIDDEN_AT:
        if t >= first_of_last:
            plan.setdefault(t - first_of_last, []).append(start_hidden)
    plan.setdefault(OUT_AT, []).append(lambda: start_out(1))
    plan.setdefault(SUMS_AT, []).append(start_sums)

    def run_all(steps):
        def run():
            for step in steps:
                step()
        return run

    pieces_proj, arrays_proj = gather(
        got["shards"], {t: run_all(steps) for t, steps in plan.items()}
    )

    merged = stream(own, got["keep", 0], got["core", 0], got["x_sums"])
    keep, give = proj(pieces_proj, arrays_proj, merged)
    core_sums = near(give)
    x_sums = far(add(keep[1], core_sums[1]))
    return exchange_and_place(pack(got["slots_of"], keep, core_sums, x_sums), got["targets"])


def solution(mesh):
    placed = (
        P("wide", "narrow"),
        P(),
        P(),
        P("wide", "narrow"),
        P("narrow"),
        P("narrow", "wide"),
        P("narrow"),
        P(None, "narrow", "wide"),
        P("narrow"),
        P("wide", "narrow"),
        P(),
    )
    return jax.shard_map(
        per_device, mesh=mesh, in_specs=placed, out_specs=P("wide", "narrow"), check_vma=False
    )
```

```python
import functools

import jax
import jax.numpy as jnp
from jax import lax
from jax.experimental import pallas as pl
from jax.experimental.pallas import tpu as pltpu
from jax.sharding import PartitionSpec as P

F32 = jnp.float32
BF16 = jnp.bfloat16
WINDOW = 4
LATE = (2, 2, 3)
HIDDEN_AT = (7, 7, 8, 8, 8)
OUT_AT = 1
OWN_PARTS = 1
SUMS_AT = 2
VMEM = pl.BlockSpec(memory_space=pltpu.VMEM)


def call(kernel, operands, outs, scratch=(), name=None):
    single = not isinstance(outs, (list, tuple))
    return pl.pallas_call(
        kernel,
        out_shape=outs,
        in_specs=[VMEM] * len(operands),
        out_specs=VMEM if single else [VMEM] * len(outs),
        scratch_shapes=list(scratch),
        compiler_params=pltpu.CompilerParams(vmem_limit_bytes=28 * 1024 * 1024),
        cost_estimate=pl.CostEstimate(flops=0, bytes_accessed=0, transcendentals=0),
        name=name,
    )(*operands)


def shape(*dims, dtype=BF16):
    return jax.ShapeDtypeStruct(dims, dtype)


def after(x, *others):
    return lax.optimization_barrier((x, *others))[0]


def ring_order(count):
    return list(range(0, count, 2)) + list(range(count - 1, 0, -2))


def ring_owner(me, shift, count):
    half = me // 2
    at = jnp.where(me % 2 == 0, half, count - 1 - half) + (shift + count)
    at = at % count
    return jnp.where(at < count // 2, 2 * at, 2 * (count - 1 - at) + 1)


class Piece:
    def __init__(self, array, start, rows, shift, base, index=0):
        self.array, self.start, self.rows = array, start, rows
        self.shift, self.base, self.index = shift, base, index

    def row(self, count, shard_rows):
        if self.shift is None:
            return self.index * self.rows
        return ring_owner(lax.axis_index("wide"), self.shift, count) * shard_rows + self.base

    def block_row(self, count, shard_rows, block):
        if self.shift is None:
            of, inside = self.index, 0
        else:
            owner = ring_owner(lax.axis_index("wide"), self.shift, count)
            per_block = block // shard_rows
            of, inside = owner // per_block, (owner % per_block) * shard_rows + self.base
        mine = lax.axis_index("narrow")
        over_x = jnp.where(of // 2 == mine // 2, 0, 1)
        over_core = jnp.where(of % 2 == mine % 2, 0, 1)
        return over_x, over_core, inside


def rows_at(start, rows):
    return pl.ds(pl.multiple_of(start, 16), rows)


def order_kernel(x_ref, *outs):
    tokens = x_ref.shape[1]
    windows = tokens // WINDOW
    source = lax.broadcasted_iota(jnp.int32, (tokens, windows), 0)
    window = lax.broadcasted_iota(jnp.int32, (tokens, windows), 1)
    each = WINDOW // len(outs)
    for p in range(WINDOW):
        pick = jnp.where(source == WINDOW * window + p, 1.0, 0.0).astype(BF16)
        outs[p // each][p % each] = jnp.dot(
            x_ref[...], pick, preferred_element_type=F32
        ).astype(BF16)


def shards_kernel(w_proj, *outs):
    half = w_proj.shape[1] // len(outs)
    flat = jnp.concatenate([w_proj[p] for p in range(WINDOW)], axis=1)
    for i, o_ref in enumerate(outs):
        o_ref[...] = flat[i * half : (i + 1) * half, :]


def route_kernel(seq_rows, bucket, place, slots_of, targets):
    groups, windows = place.shape
    me = lax.axis_index("wide")
    table = place[...]
    owner = jnp.where(table >= 0, 0, -1)
    for d in range(1, groups):
        owner = owner + jnp.where(table >= d * seq_rows, 1, 0)
    earlier = jnp.where(
        lax.broadcasted_iota(jnp.int32, (windows, windows), 0)
        <= lax.broadcasted_iota(jnp.int32, (windows, windows), 1),
        1.0,
        0.0,
    ).astype(BF16)
    here = jnp.where(owner == me, 1.0, 0.0)
    rank = jnp.dot(here.astype(BF16), earlier, preferred_element_type=F32)
    rank = jnp.where(owner == me, rank, 0.0).astype(jnp.int32)
    local = table - me * seq_rows
    slot = lax.broadcasted_iota(jnp.int32, (bucket, windows), 0) + 1
    source_at = lax.broadcasted_iota(jnp.int32, (groups, windows), 0)
    for k in range(groups):
        wanted = source_at == k
        of_rank = jnp.sum(jnp.where(wanted, rank, 0), axis=0, keepdims=True)
        of_local = jnp.sum(jnp.where(wanted, local, 0), axis=0, keepdims=True)
        found = jnp.where(of_rank == slot, of_local + 1, 0)
        targets[k * bucket : (k + 1) * bucket, :] = jnp.sum(found, axis=1, keepdims=True) - 1
    mine = jnp.sum(jnp.where(source_at == me, owner, 0), axis=0, keepdims=True)
    hits = source_at == mine
    rank = jnp.dot(
        jnp.where(hits, 1.0, 0.0).astype(BF16), earlier, preferred_element_type=F32
    )
    rank = jnp.sum(jnp.where(hits, rank, 0.0), axis=0, keepdims=True).astype(jnp.int32)
    slots_of[...] = jnp.where(mine >= 0, mine * bucket + rank - 1, groups * bucket)


def norm_kernel(own, over_x, over_core, over_both, gain, bias, o_ref, whole):
    parts = (own, over_x, over_core, over_both)
    each, rows, windows = own.shape
    tokens = each * windows
    mine = lax.axis_index("narrow")
    for part, flip in zip(parts, (0, 2, 1, 3)):
        at = (mine ^ flip) * rows
        for j in range(each):
            whole[rows_at(at, rows), j * windows : (j + 1) * windows] = part[j]
    width = whole.shape[0]
    step = 128
    for t in range(0, tokens, step):
        values = whole[:, t : t + step].astype(F32)
        center = jnp.sum(values, axis=0, keepdims=True) * (1.0 / width)
        values = values - center
        spread = jnp.sum(values * values, axis=0, keepdims=True) * (1.0 / width)
        values = (values * lax.rsqrt(spread + 1e-06)).T
        o_ref[t : t + step, :] = (values * gain[...] + bias[...]).astype(BF16)


def hidden_kernel(pieces, count, shard_rows, first, columns, bias, *refs):
    arrays = 1 + max(p.array for p in pieces)
    sources, normed, (o_ref, part) = refs[:arrays], refs[arrays:-2], refs[-2:]
    for p in pieces:
        part[rows_at(p.row(count, shard_rows), p.rows), :] = sources[p.array][
            p.start : p.start + p.rows, first : first + columns
        ]
    at = 0
    for rows in normed:
        v = jnp.dot(rows[...], part[...], preferred_element_type=F32)
        v = v + bias[:, first : first + columns]
        o_ref[at : at + rows.shape[0], :] = (
            0.5 * v * (1.0 + lax.erf(v * (2.0**-0.5)))
        ).astype(BF16)
        at += rows.shape[0]


def out_kernel(pieces, count, shard_rows, over_x, hidden_count, chunks, *refs):
    hidden, refs = refs[:hidden_count], refs[hidden_count:]
    outs, part = refs[-1 - 2 * chunks : -1], refs[-1]
    keep, give = outs[:chunks], outs[chunks:]
    sources = refs[: -1 - 2 * chunks]
    block, tokens = keep[0].shape
    for p in pieces:
        x, core, inside = p.block_row(count, shard_rows, block)

        @pl.when(x == over_x)
        def _():
            part[rows_at(core * block + inside, p.rows), :] = sources[p.array][
                p.start : p.start + p.rows, :
            ]

    columns = hidden[0].shape[1]
    step = 256
    for t in range(0, tokens * chunks, step):
        total = None
        for i, h in enumerate(hidden):
            v = lax.dot_general(
                part[:, i * columns : (i + 1) * columns],
                h[t : t + step, :],
                (((1,), (1,)), ((), ())),
                preferred_element_type=F32,
            )
            total = v if total is None else total + v
        total = total.astype(BF16)
        c, at = t // tokens, t % tokens
        keep[c][:, at : at + step] = total[:block]
        give[c][:, at : at + step] = total[block:]


def proj_kernel(pieces, count, shard_rows, merged, *refs):
    sources, (keep, give, part) = refs[:-3], refs[-3:]
    block = keep.shape[1]
    for p in pieces:
        x, core, inside = p.block_row(count, shard_rows, block)
        at = rows_at(core * 2 * block + x * block + inside, p.rows)
        part[at, :] = sources[p.array][p.start : p.start + p.rows, :]
    for core, target in ((1, give), (0, keep)):
        v = jnp.dot(
            part[core * 2 * block : (core + 1) * 2 * block, :],
            merged[...],
            preferred_element_type=F32,
        ).astype(BF16)
        target[0] = v[:block]
        target[1] = v[block:]


def stream_kernel(chunks, bias, *refs):
    o_ref = refs[-1]
    own, refs = refs[:chunks], refs[chunks:-1]
    keep, near, far = refs[:OWN_PARTS], refs[OWN_PARTS : 2 * OWN_PARTS], refs[2 * OWN_PARTS :]
    of_own = WINDOW // OWN_PARTS
    each, rows, windows = own[0].shape
    for p in range(WINDOW):
        at = slice(p % of_own * windows, (p % of_own + 1) * windows)
        total = keep[p // of_own][:, at].astype(F32) + near[p // of_own][:, at].astype(F32)
        total = total + far[p][...].astype(F32)
        v = own[p // each][p % each].astype(F32) + (total + bias[...])
        o_ref[p * rows : (p + 1) * rows, :] = v.astype(BF16)


LANES = 128


def compact(width, bucket):
    rest = width % LANES
    return rest > 0 and LANES % rest == 0 and bucket % (16 * (LANES // rest)) == 0


def pack_kernel(groups, slots_of, keep, near, far, bias, o_ref):
    total = keep[0].astype(F32) + near[0].astype(F32) + far[...].astype(F32)
    vision = (total + bias[...]).astype(BF16)
    width = vision.shape[0]
    bucket = o_ref.shape[1] * o_ref.shape[2] // width
    slot = lax.broadcasted_iota(jnp.int32, (groups * bucket, vision.shape[1]), 0)
    pick = jnp.where(slot == slots_of[...], 1.0, 0.0).astype(BF16)
    moved = lax.dot_general(
        pick, vision, (((1,), (1,)), ((), ())), preferred_element_type=F32
    ).astype(BF16)
    for k in range(groups):
        rows = moved[k * bucket : (k + 1) * bucket]
        if o_ref.shape[2] == width:
            o_ref[k] = rows
            continue
        tiles = width // LANES
        for i in range(tiles):
            o_ref[k, i * bucket : (i + 1) * bucket, :] = rows[:, i * LANES : (i + 1) * LANES]
        rest = rows[:, tiles * LANES :]
        fold = LANES // rest.shape[1]
        piece = bucket // fold
        o_ref[k, tiles * bucket :, :] = jnp.concatenate(
            [rest[i * piece : (i + 1) * piece] for i in range(fold)], axis=1
        )


def place_kernel(targets, text, arrived, o_ref):
    width, rows = text.shape
    groups = arrived.shape[0]
    bucket = arrived.shape[1] * arrived.shape[2] // width
    slots = groups * bucket
    row = lax.broadcasted_iota(jnp.int32, (slots, rows), 1)
    pick = jnp.where(row == targets[...], 1.0, 0.0)
    hit = jnp.sum(pick, axis=0, keepdims=True) > 0.5
    pick = pick.astype(BF16)

    def moved(blocks):
        return lax.dot_general(
            blocks, pick, (((0,), (0,)), ((), ())), preferred_element_type=F32
        ).astype(BF16)

    if arrived.shape[2] == width:
        whole = jnp.concatenate([arrived[k] for k in range(groups)], axis=0)
        o_ref[...] = jnp.where(hit, moved(whole), text[...])
        return
    tiles = width // LANES
    for i in range(tiles):
        part = jnp.concatenate(
            [arrived[k, i * bucket : (i + 1) * bucket, :] for k in range(groups)], axis=0
        )
        at = slice(i * LANES, (i + 1) * LANES)
        o_ref[at, :] = jnp.where(hit, moved(part), text[at, :])
    rest = width % LANES
    parts = []
    for k in range(groups):
        folded = arrived[k, tiles * bucket :, :]
        parts += [folded[:, i * rest : (i + 1) * rest] for i in range(LANES // rest)]
    at = slice(tiles * LANES, width)
    o_ref[at, :] = jnp.where(hit, moved(jnp.concatenate(parts, axis=0)), text[at, :])


def add_kernel(keep, near, o_ref):
    o_ref[...] = (keep[...].astype(F32) + near[...].astype(F32)).astype(BF16)


class Ring:
    def __init__(self, count):
        self.count = count
        order = ring_order(count)
        self.right = [(order[i], order[(i + 1) % count]) for i in range(count)]
        self.left = [(b, a) for a, b in self.right]
        self.done = []
        self.work = []

    def step(self, to_right, to_left):
        t = len(self.done)
        waits = [x for at, x in self.work if at == t - 2]
        if t >= 2:
            before = [self.done[t - 3][1]] if t >= 3 else []
            to_right = after(to_right, self.done[t - 2][0], *before, *waits)
            to_left = after(to_left, *self.done[t - 2])
        pair = (
            lax.ppermute(to_right, "wide", self.right),
            lax.ppermute(to_left, "wide", self.left),
        )
        self.done.append(pair)
        return pair

    def now(self, x):
        if len(self.done) >= 2:
            return after(x, *self.done[-2])
        return x

    def add_work(self, x):
        self.work.append((len(self.done) - 1, x))

    def add_late(self, x, steps):
        self.work.append((len(self.done) - 1 + steps, x))


def per_device(
    patches, norm_gain, norm_bias, w_in, b_in, w_out, b_out, w_proj, b_proj, text, place
):
    groups, parts = lax.axis_size("wide"), lax.axis_size("narrow")
    width, tokens = patches.shape[1], patches.shape[0]
    full = width * parts
    ff = w_in.shape[1]
    windows = tokens // WINDOW
    seq_rows = text.shape[0]
    bucket = seq_rows // groups
    slots = groups * bucket
    shard_rows = [w_in.shape[0], w_out.shape[1], w_proj.shape[2]]
    small = groups == 8 and all(r % 32 == 0 for r in shard_rows)
    chunks = 2

    near_pairs = [(i, i ^ 1) for i in range(parts)]
    far_pairs = [(i, i ^ 2) for i in range(parts)]

    def near(x):
        return lax.ppermute(x, "narrow", near_pairs)

    def far(x):
        return lax.ppermute(x, "narrow", far_pairs)


    def order(x):
        return call(
            order_kernel, (x,), [shape(WINDOW // chunks, width, windows)] * chunks,
            name="order_tokens",
        )

    def shards(count):
        rows = shard_rows[2] // count
        return call(
            shards_kernel, (jnp.transpose(w_proj, (0, 2, 1)),),
            [shape(rows, WINDOW * width)] * count, name="shards",
        )

    def route():
        return call(
            functools.partial(route_kernel, seq_rows, bucket), (place.reshape(groups, windows),),
            [shape(1, windows, dtype=jnp.int32), shape(slots, 1, dtype=jnp.int32)], name="route",
        )

    def norm(blocks):
        count = tokens // chunks
        return call(
            norm_kernel, (*blocks, norm_gain[None], norm_bias[None]), shape(count, full),
            scratch=[pltpu.VMEM((full, count), BF16)], name="norm",
        )

    def hidden(pieces, arrays, normed, first, columns):
        return call(
            functools.partial(hidden_kernel, pieces, groups, shard_rows[0], first, columns),
            (b_in[None], *arrays, *normed), shape(tokens, columns),
            scratch=[pltpu.VMEM((full, columns), BF16)], name="hidden",
        )

    def mlp_out(pieces, arrays, hiddens, over_x):
        count = WINDOW if over_x else OWN_PARTS
        outs = call(
            functools.partial(
                out_kernel, pieces, groups, shard_rows[1], over_x, len(hiddens), count
            ),
            (*hiddens, *arrays), [shape(width, tokens // count)] * (2 * count),
            scratch=[pltpu.VMEM((2 * width, ff), BF16)], name="mlp_out",
        )
        return outs[:count], outs[count:]

    def add(keep, other):
        return call(add_kernel, (keep, other), shape(*keep.shape), name="add")

    def stream(own, keep, core_sums, x_sums):
        return call(
            functools.partial(stream_kernel, chunks),
            (b_out[:, None], *own, *keep, *core_sums, *x_sums),
            shape(WINDOW * width, windows), name="stream",
        )

    def proj(pieces, arrays, merged):
        return call(
            functools.partial(proj_kernel, pieces, groups, shard_rows[2]),
            (merged, *arrays), [shape(2, width, windows)] * 2,
            scratch=[pltpu.VMEM((full, WINDOW * width), BF16)], name="proj",
        )

    def pack(slots_of, keep, core_sums, x_sums):
        block = (bucket, width)
        if compact(width, bucket):
            block = (bucket * width // LANES, LANES)
        return call(
            functools.partial(pack_kernel, groups),
            (slots_of, keep, core_sums, x_sums, b_proj[:, None]), shape(groups, *block),
            name="pack",
        )

    def exchange_and_place(buffer, targets):
        arrived = lax.all_to_all(buffer, "wide", split_axis=0, concat_axis=0, tiled=True)
        return call(
            place_kernel, (targets, text.T, arrived), shape(width, seq_rows), name="place"
        ).T


    if not small:
        shard = [w_in, w_out.T, *shards(1)]
        wholes = [lax.all_gather(s, "wide", axis=0, tiled=True) for s in shard]
        pieces = [Piece(0, k * width, width, None, 0, k) for k in range(parts)]
        own = order(patches.T)
        over_x = [far(x) for x in own]
        normed = [norm((x, y, near(x), near(y))) for x, y in zip(own, over_x)]
        act = hidden(pieces, wholes[:1], normed, 0, ff)
        keep_x, give_x = mlp_out(pieces, wholes[1:2], [act], 1)
        keep, give = mlp_out(pieces, wholes[1:2], [act], 0)
        x_sums = [far(add(k, near(g))) for k, g in zip(keep_x, give_x)]
        merged = stream(own, keep, [near(g) for g in give], x_sums)
        slots_of, targets = route()
        keep, give = proj(pieces, wholes[2:], merged)
        core_sums = near(give)
        x_sums = far(add(keep[1], core_sums[1]))
        return exchange_and_place(pack(slots_of, keep, core_sums, x_sums), targets)


    ring = Ring(groups)
    half_rows = shard_rows[0] // 2
    last = groups // 2

    def gather(halves, work):
        arrays = list(halves)
        pieces = [Piece(h, 0, half_rows, 0, h * half_rows) for h in (0, 1)]
        held = {(way, h): halves[h] for way in (0, 1) for h in (0, 1)}
        t = 0
        for step in range(1, last + 1):
            for first in (0, 1):
                if step == last and first == 1:
                    continue
                pair = ring.step(held[0, first], held[1, 1 - first])
                for way, h in ((0, first), (1, 1 - first)):
                    held[way, h] = pair[way]
                    shift = -step if way == 0 else step
                    pieces.append(Piece(len(arrays), 0, half_rows, shift, h * half_rows))
                    arrays.append(pair[way])
                if t in work:
                    work[t]()
                t += 1
        return pieces, arrays

    def hops_of_two(shards, work):
        arrays = [[x] for x in shards]
        pieces = [[Piece(0, 0, 2 * half_rows, 0, 0)] for _ in shards]
        held = {(way, k): x for way in (0, 1) for k, x in enumerate(shards)}
        t = 0
        for step in range(1, last + 1):
            for k in range(len(shards)):
                sent = [held[0, k], held[1, k]]
                rows, bases = 2 * half_rows, (0, 0)
                if step == last:
                    sent = [sent[0][:half_rows], sent[1][half_rows:]]
                    rows, bases = half_rows, (0, half_rows)
                pair = ring.step(*sent)
                for way in (0, 1):
                    held[way, k] = pair[way]
                    shift = -step if way == 0 else step
                    pieces[k].append(Piece(len(arrays[k]), 0, rows, shift, bases[way]))
                    arrays[k].append(pair[way])
                if t in work:
                    for run in work[t]:
                        run(pieces, arrays)
                t += 1
        return pieces, arrays

    own, over_x, over_core, over_both, normed = [], [], [], [], []
    got = {}

    def start_tokens():
        own.extend(order(patches.T))
        over_x.append(far(own[0]))
        ring.add_work(own[0])

    def start_shards():
        got["shards"] = shards(2)
        ring.add_work(got["shards"][0])
        over_core.extend(near(x) for x in own)

    def send_second():
        over_x.append(far(ring.now(own[1])))
        got["slots_of"], got["targets"] = route()

    def send_both():
        over_both.append(near(ring.now(over_x[len(over_both)])))

    def start_norm():
        i = len(normed)
        first = ring.now(own[i])
        normed.append(norm((first, over_x[i], over_core[i], over_both[i])))
        ring.add_work(normed[i])

    def both_and_norm():
        send_both()
        start_norm()

    columns = 256
    hiddens = []

    def start_hidden():
        rows = [ring.now(normed[0]), *normed[1:]]
        hiddens.append(hidden(pieces_in, arrays_in, rows, len(hiddens) * columns, columns))
        ring.add_work(hiddens[-1])

    early = {0: start_tokens, 1: send_second, 2: start_shards, 3: send_both, 4: both_and_norm,
             5: start_norm}
    work = {t: [lambda p, a, run=run: run()] for t, run in early.items()}
    first_of_last = 2 * last

    def hidden_in_pair(pieces, arrays):
        rows = [ring.now(normed[0]), *normed[1:]]
        hiddens.append(hidden(pieces[0], arrays[0], rows, len(hiddens) * columns, columns))
        ring.add_work(hiddens[-1])

    for t in HIDDEN_AT:
        if t < first_of_last:
            work.setdefault(t, []).append(hidden_in_pair)
    (pieces_in, pieces_out), (arrays_in, arrays_out) = hops_of_two([w_in, w_out.T], work)

    def start_out(over_x):
        acts = [ring.now(hiddens[0]), *hiddens[1:]]
        keep, give = mlp_out(pieces_out, arrays_out, acts, over_x)
        got["keep", over_x] = keep
        got["core", over_x] = [near(g) for g in give]
        ring.add_work(keep[0])

    def start_sums():
        core = [ring.now(got["core", 1][0]), *got["core", 1][1:]]
        sums = [add(k, c) for k, c in zip(got["keep", 1], core)]
        got["x_sums"] = [far(x) for x in sums]
        for steps, x in zip(LATE, got["x_sums"]):
            ring.add_late(x, steps)
        ring.add_work(sums[0])
        start_out(0)

    plan = {}
    for t in HIDDEN_AT:
        if t >= first_of_last:
            plan.setdefault(t - first_of_last, []).append(start_hidden)
    plan.setdefault(OUT_AT, []).append(lambda: start_out(1))
    plan.setdefault(SUMS_AT, []).append(start_sums)

    def run_all(steps):
        def run():
            for step in steps:
                step()
        return run

    pieces_proj, arrays_proj = gather(
        got["shards"], {t: run_all(steps) for t, steps in plan.items()}
    )

    merged = stream(own, got["keep", 0], got["core", 0], got["x_sums"])
    keep, give = proj(pieces_proj, arrays_proj, merged)
    core_sums = near(give)
    x_sums = far(add(keep[1], core_sums[1]))
    return exchange_and_place(pack(got["slots_of"], keep, core_sums, x_sums), got["targets"])


def solution(mesh):
    placed = (
        P("wide", "narrow"),
        P(),
        P(),
        P("wide", "narrow"),
        P("narrow"),
        P("narrow", "wide"),
        P("narrow"),
        P(None, "narrow", "wide"),
        P("narrow"),
        P("wide", "narrow"),
        P(),
    )
    return jax.shard_map(
        per_device, mesh=mesh, in_specs=placed, out_specs=P("wide", "narrow"), check_vma=False
    )
```
